32 devices in a mesh: dp: 16 (over z, x, core), pair: 2 (over y).
Axes of the slice: x: 2, y: 2, z: 4, core: 2. Of those that a mesh axis runs over, the one named last changes fastest.
Arguments:
- tokens: bfloat16 [65536, 512], P(('dp', 'pair')), may hold values from -12 to 12
- cotangent: bfloat16 [65536, 512], P(('dp', 'pair')), may hold values from -6 to 6
- counts: int32 [128], P(('dp', 'pair')), may hold values from 12 to 64, as said below
- shifts: int32 [128, 2], P(('dp', 'pair')), may hold values from 0 to 3
- qkv_weight: bfloat16 [512, 1536], P(('dp', 'pair')), may hold values from -0.25 to 0.25
- proj_weight: bfloat16 [512, 512], P(('dp', 'pair')), may hold values from -1 to 1
- up_weight: bfloat16 [512, 2048], P(('dp', 'pair')), may hold values from -0.25 to 0.25
- down_weight: bfloat16 [2048, 512], P(('dp', 'pair')), may hold values from -0.1875 to 0.1875
- first_gain: bfloat16 [512], P(('dp', 'pair')), may hold values from 0.099609375 to 1.8984375
- first_bias: bfloat16 [512], P(('dp', 'pair')), may hold values from -3 to 3
- second_gain: bfloat16 [512], P(('dp', 'pair')), may hold values from 0.099609375 to 1.8984375
- second_bias: bfloat16 [512], P(('dp', 'pair')), may hold values from -3 to 3
- query_bias: bfloat16 [512], P(('dp', 'pair')), may hold values from -3 to 3
- value_bias: bfloat16 [512], P(('dp', 'pair')), may hold values from -3 to 3
- proj_bias: bfloat16 [512], P(('dp', 'pair')), may hold values from -3 to 3
- up_bias: bfloat16 [2048], P(('dp', 'pair')), may hold values from -3 to 3
- down_bias: bfloat16 [512], P(('dp', 'pair')), may hold values from -3 to 3
- rel_table: bfloat16 [49, 16], replicated, may hold values from -6 to 6
Outputs:
- out: bfloat16 [65536, 512], P(('dp', 'pair'))
- grad_tokens: float32 [65536, 512], P(('dp', 'pair'))
- grad_qkv_weight: float32 [512, 1536], P(('dp', 'pair'))
- grad_proj_weight: float32 [512, 512], P(('dp', 'pair'))
- grad_up_weight: float32 [512, 2048], P(('dp', 'pair'))
- grad_down_weight: float32 [2048, 512], P(('dp', 'pair'))
- grad_first_gain: float32 [512], P(('dp', 'pair'))
- grad_first_bias: float32 [512], P(('dp', 'pair'))
- grad_second_gain: float32 [512], P(('dp', 'pair'))
- grad_second_bias: float32 [512], P(('dp', 'pair'))
- grad_query_bias: float32 [512], P(('dp', 'pair'))
- grad_value_bias: float32 [512], P(('dp', 'pair'))
- grad_proj_bias: float32 [512], P(('dp', 'pair'))
- grad_up_bias: float32 [2048], P(('dp', 'pair'))
- grad_down_bias: float32 [512], P(('dp', 'pair'))
- grad_rel_table: float32 [49, 16], replicated
The draws below stay inside these ranges and needn't reach their ends.
Inputs may be any that keep to these rules, and one draw needn't show every extreme that they name: `counts`: patch rows at or beyond a clip's count are padding; some clip has all 64 rows visible.
All inputs are finite; a program needn't handle non-finite values.
Results may differ from the reference program's by a relative error of at most 0.014.
Values may be sent and summed in bfloat16 or wider, within the bound.
No kernel may reach another device: no remote copies, remote signals or barrier semaphores. Data moves between devices by JAX's collectives and lax.ppermute only.
A program may use at most 192 MiB of HBM per device.

```python
import jax
import jax.numpy as jnp
from jax import lax

D = 512
FF = 2048
HEADS = 16
GRID_T = 64
GRID_F = 8
WIN = 4
CLIPS = 128
TOKENS = 65536
RELS = 49


def draw_counts(key, part):
    key = jax.random.fold_in(key, 11)
    least_rows = max(1, GRID_T // 5)
    first_key, second_key = jax.random.split(key)
    drawn = jax.random.randint(first_key, (CLIPS,), least_rows, GRID_T + 1, dtype=jnp.int32)
    chosen = jax.random.permutation(second_key, CLIPS)
    drawn = drawn.at[chosen[0]].set(GRID_T)
    drawn = drawn.at[chosen[1]].set(least_rows)
    return drawn.astype(jnp.int32)


def plant(values, rng, low, high):
    extent = values.shape
    index_at = [jax.random.randint(jax.random.fold_in(rng, axis), (), 0, extent[axis]) for axis in range(len(extent))]
    values = values.at[tuple(index_at)].set(low)
    longest = extent.index(max(extent))
    index_at[longest] = (index_at[longest] + 1) % extent[longest]
    return values.at[tuple(index_at)].set(high)


def strengthened(values, key, source, target, blocks, factor):
    owner, partner = [(jnp.arange(values.shape[dim]) // (values.shape[dim] // blocks)).reshape([-1 if axis == dim else 1 for axis in range(values.ndim)]) for dim in (source, target)]
    chosen = jax.random.permutation(key, blocks)[partner]
    strong = (owner == chosen) | (owner == (partner + blocks // 2) % blocks)
    return jnp.where(strong, factor * values, values)


def block_levels(key, shape, shards, smallest, largest):
    level, own = 1.0, jax.random.fold_in(key, 6)
    for axis_at, parts in shards:
        draws = jnp.exp(jax.random.uniform(jax.random.fold_in(own, axis_at), (parts,), jnp.float32, smallest / len(shards), largest / len(shards)))
        level = level * jnp.repeat(draws, shape[axis_at] // parts).reshape([-1 if axis == axis_at else 1 for axis in range(len(shape))])
    return level


def bell_draw(rng, extent, scale, limit, pieces=(), kind=jnp.bfloat16):
    values = scale * jax.random.normal(rng, extent, jnp.float32)
    if pieces:
        values = values * block_levels(rng, extent, pieces, -0.22, 0.18)
    return jnp.clip(values, -limit, limit).astype(kind)


def gaussian_with(key, dims, scale, limit, shards, heavy, held_as=jnp.bfloat16):
    values = scale * jax.random.normal(key, dims, jnp.float32)
    if shards:
        values = values * block_levels(key, dims, shards, -0.22, 0.18)
    return jnp.clip(strengthened(values, jax.random.fold_in(key, 3), *heavy), -limit, limit).astype(held_as)


def setup_inputs(seed: int = 0) -> dict:
    splits = jax.random.split(jax.random.key(seed), 19)
    tokens = gaussian_with(splits[0], (TOKENS, D), 1.0, 12.0, ((0, 32),), (0, 1, 32, 2.75))
    cotangent = bell_draw(splits[1], (TOKENS, D), 1.0, 6.0, ((0, 32),))
    counts = draw_counts(jax.random.fold_in(splits[18], 71), 0)
    shifts = plant(jax.random.randint(splits[3], (CLIPS, 2), 0, WIN), jax.random.fold_in(splits[3], 1), 0, WIN - 1).astype(jnp.int32)
    qkv_weight = bell_draw(splits[4], (D, 3 * D), D ** -0.5, 0.25, ((0, 32),))
    proj_weight = bell_draw(splits[5], (D, D), (D // 16) ** -0.5, 1.0, ((0, 32),))
    up_weight = bell_draw(splits[6], (D, FF), D ** -0.5, 0.25, ((0, 32),))
    down_weight = bell_draw(splits[7], (FF, D), (FF // 2) ** -0.5, 0.1875, ((0, 32),))
    first_gain = jnp.clip(1.0 + 0.18 * jax.random.normal(splits[8], (D,), jnp.float32), 0.099609375, 1.8984375).astype(jnp.bfloat16)
    first_bias = bell_draw(splits[9], (D,), 0.5, 3.0, ((0, 32),))
    second_gain = jnp.clip(1.0 + 0.18 * jax.random.normal(splits[10], (D,), jnp.float32), 0.099609375, 1.8984375).astype(jnp.bfloat16)
    second_bias = bell_draw(splits[11], (D,), 0.5, 3.0, ((0, 32),))
    query_bias = bell_draw(splits[12], (D,), 0.5, 3.0, ((0, 32),))
    value_bias = bell_draw(splits[13], (D,), 0.5, 3.0, ((0, 32),))
    proj_bias = bell_draw(splits[14], (D,), 0.5, 3.0, ((0, 32),))
    up_bias = bell_draw(splits[15], (FF,), 0.5, 3.0, ((0, 32),))
    down_bias = bell_draw(splits[16], (D,), 0.5, 3.0, ((0, 32),))
    rel_table = bell_draw(splits[17], (RELS, HEADS), 1.0, 6.0)
    return {"tokens": tokens, "cotangent": cotangent, "counts": counts, "shifts": shifts, "qkv_weight": qkv_weight, "proj_weight": proj_weight, "up_weight": up_weight, "down_weight": down_weight, "first_gain": first_gain, "first_bias": first_bias, "second_gain": second_gain, "second_bias": second_bias, "query_bias": query_bias, "value_bias": value_bias, "proj_bias": proj_bias, "up_bias": up_bias, "down_bias": down_bias, "rel_table": rel_table}


@jax.custom_vjp
def low(v):
    return lax.optimization_barrier(v.astype(jnp.bfloat16)).astype(jnp.float32)

@jax.custom_vjp
def low_back(v):
    return v

def low_keep(v):
    return (low(v), None)

def low_pass(kept, grad):
    return (grad,)

def back_keep(v):
    return (v, None)

def back_low(kept, grad):
    return (low(grad),)
low.defvjp(low_keep, low_pass)
low_back.defvjp(back_keep, back_low)
EPS = 1e-06
HIGH = lax.Precision.HIGHEST
NEGATIVE = -1e+30

def window_index(shift_pair, visible_rows):
    across = GRID_F // WIN
    position = jnp.arange(GRID_T * GRID_F, dtype=jnp.int32)
    window_no = position // (WIN * WIN)
    inner_pos = position % (WIN * WIN)
    rolled_t = window_no // across * WIN + inner_pos // WIN
    rolled_f = window_no % across * WIN + inner_pos % WIN
    wide_t = rolled_t + shift_pair[0]
    wide_f = rolled_f + shift_pair[1]
    source_t = wide_t % GRID_T
    source_f = wide_f % GRID_F
    order_in = (source_t * GRID_F + source_f).astype(jnp.int32)
    region = (wide_t >= GRID_T).astype(jnp.int32) * 2 + (wide_f >= GRID_F).astype(jnp.int32)
    visible = source_t < visible_rows
    back_t = (position // GRID_F - shift_pair[0]) % GRID_T
    back_f = (position % GRID_F - shift_pair[1]) % GRID_F
    order_out = ((back_t // WIN * across + back_f // WIN) * (WIN * WIN) + back_t % WIN * WIN + back_f % WIN).astype(jnp.int32)
    return (order_in, order_out, region, visible)

def allowed_mask(region, visible):
    region = region.reshape(-1, WIN * WIN)
    visible = visible.reshape(-1, WIN * WIN)
    same_region = region[:, :, None] == region[:, None, :]
    diagonal_on = jnp.eye(WIN * WIN, dtype=bool)
    return same_region & (visible[:, None, :] | diagonal_on[None])

def offset_codes():
    inner_pos = jnp.arange(WIN * WIN, dtype=jnp.int32)
    row_diff = inner_pos[:, None] // WIN - inner_pos[None, :] // WIN + WIN - 1
    col_diff = inner_pos[:, None] % WIN - inner_pos[None, :] % WIN + WIN - 1
    return (row_diff * (2 * WIN - 1) + col_diff).astype(jnp.int32)

def layer_norm(values, gain, shift_b):
    row_mean = lax.optimization_barrier(jnp.mean(values, -1, keepdims=True))
    centred = values - row_mean
    variance = lax.optimization_barrier(jnp.mean(centred * centred, -1, keepdims=True))
    return centred * lax.rsqrt(variance + EPS) * gain + shift_b

def forward(x_rows, allowed, params):
    qkv_w, proj_w, up_w, down_w, gain_one, bias_one, gain_two, bias_two, q_bias, v_bias, p_bias, u_bias, d_bias, table = params
    width = x_rows.shape[1]
    windows = x_rows.shape[0] // (WIN * WIN)
    shape_w = (windows, WIN * WIN, HEADS, width // HEADS)
    act_one = low(layer_norm(x_rows, gain_one, bias_one))
    qkv_out = jnp.dot(act_one, qkv_w, precision=HIGH, preferred_element_type=jnp.float32)
    queries = low(low_back(qkv_out[:, :width] + q_bias)).reshape(shape_w)
    key_rows = low(low_back(qkv_out[:, width:2 * width])).reshape(shape_w)
    value_rows = low(low_back(qkv_out[:, 2 * width:] + v_bias)).reshape(shape_w)
    pos_bias = jnp.take(table, offset_codes().reshape(-1), axis=0).reshape(WIN * WIN, WIN * WIN, HEADS).transpose(2, 0, 1)
    scale = (width // HEADS) ** (-0.5)
    scores = jnp.einsum('wihd,wjhd->whij', queries, key_rows, precision=HIGH) * scale + pos_bias[None]
    scores = low_back(scores)
    mask_b = allowed[:, None]
    masked = jnp.where(mask_b, scores, NEGATIVE)
    row_top = lax.optimization_barrier(jnp.max(masked, -1, keepdims=True))
    exp_terms = jnp.where(mask_b, jnp.exp(masked - row_top), 0.0)
    probs = exp_terms / lax.optimization_barrier(jnp.sum(exp_terms, -1, keepdims=True))
    context = jnp.einsum('whij,wjhd->wihd', low(probs), value_rows, precision=HIGH).reshape(-1, width)
    context = low(low_back(context))
    branch = low_back(jnp.dot(context, proj_w, precision=HIGH, preferred_element_type=jnp.float32) + p_bias)
    mid = x_rows + branch
    act_two = low(layer_norm(mid, gain_two, bias_two))
    hidden = low_back(jnp.dot(act_two, up_w, precision=HIGH, preferred_element_type=jnp.float32) + u_bias)
    gelu_low = low(jax.nn.gelu(hidden, approximate=False))
    return mid + jnp.dot(gelu_low, down_w, precision=HIGH, preferred_element_type=jnp.float32) + d_bias

def reference(tokens, cotangent, counts, shifts, qkv_weight, proj_weight, up_weight, down_weight, first_gain, first_bias, second_gain, second_bias, query_bias, value_bias, proj_bias, up_bias, down_bias, rel_table):
    patches = GRID_T * GRID_F
    clip_total = counts.shape[0]
    group_size = 8
    rounds = clip_total // group_size
    order_in, order_out, region, visible = jax.vmap(window_index)(shifts, counts)
    params = tuple((weight.astype(jnp.float32) for weight in (qkv_weight, proj_weight, up_weight, down_weight, first_gain, first_bias, second_gain, second_bias, query_bias, value_bias, proj_bias, up_bias, down_bias, rel_table)))

    def regroup(array):
        return array.reshape((rounds, group_size) + array.shape[1:])
    scanned = (regroup(tokens.reshape(clip_total, patches, D)), regroup(cotangent.reshape(clip_total, patches, D)), regroup(order_in), regroup(order_out), regroup(region), regroup(visible))

    def one_group(totals, inputs):
        x_group, dy_group, in_group, out_group, reg_group, vis_group = inputs
        allowed = allowed_mask(reg_group, vis_group)
        x_rows = jnp.take_along_axis(x_group, in_group[:, :, None], axis=1).astype(jnp.float32).reshape(-1, D)
        dy_rows = jnp.take_along_axis(dy_group, in_group[:, :, None], axis=1).astype(jnp.float32).reshape(-1, D)
        result, pullback = jax.vjp(lambda inner_x, inner_p: forward(inner_x, allowed, inner_p), x_rows, params)
        grad_x, grad_params = pullback(dy_rows)
        result = jnp.take_along_axis(result.reshape(group_size, patches, D), out_group[:, :, None], axis=1)
        grad_x = jnp.take_along_axis(grad_x.reshape(group_size, patches, D), out_group[:, :, None], axis=1)
        totals = jax.tree.map(jnp.add, totals, grad_params)
        return (totals, (result.astype(jnp.bfloat16), grad_x))
    zeros = tuple((jnp.zeros_like(param) for param in params))
    totals, (outputs, grad_in) = lax.scan(one_group, zeros, scanned)
    return (outputs.reshape(-1, D), grad_in.reshape(-1, D), totals[0], totals[1], totals[2], totals[3], totals[4], totals[5], totals[6], totals[7], totals[8], totals[9], totals[10], totals[11], totals[12], totals[13])
```

```python
import functools

import jax
import jax.numpy as jnp
import numpy as np
from jax import lax
from jax.experimental import pallas as pl
from jax.experimental.pallas import tpu as pltpu
from jax.sharding import PartitionSpec as P

HEADS = 16
GRID_T = 64
GRID_F = 8
WIN = 4
PLACES = WIN * WIN
PATCHES = GRID_T * GRID_F
BLOCK = 64
BLOCKS = PATCHES // BLOCK
AXES = ("dp", "pair")

EPS = 1e-06
HIGH = lax.Precision.HIGHEST
NEGATIVE = -1e30
F32 = jnp.float32
BF16 = jnp.bfloat16
VMEM_BYTES = 60 * 1024 * 1024
ROWS = 32


def dot_nn(a, b):
    return lax.dot_general(a, b, (((1,), (0,)), ((), ())), preferred_element_type=F32)


def dot_nt(a, b):
    return lax.dot_general(a, b, (((1,), (1,)), ((), ())), preferred_element_type=F32)


def dot_tn(a, b):
    return lax.dot_general(a, b, (((0,), (0,)), ((), ())), preferred_element_type=F32)


def norm_stats(values):
    row_mean = jnp.mean(values, -1, keepdims=True)
    centred = values - row_mean
    inv_std = lax.rsqrt(jnp.mean(centred * centred, -1, keepdims=True) + EPS)
    return centred * inv_std, inv_std


def norm_back(grad_out, normed, inv_std, gain):
    grad_normed = grad_out * gain
    return inv_std * (
        grad_normed
        - jnp.mean(grad_normed, -1, keepdims=True)
        - normed * jnp.mean(grad_normed * normed, -1, keepdims=True)
    )


def iota(shape, dim):
    return lax.broadcasted_iota(jnp.int32, shape, dim)


def fill_perm(perm_ref, s, u, to_windows):
    for r0 in range(0, PATCHES, BLOCK):
        row = iota((BLOCK, 128), 0) + r0
        if to_windows:
            a = (row >> 2) & 3
            b = row & 3
            t = (4 * (row >> 5) + a + s) & (GRID_T - 1)
            f = (4 * ((row >> 4) & 1) + b + u) & (GRID_F - 1)
            source = t * GRID_F + f
        else:
            r = ((row >> 3) - s) & (GRID_T - 1)
            q = ((row & 7) - u) & (GRID_F - 1)
            source = (r >> 2) * 32 + (q >> 2) * 16 + (r & 3) * 4 + (q & 3)
        lane = iota((BLOCK, 128), 1)
        for c0 in range(0, PATCHES, 128):
            perm_ref[r0 : r0 + BLOCK, c0 : c0 + 128] = jnp.where(
                source == lane + c0, 1.0, 0.0
            ).astype(BF16)


def compact_code(rows):
    row = iota((rows, 128), 0)
    lane = iota((rows, 128), 1)
    return ((lane >> 4) - (row >> 4) - (lane >> 6)) & 3


def head_lanes(dtype):
    lane = iota((16, 128), 1) >> 5
    return [jnp.where(lane == hh, 1.0, 0.0).astype(dtype) for hh in range(4)]


def expand_rows(tile, g, lanes):
    parts = []
    for hh in range(4):
        half, ab = hh & 1, hh >> 1
        for slot in range(4):
            w = (slot - half - g - 2 * ab) % 4
            parts.append(tile[16 * w : 16 * w + 16, :] * lanes[hh])
    return jnp.concatenate(parts, axis=0)


def compact(code, s0, s1):
    return jnp.where(
        code == 0,
        s0[:, :128],
        jnp.where(code == 1, s1[:, :128], jnp.where(code == 2, s0[:, 128:], s1[:, 128:])),
    )


def lane_partner(x, k):
    lane = iota(x.shape, 1)
    return jnp.where((lane & k) == 0, pltpu.roll(x, 128 - k, 1), pltpu.roll(x, k, 1))


def group_max(x):
    for k in (1, 2, 4, 8):
        x = jnp.maximum(x, lane_partner(x, k))
    return x


def group_sum(x):
    for k in (1, 2, 4, 8):
        x = x + lane_partner(x, k)
    return x


def allowed_tile(block, s, u, count):
    row = iota((BLOCK, 128), 0)
    key = iota((BLOCK, 128), 1) & 15
    band = 4 * (2 * block + (row >> 5))
    side = 4 * ((row >> 4) & 1)
    r_i = band + ((row >> 2) & 3) + s
    q_i = side + (row & 3) + u
    r_j = band + (key >> 2) + s
    q_j = side + (key & 3) + u
    wrap_i = (r_i >> 6) * 2 + (q_i >> 3)
    wrap_j = (r_j >> 6) * 2 + (q_j >> 3)
    visible = ((r_j & (GRID_T - 1)) < count) | ((row & 15) == key)
    return (wrap_i == wrap_j) & visible


def attend_kernel(
    shift_ref, count_ref, tok_ref, w_ref, vec_ref, pos_ref,
    qkv_ref, prob_ref, ctx_ref,
    perm_ref, rows_ref, act_ref, score_ref, low_ref, ctxw_ref,
):
    width = tok_ref.shape[1]
    scale = (width // HEADS) ** (-0.5)
    clip = pl.program_id(0)
    s = shift_ref[clip, 0]
    u = shift_ref[clip, 1]
    count = count_ref[clip]
    fill_perm(perm_ref, s, u, True)
    rows_ref[...] = dot_nn(perm_ref[...], tok_ref[...])
    for r in range(0, PATCHES, ROWS):
        normed, _ = norm_stats(rows_ref[r : r + ROWS, :])
        act_ref[r : r + ROWS, :] = (normed * vec_ref[0:1, :] + vec_ref[1:2, :]).astype(BF16)
    for c in range(3):
        cols = slice(c * width, (c + 1) * width)
        out = dot_nn(act_ref[...], w_ref[:, cols])
        if c == 0:
            out = out + vec_ref[2:3, :]
        if c == 2:
            out = out + vec_ref[3:4, :]
        qkv_ref[:, cols] = out.astype(BF16)
    lanes = head_lanes(BF16)
    code = compact_code(BLOCK)
    for b in range(BLOCKS):
        rows = slice(b * BLOCK, (b + 1) * BLOCK)
        for p in range(2):
            parts = []
            for g in range(2):
                c0 = 128 * (2 * p + g)
                keys = expand_rows(qkv_ref[rows, width + c0 : width + c0 + 128], g, lanes)
                parts.append(dot_nt(qkv_ref[rows, c0 : c0 + 128], keys))
            score_ref[rows, 128 * p : 128 * p + 128] = compact(code, *parts)
    for b in range(BLOCKS):
        rows = slice(b * BLOCK, (b + 1) * BLOCK)
        allowed = allowed_tile(b, s, u, count)
        for p in range(2):
            cols = slice(128 * p, 128 * p + 128)
            logits = score_ref[rows, cols] * scale + pos_ref[:, cols]
            logits = jnp.where(allowed, logits, NEGATIVE)
            e = jnp.exp(logits - group_max(logits))
            prob = e * pl.reciprocal(group_sum(e))
            prob_ref[rows, cols] = prob
            low_ref[rows, cols] = prob.astype(BF16)
    spread = [jnp.where(code == e, 1.0, 0.0).astype(BF16) for e in range(4)]
    for b in range(BLOCKS):
        rows = slice(b * BLOCK, (b + 1) * BLOCK)
        for p in range(2):
            low = low_ref[rows, 128 * p : 128 * p + 128]
            for g in range(2):
                c0 = 128 * (2 * p + g)
                values = expand_rows(qkv_ref[rows, 2 * width + c0 : 2 * width + c0 + 128], g, lanes)
                wide = jnp.concatenate([low * spread[g], low * spread[2 + g]], axis=1)
                ctxw_ref[rows, c0 : c0 + 128] = dot_nn(wide, values).astype(BF16)
    fill_perm(perm_ref, s, u, False)
    ctx_ref[...] = dot_nn(perm_ref[...], ctxw_ref[...]).astype(BF16)


def mlp_kernel(
    tok_ref, ctx_ref, cot_ref, wp_ref, wu_ref, wd_ref, vec_ref, ub_ref,
    out_ref, gmid_ref, gctx_ref, gwp_ref, gwu_ref, gwd_ref, small_ref, gub_ref,
    accp_ref, accu_ref, accd_ref, mid_ref, act_ref, hid_ref, gg_ref, gl_ref, gh_ref, gact_ref, gb_ref,
):
    step = pl.program_id(0)
    tile = tok_ref.shape[0]
    ff = wu_ref.shape[1]
    chunk = 512

    @pl.when(step == 0)
    def _():
        accp_ref[...] = jnp.zeros_like(accp_ref)
        accu_ref[...] = jnp.zeros_like(accu_ref)
        accd_ref[...] = jnp.zeros_like(accd_ref)
        small_ref[...] = jnp.zeros_like(small_ref)
        gub_ref[...] = jnp.zeros_like(gub_ref)

    gain = vec_ref[0:1, :]
    bias = vec_ref[1:2, :]
    mid_ref[...] = dot_nn(ctx_ref[...], wp_ref[...])
    for r in range(0, tile, ROWS):
        rows = slice(r, r + ROWS)
        mid = mid_ref[rows, :] + tok_ref[rows, :].astype(F32) + vec_ref[2:3, :]
        mid_ref[rows, :] = mid
        normed, _ = norm_stats(mid)
        act_ref[rows, :] = (normed * gain + bias).astype(BF16)
    for c in range(0, ff, chunk):
        cols = slice(c, c + chunk)
        hid_ref[...] = dot_nn(act_ref[...], wu_ref[:, cols])
        gg_ref[...] = dot_nt(cot_ref[...], wd_ref[cols, :])
        for k in range(0, chunk, 128):
            lanes = slice(k, k + 128)
            total = jnp.zeros((1, 128), F32)
            for r in range(0, tile, 64):
                rows = slice(r, r + 64)
                h = hid_ref[rows, lanes] + ub_ref[0:1, c + k : c + k + 128]
                phi = 0.5 + 0.5 * lax.erf(h * (0.5**0.5))
                bell = jnp.exp(-0.5 * h * h) * 0.3989422804014327
                gl_ref[rows, lanes] = (h * phi).astype(BF16)
                g_hidden = (gg_ref[rows, lanes] * (phi + h * bell)).astype(BF16)
                gh_ref[rows, lanes] = g_hidden
                total = total + jnp.sum(g_hidden.astype(F32), 0, keepdims=True)
            gub_ref[0:1, c + k : c + k + 128] += total
        down = dot_nn(gl_ref[...], wd_ref[cols, :])
        back = dot_nt(gh_ref[...], wu_ref[:, cols])
        if c == 0:
            gb_ref[...] = down
            gact_ref[...] = back
        else:
            gb_ref[...] += down
            gact_ref[...] += back
        accd_ref[cols, :] += dot_tn(gl_ref[...], cot_ref[...])
        accu_ref[:, cols] += dot_tn(act_ref[...], gh_ref[...])
    sums = [jnp.zeros((1, tok_ref.shape[1]), F32) for _ in range(4)]
    for r in range(0, tile, ROWS):
        rows = slice(r, r + ROWS)
        mid = mid_ref[rows, :]
        out_ref[rows, :] = (mid + gb_ref[rows, :] + vec_ref[3:4, :]).astype(BF16)
        normed, inv = norm_stats(mid)
        g_act = gact_ref[rows, :]
        cot = cot_ref[rows, :].astype(F32)
        g_mid = cot + norm_back(g_act, normed, inv, gain)
        gmid_ref[rows, :] = g_mid
        g_branch = g_mid.astype(BF16)
        act_ref[rows, :] = g_branch
        sums[0] = sums[0] + jnp.sum(g_act * normed, 0, keepdims=True)
        sums[1] = sums[1] + jnp.sum(g_act, 0, keepdims=True)
        sums[2] = sums[2] + jnp.sum(g_branch.astype(F32), 0, keepdims=True)
        sums[3] = sums[3] + jnp.sum(cot, 0, keepdims=True)
    for i in range(4):
        small_ref[i : i + 1, :] += sums[i]
    gctx_ref[...] = dot_nt(act_ref[...], wp_ref[...]).astype(BF16)
    accp_ref[...] += dot_tn(ctx_ref[...], act_ref[...])

    @pl.when(step == pl.num_programs(0) - 1)
    def _():
        gwp_ref[...] = accp_ref[...].astype(BF16)
        gwu_ref[...] = accu_ref[...].astype(BF16)
        gwd_ref[...] = accd_ref[...].astype(BF16)


def attend_back_kernel(
    shift_ref, qkv_ref, prob_ref, gctx_ref, tok_ref, gmid_ref, w_ref, vec_ref,
    gtok_ref, gw_ref, small_ref, gpos_ref,
    acc_ref, perm_ref, do_ref, dp_ref, low_ref, gs_ref, lowt_ref, gst_ref, gqw_ref, gqn_ref, act_ref, gact_ref,
):
    width = tok_ref.shape[1]
    scale = (width // HEADS) ** (-0.5)
    clip = pl.program_id(0)
    s = shift_ref[clip, 0]
    u = shift_ref[clip, 1]

    @pl.when(clip == 0)
    def _():
        acc_ref[...] = jnp.zeros_like(acc_ref)
        small_ref[...] = jnp.zeros_like(small_ref)
        gpos_ref[...] = jnp.zeros_like(gpos_ref)

    fill_perm(perm_ref, s, u, True)
    do_ref[...] = dot_nn(perm_ref[...], gctx_ref[...]).astype(BF16)
    lanes = head_lanes(BF16)
    code = compact_code(BLOCK)
    for b in range(BLOCKS):
        rows = slice(b * BLOCK, (b + 1) * BLOCK)
        for p in range(2):
            parts = []
            for g in range(2):
                c0 = 128 * (2 * p + g)
                values = expand_rows(qkv_ref[rows, 2 * width + c0 : 2 * width + c0 + 128], g, lanes)
                parts.append(dot_nt(do_ref[rows, c0 : c0 + 128], values))
            dp_ref[rows, 128 * p : 128 * p + 128] = compact(code, *parts)
    for p in range(2):
        cols = slice(128 * p, 128 * p + 128)
        total = jnp.zeros((BLOCK, 128), F32)
        for b in range(BLOCKS):
            rows = slice(b * BLOCK, (b + 1) * BLOCK)
            prob = prob_ref[rows, cols]
            d_prob = dp_ref[rows, cols]
            g_scores = (prob * (d_prob - group_sum(prob * d_prob))).astype(BF16)
            gs_ref[rows, cols] = g_scores
            low_ref[rows, cols] = prob.astype(BF16)
            total = total + g_scores.astype(F32)
        gpos_ref[:, cols] += total
    spread = [jnp.where(code == e, 1.0, 0.0).astype(BF16) for e in range(4)]
    for b in range(BLOCKS):
        rows = slice(b * BLOCK, (b + 1) * BLOCK)
        for p in range(2):
            low = gs_ref[rows, 128 * p : 128 * p + 128]
            for g in range(2):
                c0 = 128 * (2 * p + g)
                keys = expand_rows(qkv_ref[rows, width + c0 : width + c0 + 128], g, lanes)
                wide = jnp.concatenate([low * spread[g], low * spread[2 + g]], axis=1)
                gqw_ref[rows, c0 : c0 + 128] = (dot_nn(wide, keys) * scale).astype(BF16)
    lowt_ref[...] = jnp.transpose(low_ref[...])
    gst_ref[...] = jnp.transpose(gs_ref[...])
    row_t = iota((BLOCK, 128), 0)
    lane_t = iota((BLOCK, 128), 1)
    code_t = ((row_t >> 4) - (lane_t >> 4)) & 3
    spread_t = [
        [jnp.where((code_t == d) & ((lane_t >> 6) == blk), 1.0, 0.0).astype(BF16) for d in range(4)]
        for blk in range(2)
    ]
    lane16 = iota((16, 128), 1) >> 5
    for source_ref, other_ref, other_at, out_at, factor in (
        (gst_ref, qkv_ref, 0, width, scale),
        (lowt_ref, do_ref, 0, 2 * width, 1.0),
    ):
        for two in range(BLOCKS // 2):
            places = slice(128 * two, 128 * two + 128)
            for p in range(2):
                halves = [source_ref[128 * p + 64 * h : 128 * p + 64 * h + 64, places] for h in range(2)]
                for g in range(2):
                    c0 = 128 * (2 * p + g)
                    parts = []
                    for blk in range(2):
                        for hh in range(4):
                            half, ab = hh & 1, hh >> 1
                            d = (g + 2 * ab + half) & 3
                            parts.append(halves[half] * spread_t[blk][d])
                    wide = dot_nn(
                        jnp.concatenate(parts, axis=0), other_ref[places, other_at + c0 : other_at + c0 + 128]
                    )
                    for blk in range(2):
                        for w in range(4):
                            pieces = []
                            for hh in range(4):
                                half, ab = hh & 1, hh >> 1
                                slot = (w + half + g + 2 * ab) & 3
                                at = 256 * blk + 64 * hh + 16 * slot
                                pieces.append(wide[at : at + 16, :])
                            total = jnp.where(
                                lane16 == 0,
                                pieces[0],
                                jnp.where(lane16 == 1, pieces[1], jnp.where(lane16 == 2, pieces[2], pieces[3])),
                            )
                            at = 128 * two + 64 * blk + 16 * w
                            gqw_ref[at : at + 16, out_at + c0 : out_at + c0 + 128] = (total * factor).astype(BF16)
    fill_perm(perm_ref, s, u, False)
    for c in range(3):
        cols = slice(c * width, (c + 1) * width)
        gqn_ref[:, cols] = dot_nn(perm_ref[...], gqw_ref[:, cols]).astype(BF16)
    for r in range(0, PATCHES, ROWS):
        rows = slice(r, r + ROWS)
        normed, _ = norm_stats(tok_ref[rows, :].astype(F32))
        act_ref[rows, :] = (normed * vec_ref[0:1, :] + vec_ref[1:2, :]).astype(BF16)
    gact_ref[...] = dot_nt(gqn_ref[...], w_ref[...])
    for c in range(3):
        cols = slice(c * width, (c + 1) * width)
        acc_ref[:, cols] += dot_tn(act_ref[...], gqn_ref[:, cols])
    sums = [jnp.zeros((1, width), F32) for _ in range(4)]
    for r in range(0, PATCHES, ROWS):
        rows = slice(r, r + ROWS)
        normed, inv = norm_stats(tok_ref[rows, :].astype(F32))
        g_act = gact_ref[rows, :]
        gtok_ref[rows, :] = gmid_ref[rows, :] + norm_back(g_act, normed, inv, vec_ref[0:1, :])
        sums[0] = sums[0] + jnp.sum(g_act * normed, 0, keepdims=True)
        sums[1] = sums[1] + jnp.sum(g_act, 0, keepdims=True)
        sums[2] = sums[2] + jnp.sum(gqn_ref[rows, :width].astype(F32), 0, keepdims=True)
        sums[3] = sums[3] + jnp.sum(gqn_ref[rows, 2 * width :].astype(F32), 0, keepdims=True)
    for i in range(4):
        small_ref[i : i + 1, :] += sums[i]

    @pl.when(clip == pl.num_programs(0) - 1)
    def _():
        gw_ref[...] = acc_ref[...].astype(BF16)


SMEM_SPEC = pl.BlockSpec(memory_space=pltpu.SMEM)


def rows_spec(rows, cols):
    return pl.BlockSpec((rows, cols), lambda i: (i, 0))


def whole_spec(shape):
    return pl.BlockSpec(shape, lambda i: (0,) * len(shape))


def struct(shape, dtype):
    return jax.ShapeDtypeStruct(shape, dtype)


def params():
    return pltpu.CompilerParams(vmem_limit_bytes=VMEM_BYTES, dimension_semantics=("arbitrary",))


def attend(shifts, counts, tokens, w_qkv, vec, pos):
    n, width = tokens.shape
    return pl.pallas_call(
        attend_kernel,
        grid=(n // PATCHES,),
        in_specs=[
            SMEM_SPEC, SMEM_SPEC, rows_spec(PATCHES, width),
            whole_spec(w_qkv.shape), whole_spec(vec.shape), whole_spec(pos.shape),
        ],
        out_specs=[rows_spec(PATCHES, 3 * width), rows_spec(PATCHES, 256), rows_spec(PATCHES, width)],
        out_shape=[struct((n, 3 * width), BF16), struct((n, 256), F32), struct((n, width), BF16)],
        scratch_shapes=[
            pltpu.VMEM((PATCHES, PATCHES), BF16),
            pltpu.VMEM((PATCHES, width), F32),
            pltpu.VMEM((PATCHES, width), BF16),
            pltpu.VMEM((PATCHES, 256), F32),
            pltpu.VMEM((PATCHES, 256), BF16),
            pltpu.VMEM((PATCHES, width), BF16),
        ],
        compiler_params=params(),
        name="attend",
    )(shifts, counts, tokens, w_qkv, vec, pos)


def mlp(tokens, ctx, cot, wp, wu, wd, vec, ub, tile=512):
    n, width = tokens.shape
    ff = wu.shape[1]
    return pl.pallas_call(
        mlp_kernel,
        grid=(n // tile,),
        in_specs=[rows_spec(tile, width)] * 3
        + [whole_spec(wp.shape), whole_spec(wu.shape), whole_spec(wd.shape), whole_spec(vec.shape), whole_spec(ub.shape)],
        out_specs=[rows_spec(tile, width)] * 3
        + [whole_spec(wp.shape), whole_spec(wu.shape), whole_spec(wd.shape), whole_spec((8, width)), whole_spec((8, ff))],
        out_shape=[
            struct((n, width), BF16), struct((n, width), F32), struct((n, width), BF16),
            struct(wp.shape, BF16), struct(wu.shape, BF16), struct(wd.shape, BF16),
            struct((8, width), F32), struct((8, ff), F32),
        ],
        scratch_shapes=[
            pltpu.VMEM((width, width), F32),
            pltpu.VMEM((width, ff), F32),
            pltpu.VMEM((ff, width), F32),
            pltpu.VMEM((tile, width), F32),
            pltpu.VMEM((tile, width), BF16),
            pltpu.VMEM((tile, 512), F32),
            pltpu.VMEM((tile, 512), F32),
            pltpu.VMEM((tile, 512), BF16),
            pltpu.VMEM((tile, 512), BF16),
            pltpu.VMEM((tile, width), F32),
            pltpu.VMEM((tile, width), F32),
        ],
        compiler_params=params(),
        name="mlp",
    )(tokens, ctx, cot, wp, wu, wd, vec, ub)


def attend_back(shifts, qkv, prob, gctx, tokens, gmid, w_qkv, vec):
    n, width = tokens.shape
    return pl.pallas_call(
        attend_back_kernel,
        grid=(n // PATCHES,),
        in_specs=[
            SMEM_SPEC, rows_spec(PATCHES, 3 * width), rows_spec(PATCHES, 256), rows_spec(PATCHES, width),
            rows_spec(PATCHES, width), rows_spec(PATCHES, width), whole_spec(w_qkv.shape), whole_spec(vec.shape),
        ],
        out_specs=[rows_spec(PATCHES, width), whole_spec(w_qkv.shape), whole_spec((8, width)), whole_spec((BLOCK, 256))],
        out_shape=[
            struct((n, width), F32), struct(w_qkv.shape, BF16), struct((8, width), F32), struct((BLOCK, 256), F32),
        ],
        scratch_shapes=[
            pltpu.VMEM(w_qkv.shape, F32),
            pltpu.VMEM((PATCHES, PATCHES), BF16),
            pltpu.VMEM((PATCHES, width), BF16),
            pltpu.VMEM((PATCHES, 256), F32),
            pltpu.VMEM((PATCHES, 256), BF16),
            pltpu.VMEM((PATCHES, 256), BF16),
            pltpu.VMEM((256, PATCHES), BF16),
            pltpu.VMEM((256, PATCHES), BF16),
            pltpu.VMEM((PATCHES, 3 * width), BF16),
            pltpu.VMEM((PATCHES, 3 * width), BF16),
            pltpu.VMEM((PATCHES, width), BF16),
            pltpu.VMEM((PATCHES, width), F32),
        ],
        compiler_params=params(),
        name="attend_back",
    )(shifts, qkv, prob, gctx, tokens, gmid, w_qkv, vec)


def offset_onehot():
    place = np.arange(PLACES)
    rows = place[:, None] // WIN - place[None, :] // WIN + WIN - 1
    cols = place[:, None] % WIN - place[None, :] % WIN + WIN - 1
    code = (rows * (2 * WIN - 1) + cols).reshape(-1)
    return (code[:, None] == np.arange((2 * WIN - 1) ** 2)[None, :]).astype(np.float32)


def head_spread():
    spread = np.zeros((HEADS * PLACES, 4, 2 * 128), np.float32)
    for w in range(4):
        for lane in range(256):
            p, half, slot, key = lane // 128, lane // 64 % 2, lane // 16 % 4, lane % 16
            e = (slot - w - half) % 4
            head = 8 * p + 4 * (e & 1) + 2 * (e >> 1) + half
            spread[head * PLACES + key, w, lane] = 1.0
    return spread.reshape(HEADS * PLACES, 1024)


def position_tile(table):
    by_pair = jnp.dot(jnp.asarray(offset_onehot()), table.astype(F32), precision=HIGH)
    by_row = by_pair.reshape(PLACES, PLACES, HEADS).transpose(0, 2, 1).reshape(PLACES, HEADS * PLACES)
    tiles = jnp.dot(by_row, jnp.asarray(head_spread()), precision=HIGH)
    return tiles.reshape(PLACES, 4, 256).transpose(1, 0, 2).reshape(BLOCK, 256)


def table_gradient(gpos):
    tiles = gpos.reshape(4, PLACES, 256).transpose(1, 0, 2).reshape(PLACES, 1024)
    by_row = jnp.dot(tiles, jnp.asarray(head_spread().T.copy()), precision=HIGH)
    by_pair = by_row.reshape(PLACES, HEADS, PLACES).transpose(0, 2, 1).reshape(PLACES * PLACES, HEADS)
    return jnp.dot(jnp.asarray(offset_onehot().T.copy()), by_pair, precision=HIGH)


def gather(x):
    return lax.all_gather(x, AXES, axis=0, tiled=True)


def scatter(x):
    return lax.psum_scatter(x, AXES, scatter_dimension=0, tiled=True)


def on_device(
    tokens, cotangent, counts, shifts, qkv_weight, proj_weight, up_weight, down_weight,
    first_gain, first_bias, second_gain, second_bias, query_bias, value_bias, proj_bias, up_bias, down_bias,
    rel_table,
):
    w_qkv = gather(qkv_weight)
    smalls = jnp.stack(
        [first_gain, first_bias, query_bias, value_bias, second_gain, second_bias, proj_bias, down_bias]
    )
    part = first_gain.shape[0]
    packed = jnp.concatenate([smalls.reshape(-1), up_bias])
    full = gather(packed[None]).astype(F32)
    vecs = full[:, : 8 * part].reshape(-1, 8, part).transpose(1, 0, 2).reshape(8, -1)
    ub = full[:, 8 * part :].reshape(1, -1)
    vec_one, vec_two = vecs[:4], vecs[4:]
    wp, wu, wd = gather(proj_weight), gather(up_weight), gather(down_weight)
    pos = position_tile(rel_table)
    qkv, prob, ctx = attend(shifts, counts, tokens, w_qkv, vec_one, pos)
    out, gmid, gctx, gwp, gwu, gwd, small_two, gub = mlp(tokens, ctx, cotangent, wp, wu, wd, vec_two, ub)
    gtok, gw_qkv, small_one, gpos = attend_back(shifts, qkv, prob, gctx, tokens, gmid, w_qkv, vec_one)
    table = lax.psum(table_gradient(gpos), AXES)
    ready = [scatter(x).astype(F32) for x in (gw_qkv, gwp, gwu, gwd)]
    rows = jnp.concatenate([small_one[:4], small_two[:4]])
    small = jnp.concatenate(
        [rows.reshape(8, -1, part).transpose(1, 0, 2).reshape(-1, 8 * part), gub[0].reshape(-1, up_bias.shape[0])], 1
    )
    mine = scatter(small)[0]
    grads = mine[: 8 * part].reshape(8, part)
    return (
        out, gtok, *ready,
        grads[0], grads[1], grads[4], grads[5], grads[2], grads[3], grads[6], mine[8 * part :], grads[7], table,
    )


def solution(mesh):
    sharded = P(AXES, None)
    line = P(AXES)
    in_specs = (sharded, sharded, line, sharded) + (sharded,) * 4 + (line,) * 9 + (P(),)
    out_specs = (sharded,) * 6 + (line,) * 9 + (P(),)
    return jax.shard_map(on_device, mesh=mesh, in_specs=in_specs, out_specs=out_specs, check_vma=False)
```

```python
import functools

import jax
import jax.numpy as jnp
import numpy as np
from jax import lax
from jax.experimental import pallas as pl
from jax.experimental.pallas import tpu as pltpu
from jax.sharding import PartitionSpec as P

HEADS = 16
GRID_T = 64
GRID_F = 8
WIN = 4
PLACES = WIN * WIN
PATCHES = GRID_T * GRID_F
BLOCK = 64
BLOCKS = PATCHES // BLOCK
AXES = ("dp", "pair")
UNIT = 16
SHARDS = 32
RELS = (2 * WIN - 1) ** 2
CORE = (2,)
PLANE = (4, 1, 5)
COLUMN = (8, 16, 24)

EPS = 1e-06
HIGH = lax.Precision.HIGHEST
NEGATIVE = -1e30
F32 = jnp.float32
BF16 = jnp.bfloat16
VMEM_BYTES = 60 * 1024 * 1024
ROWS = 32


def dot_nn(a, b):
    return lax.dot_general(a, b, (((1,), (0,)), ((), ())), preferred_element_type=F32)


def dot_nt(a, b):
    return lax.dot_general(a, b, (((1,), (1,)), ((), ())), preferred_element_type=F32)


def dot_tn(a, b):
    return lax.dot_general(a, b, (((0,), (0,)), ((), ())), preferred_element_type=F32)


def norm_stats(values):
    row_mean = jnp.mean(values, -1, keepdims=True)
    centred = values - row_mean
    inv_std = lax.rsqrt(jnp.mean(centred * centred, -1, keepdims=True) + EPS)
    return centred * inv_std, inv_std


def norm_back(grad_out, normed, inv_std, gain):
    grad_normed = grad_out * gain
    return inv_std * (
        grad_normed
        - jnp.mean(grad_normed, -1, keepdims=True)
        - normed * jnp.mean(grad_normed * normed, -1, keepdims=True)
    )


def iota(shape, dim):
    return lax.broadcasted_iota(jnp.int32, shape, dim)


def fill_perm(perm_ref, s, u, to_windows):
    for r0 in range(0, PATCHES, BLOCK):
        row = iota((BLOCK, 128), 0) + r0
        if to_windows:
            a = (row >> 2) & 3
            b = row & 3
            t = (4 * (row >> 5) + a + s) & (GRID_T - 1)
            f = (4 * ((row >> 4) & 1) + b + u) & (GRID_F - 1)
            source = t * GRID_F + f
        else:
            r = ((row >> 3) - s) & (GRID_T - 1)
            q = ((row & 7) - u) & (GRID_F - 1)
            source = (r >> 2) * 32 + (q >> 2) * 16 + (r & 3) * 4 + (q & 3)
        lane = iota((BLOCK, 128), 1)
        for c0 in range(0, PATCHES, 128):
            perm_ref[r0 : r0 + BLOCK, c0 : c0 + 128] = jnp.where(
                source == lane + c0, 1.0, 0.0
            ).astype(BF16)


def compact_code(rows):
    row = iota((rows, 128), 0)
    lane = iota((rows, 128), 1)
    return ((lane >> 4) - (row >> 4) - (lane >> 6)) & 3


def head_lanes(dtype):
    lane = iota((16, 128), 1) >> 5
    return [jnp.where(lane == hh, 1.0, 0.0).astype(dtype) for hh in range(4)]


def expand_rows(tile, g, lanes):
    parts = []
    for hh in range(4):
        half, ab = hh & 1, hh >> 1
        for slot in range(4):
            w = (slot - half - g - 2 * ab) % 4
            parts.append(tile[16 * w : 16 * w + 16, :] * lanes[hh])
    return jnp.concatenate(parts, axis=0)


def compact(code, s0, s1):
    return jnp.where(
        code == 0,
        s0[:, :128],
        jnp.where(code == 1, s1[:, :128], jnp.where(code == 2, s0[:, 128:], s1[:, 128:])),
    )


def lane_partner(x, k):
    lane = iota(x.shape, 1)
    return jnp.where((lane & k) == 0, pltpu.roll(x, 128 - k, 1), pltpu.roll(x, k, 1))


def group_max(x):
    for k in (1, 2, 4, 8):
        x = jnp.maximum(x, lane_partner(x, k))
    return x


def group_sum(x):
    for k in (1, 2, 4, 8):
        x = x + lane_partner(x, k)
    return x


def allowed_tile(block, s, u, count):
    row = iota((BLOCK, 128), 0)
    key = iota((BLOCK, 128), 1) & 15
    band = 4 * (2 * block + (row >> 5))
    side = 4 * ((row >> 4) & 1)
    r_i = band + ((row >> 2) & 3) + s
    q_i = side + (row & 3) + u
    r_j = band + (key >> 2) + s
    q_j = side + (key & 3) + u
    wrap_i = (r_i >> 6) * 2 + (q_i >> 3)
    wrap_j = (r_j >> 6) * 2 + (q_j >> 3)
    visible = ((r_j & (GRID_T - 1)) < count) | ((row & 15) == key)
    return (wrap_i == wrap_j) & visible


def device_id():
    return lax.axis_index("dp") * lax.axis_size("pair") + lax.axis_index("pair")


def place_code():
    row = iota((PLACES, 256), 0)
    key = iota((PLACES, 256), 1) & 15
    return ((row >> 2) - (key >> 2) + WIN - 1) * (2 * WIN - 1) + ((row & 3) - (key & 3) + WIN - 1)


def head_select(w):
    row = iota((256, 256), 0)
    lane = iota((256, 256), 1)
    half = (lane >> 6) & 1
    e = ((lane >> 4) - w - half) & 3
    head = 8 * (lane >> 7) + 4 * (e & 1) + 2 * (e >> 1) + half
    return jnp.where((row & 15 == lane & 15) & (row >> 4 == head), 1.0, 0.0).astype(BF16)


def head_repeat():
    return jnp.where(iota((HEADS, 256), 0) == iota((HEADS, 256), 1) >> 4, 1.0, 0.0).astype(BF16)


def fill_positions(pos_ref, table_ref):
    spread = dot_nn(table_ref[...], head_repeat())
    code = place_code()
    rows = jnp.zeros((PLACES, 256), F32)
    for e in range(RELS):
        rows = jnp.where(code == e, spread[e : e + 1, :], rows)
    rows = rows.astype(BF16)
    for w in range(4):
        pos_ref[16 * w : 16 * w + 16, :] = dot_nn(rows, head_select(w))


def split(x):
    high = x.astype(BF16)
    return high, (x - high.astype(F32)).astype(BF16)


def table_rows(gpos, scratch_ref):
    rows = jnp.zeros((PLACES, 256), F32)
    for w in range(4):
        select = head_select(w)
        for part in split(gpos[16 * w : 16 * w + 16, :]):
            rows = rows + dot_nt(part, select)
    code = place_code()
    scratch_ref[...] = jnp.zeros_like(scratch_ref)
    for e in range(RELS):
        scratch_ref[e : e + 1, :] = jnp.sum(jnp.where(code == e, rows, 0.0), 0, keepdims=True)
    repeat = head_repeat()
    high, low = split(scratch_ref[...])
    return dot_nt(repeat, high) + dot_nt(repeat, low)


def mix_matrix():
    row = iota((512, 512), 0)
    lane = iota((512, 512), 1)
    return jnp.where(row == 128 * ((lane >> 4) & 3) + 16 * (lane >> 6) + (lane & 15), 1.0, 0.0).astype(BF16)


def fetch_blocks(piece_refs, masks, full_ref, sems):
    if masks is None:
        copies = [pltpu.make_async_copy(piece_refs[0], full_ref, sems.at[0])]
    else:
        me = device_id()
        copies = []
        for piece, (start, piece_masks) in zip(piece_refs, masks):
            cols = pl.ds(start, piece.shape[1])
            for j, mask in enumerate(piece_masks):
                at = pl.multiple_of((me ^ mask) * UNIT, UNIT)
                copies.append(
                    pltpu.make_async_copy(
                        piece.at[pl.ds(j * UNIT, UNIT), :], full_ref.at[pl.ds(at, UNIT), cols], sems.at[len(copies)]
                    )
                )
    for copy in copies:
        copy.start()
    return copies


def block_place(device, relative):
    if not relative:
        return device
    rel = device ^ device_id()
    return ((rel >> 1) & 1) * 16 + ((rel & 1) * 2 + ((rel >> 2) & 1)) * 4 + (rel >> 3)


def put_block(send_refs, place, block):
    if len(send_refs) == 1:
        send_refs[0][UNIT * place : UNIT * place + UNIT, :] = block
        return
    half = SHARDS // 2
    at = pl.multiple_of((place & (half - 1)) * UNIT, UNIT)
    for k in range(2):

        @pl.when((place >= half) == bool(k))
        def _():
            send_refs[k][pl.ds(at, UNIT), :] = block


def pack_kernel(*refs):
    vectors, (qkv_ref, proj_ref, up_ref, down_ref, first_ref, second_ref, third_ref) = refs[:9], refs[9:]
    width = proj_ref.shape[1]
    first_ref[:, : 3 * width] = qkv_ref[...]
    rows = [v[...].astype(F32).reshape(1, UNIT) for v in vectors[:8]]
    bias = vectors[8][...].astype(F32).reshape(1, 4 * UNIT)
    rows += [bias[:, UNIT * q : UNIT * q + UNIT] for q in range(4)]
    rows = jnp.concatenate(rows + [jnp.zeros((116, UNIT), F32)], axis=0)
    first_ref[:, 3 * width :] = jnp.transpose(rows).astype(BF16)
    second_ref[:, :width] = proj_ref[...]
    second_ref[:, width : 5 * width] = up_ref[...]
    second_ref[:, 5 * width :] = down_ref[:UNIT, :]
    for q in range(3):
        third_ref[:, q * width : (q + 1) * width] = down_ref[UNIT * (q + 1) : UNIT * (q + 2), :]


def pack(vectors, weights):
    width = weights[1].shape[1]
    return pl.pallas_call(
        pack_kernel,
        out_shape=[struct((UNIT, cols * width + more), BF16) for cols, more in ((3, 128), (6, 0), (3, 0))],
        compiler_params=pltpu.CompilerParams(vmem_limit_bytes=VMEM_BYTES),
        name="pack",
    )(*vectors, *weights)


def attend_kernel(
    masks, start, shift_ref, count_ref, tok_ref, *refs
):
    if start:
        pos_in_ref, w_ref, vec_ref, _, _, _, qkv_ref, prob_ref, ctx_ref, *scratch = refs
        pos_ref = pos_in_ref
    else:
        table_ref, *refs = refs
        pieces = refs[: 1 if masks is None else len(masks)]
        qkv_ref, prob_ref, ctx_ref, w_ref, vec_ref, pos_ref, *scratch, sems = refs[len(pieces) :]
    perm_ref, rows_ref, act_ref, score_ref, low_ref, ctxw_ref = scratch
    width = tok_ref.shape[1]
    scale = (width // HEADS) ** (-0.5)
    clip = pl.program_id(0) + start
    s = shift_ref[clip, 0]
    u = shift_ref[clip, 1]
    count = count_ref[clip]

    def begin():
        copies = fetch_blocks(pieces, masks, w_ref, sems)
        fill_positions(pos_ref, table_ref)
        for copy in copies:
            copy.wait()
        vec_ref[...] = jnp.transpose(w_ref[:, 3 * width :].astype(F32))[:16, :]
        flat = vec_ref[8:16, :].astype(BF16)
        flat = jnp.concatenate(
            [
                jnp.concatenate([flat[q : q + 1, 128 * c : 128 * c + 128] for q in range(4)], axis=1)
                for c in range(4)
            ]
            + [jnp.zeros((12, width), BF16)],
            axis=0,
        )
        vec_ref[8:16, :] = dot_nn(flat, mix_matrix())[:8, :]

    if not start:
        pl.when(clip == 0)(begin)

    fill_perm(perm_ref, s, u, True)
    rows_ref[...] = dot_nn(perm_ref[...], tok_ref[...])
    for r in range(0, PATCHES, ROWS):
        normed, _ = norm_stats(rows_ref[r : r + ROWS, :])
        act_ref[r : r + ROWS, :] = (normed * vec_ref[0:1, :] + vec_ref[1:2, :]).astype(BF16)
    for c in range(3):
        cols = slice(c * width, (c + 1) * width)
        out = dot_nn(act_ref[...], w_ref[:, cols])
        if c == 0:
            out = out + vec_ref[2:3, :]
        if c == 2:
            out = out + vec_ref[3:4, :]
        qkv_ref[:, cols] = out.astype(BF16)
    lanes = head_lanes(BF16)
    code = compact_code(BLOCK)
    for b in range(BLOCKS):
        rows = slice(b * BLOCK, (b + 1) * BLOCK)
        for p in range(2):
            parts = []
            for g in range(2):
                c0 = 128 * (2 * p + g)
                keys = expand_rows(qkv_ref[rows, width + c0 : width + c0 + 128], g, lanes)
                parts.append(dot_nt(qkv_ref[rows, c0 : c0 + 128], keys))
            score_ref[rows, 128 * p : 128 * p + 128] = compact(code, *parts)
    for b in range(BLOCKS):
        rows = slice(b * BLOCK, (b + 1) * BLOCK)
        allowed = allowed_tile(b, s, u, count)
        for p in range(2):
            cols = slice(128 * p, 128 * p + 128)
            logits = score_ref[rows, cols] * scale + pos_ref[:, cols]
            logits = jnp.where(allowed, logits, NEGATIVE)
            e = jnp.exp(logits - group_max(logits))
            prob = e * pl.reciprocal(group_sum(e))
            prob_ref[rows, cols] = prob
            low_ref[rows, cols] = prob.astype(BF16)
    spread = [jnp.where(code == e, 1.0, 0.0).astype(BF16) for e in range(4)]
    for b in range(BLOCKS):
        rows = slice(b * BLOCK, (b + 1) * BLOCK)
        for p in range(2):
            low = low_ref[rows, 128 * p : 128 * p + 128]
            for g in range(2):
                c0 = 128 * (2 * p + g)
                values = expand_rows(qkv_ref[rows, 2 * width + c0 : 2 * width + c0 + 128], g, lanes)
                wide = jnp.concatenate([low * spread[g], low * spread[2 + g]], axis=1)
                ctxw_ref[rows, c0 : c0 + 128] = dot_nn(wide, values).astype(BF16)
    fill_perm(perm_ref, s, u, False)
    ctx_ref[...] = dot_nn(perm_ref[...], ctxw_ref[...]).astype(BF16)


def mlp_kernel(
    masks, relative, tok_ref, ctx_ref, cot_ref, vec_ref, *refs
):
    pieces = refs[: 1 if masks is None else len(masks)]
    (
        gelu_ref, gmid_ref, gctx_ref, *send_refs, small_ref, wp_out_ref, wd_out_ref,
        w_ref, wd_ref, accp_ref, accu_ref, accd_ref, mid_ref, act_ref, hid_ref, gg_ref, gh_ref, gact_ref,
        sems,
    ) = refs[len(pieces) :]
    keeps = [
        pltpu.make_async_copy(w_ref.at[:, : tok_ref.shape[1]], wp_out_ref, sems.at[0]),
        pltpu.make_async_copy(wd_ref, wd_out_ref, sems.at[1]),
    ]
    step = pl.program_id(0)
    tile, width = tok_ref.shape
    ff = 4 * width
    chunk = 512

    @pl.when(step == 0)
    def _():
        copies = fetch_blocks(pieces, masks, w_ref, sems)
        accp_ref[...] = jnp.zeros_like(accp_ref)
        accu_ref[...] = jnp.zeros_like(accu_ref)
        accd_ref[...] = jnp.zeros_like(accd_ref)
        small_ref[...] = jnp.zeros_like(small_ref)
        for copy in copies:
            copy.wait()
        for i in range(SHARDS):
            for q in range(4):
                at = UNIT * (4 * i + q)
                wd_ref[at : at + UNIT, :] = w_ref[UNIT * i : UNIT * i + UNIT, (5 + q) * width : (6 + q) * width]
        for keep in keeps:
            keep.start()

    gain = vec_ref[4:5, :]
    bias = vec_ref[5:6, :]
    mid_ref[...] = dot_nn(ctx_ref[...], w_ref[:, :width])
    for r in range(0, tile, ROWS):
        rows = slice(r, r + ROWS)
        mid = mid_ref[rows, :] + tok_ref[rows, :].astype(F32) + vec_ref[6:7, :]
        mid_ref[rows, :] = mid
        normed, _ = norm_stats(mid)
        act_ref[rows, :] = (normed * gain + bias).astype(BF16)
    for c in range(0, ff, chunk):
        cols = slice(c, c + chunk)
        up = slice(width + c, width + c + chunk)
        hid_ref[...] = dot_nn(act_ref[...], w_ref[:, up])
        gg_ref[...] = dot_nt(cot_ref[...], wd_ref[cols, :])
        for k in range(0, chunk, 128):
            lanes = slice(k, k + 128)
            total = jnp.zeros((1, 128), F32)
            for r in range(0, tile, 64):
                rows = slice(r, r + 64)
                h = hid_ref[rows, lanes] + vec_ref[8 + c // chunk : 9 + c // chunk, lanes]
                phi = 0.5 + 0.5 * lax.erf(h * (0.5**0.5))
                bell = jnp.exp(-0.5 * h * h) * 0.3989422804014327
                gelu_ref[rows, c + k : c + k + 128] = (h * phi).astype(BF16)
                g_hidden = (gg_ref[rows, lanes] * (phi + h * bell)).astype(BF16)
                gh_ref[rows, lanes] = g_hidden
                total = total + jnp.sum(g_hidden.astype(F32), 0, keepdims=True)
            small_ref[8 + c // chunk : 9 + c // chunk, lanes] += total
        back = dot_nt(gh_ref[...], w_ref[:, up])
        if c == 0:
            gact_ref[...] = back
        else:
            gact_ref[...] += back
        accd_ref[cols, :] += dot_tn(gelu_ref[:, cols], cot_ref[...])
        accu_ref[:, cols] += dot_tn(act_ref[...], gh_ref[...])
    sums = [jnp.zeros((1, tok_ref.shape[1]), F32) for _ in range(4)]
    for r in range(0, tile, ROWS):
        rows = slice(r, r + ROWS)
        mid = mid_ref[rows, :]
        normed, inv = norm_stats(mid)
        g_act = gact_ref[rows, :]
        cot = cot_ref[rows, :].astype(F32)
        g_mid = cot + norm_back(g_act, normed, inv, gain)
        gmid_ref[rows, :] = g_mid
        g_branch = g_mid.astype(BF16)
        act_ref[rows, :] = g_branch
        sums[0] = sums[0] + jnp.sum(g_act * normed, 0, keepdims=True)
        sums[1] = sums[1] + jnp.sum(g_act, 0, keepdims=True)
        sums[2] = sums[2] + jnp.sum(g_branch.astype(F32), 0, keepdims=True)
        sums[3] = sums[3] + jnp.sum(cot, 0, keepdims=True)
    for i in range(4):
        small_ref[4 + i : 5 + i, :] += sums[i]
    gctx_ref[...] = dot_nt(act_ref[...], w_ref[:, :width]).astype(BF16)
    accp_ref[...] += dot_tn(ctx_ref[...], act_ref[...])

    @pl.when(step == pl.num_programs(0) - 1)
    def _():
        for i in range(SHARDS):
            rows = slice(UNIT * i, UNIT * i + UNIT)
            block = [accp_ref[rows, :], accu_ref[rows, :]]
            block += [accd_ref[UNIT * (4 * i + q) : UNIT * (4 * i + q + 1), :] for q in range(4)]
            put_block(send_refs, block_place(i, relative), jnp.concatenate(block, axis=1).astype(BF16))
        for keep in keeps:
            keep.wait()


def attend_back_kernel(
    start, shift_ref, qkv_ref, prob_ref, gctx_ref, _, gqn_ref, gpos_ref,
    perm_ref, do_ref, dp_ref, low_ref, gs_ref, lowt_ref, gst_ref, gqw_ref,
):
    width = gctx_ref.shape[1]
    scale = (width // HEADS) ** (-0.5)
    step = pl.program_id(0)
    s = shift_ref[step + start, 0]
    u = shift_ref[step + start, 1]

    @pl.when(step == 0)
    def _():
        gpos_ref[...] = jnp.zeros_like(gpos_ref)

    fill_perm(perm_ref, s, u, True)
    do_ref[...] = dot_nn(perm_ref[...], gctx_ref[...]).astype(BF16)
    lanes = head_lanes(BF16)
    code = compact_code(BLOCK)
    for b in range(BLOCKS):
        rows = slice(b * BLOCK, (b + 1) * BLOCK)
        for p in range(2):
            parts = []
            for g in range(2):
                c0 = 128 * (2 * p + g)
                values = expand_rows(qkv_ref[rows, 2 * width + c0 : 2 * width + c0 + 128], g, lanes)
                parts.append(dot_nt(do_ref[rows, c0 : c0 + 128], values))
            dp_ref[rows, 128 * p : 128 * p + 128] = compact(code, *parts)
    for p in range(2):
        cols = slice(128 * p, 128 * p + 128)
        total = jnp.zeros((BLOCK, 128), F32)
        for b in range(BLOCKS):
            rows = slice(b * BLOCK, (b + 1) * BLOCK)
            prob = prob_ref[rows, cols]
            d_prob = dp_ref[rows, cols]
            g_scores = (prob * (d_prob - group_sum(prob * d_prob))).astype(BF16)
            gs_ref[rows, cols] = g_scores
            low_ref[rows, cols] = prob.astype(BF16)
            total = total + g_scores.astype(F32)
        gpos_ref[:, cols] += total
    spread = [jnp.where(code == e, 1.0, 0.0).astype(BF16) for e in range(4)]
    for b in range(BLOCKS):
        rows = slice(b * BLOCK, (b + 1) * BLOCK)
        for p in range(2):
            low = gs_ref[rows, 128 * p : 128 * p + 128]
            for g in range(2):
                c0 = 128 * (2 * p + g)
                keys = expand_rows(qkv_ref[rows, width + c0 : width + c0 + 128], g, lanes)
                wide = jnp.concatenate([low * spread[g], low * spread[2 + g]], axis=1)
                gqw_ref[rows, c0 : c0 + 128] = (dot_nn(wide, keys) * scale).astype(BF16)
    lowt_ref[...] = jnp.transpose(low_ref[...])
    gst_ref[...] = jnp.transpose(gs_ref[...])
    row_t = iota((BLOCK, 128), 0)
    lane_t = iota((BLOCK, 128), 1)
    code_t = ((row_t >> 4) - (lane_t >> 4)) & 3
    spread_t = [
        [jnp.where((code_t == d) & ((lane_t >> 6) == blk), 1.0, 0.0).astype(BF16) for d in range(4)]
        for blk in range(2)
    ]
    lane16 = iota((16, 128), 1) >> 5
    for source_ref, other_ref, other_at, out_at, factor in (
        (gst_ref, qkv_ref, 0, width, scale),
        (lowt_ref, do_ref, 0, 2 * width, 1.0),
    ):
        for two in range(BLOCKS // 2):
            places = slice(128 * two, 128 * two + 128)
            for p in range(2):
                halves = [source_ref[128 * p + 64 * h : 128 * p + 64 * h + 64, places] for h in range(2)]
                for g in range(2):
                    c0 = 128 * (2 * p + g)
                    parts = []
                    for blk in range(2):
                        for hh in range(4):
                            half, ab = hh & 1, hh >> 1
                            d = (g + 2 * ab + half) & 3
                            parts.append(halves[half] * spread_t[blk][d])
                    wide = dot_nn(
                        jnp.concatenate(parts, axis=0), other_ref[places, other_at + c0 : other_at + c0 + 128]
                    )
                    for blk in range(2):
                        for w in range(4):
                            pieces = []
                            for hh in range(4):
                                half, ab = hh & 1, hh >> 1
                                slot = (w + half + g + 2 * ab) & 3
                                at = 256 * blk + 64 * hh + 16 * slot
                                pieces.append(wide[at : at + 16, :])
                            total = jnp.where(
                                lane16 == 0,
                                pieces[0],
                                jnp.where(lane16 == 1, pieces[1], jnp.where(lane16 == 2, pieces[2], pieces[3])),
                            )
                            at = 128 * two + 64 * blk + 16 * w
                            gqw_ref[at : at + 16, out_at + c0 : out_at + c0 + 128] = (total * factor).astype(BF16)
    fill_perm(perm_ref, s, u, False)
    for c in range(3):
        cols = slice(c * width, (c + 1) * width)
        gqn_ref[:, cols] = dot_nn(perm_ref[...], gqw_ref[:, cols]).astype(BF16)


def project_back_kernel(
    relative, gqn_ref, tok_ref, w_ref, small_in_ref, gpos_a_ref, gpos_b_ref, *refs
):
    *send_refs, acc_ref, norm_ref, small_ref, sum_ref, scratch_ref = refs
    width = tok_ref.shape[1]
    step = pl.program_id(0)

    @pl.when(step == 0)
    def _():
        acc_ref[...] = jnp.zeros_like(acc_ref)
        sum_ref[...] = jnp.zeros_like(sum_ref)
        small_ref[...] = jnp.zeros_like(small_ref)
        small_ref[:16, :] = small_in_ref[...]

    for r in range(0, tok_ref.shape[0], ROWS):
        rows = slice(r, r + ROWS)
        normed, _ = norm_stats(tok_ref[rows, :].astype(F32))
        norm_ref[rows, :] = normed.astype(BF16)
    for c in range(3):
        cols = slice(c * width, (c + 1) * width)
        acc_ref[:, cols] += dot_tn(norm_ref[...], gqn_ref[:, cols])
        total = jnp.zeros((1, width), F32)
        for r in range(0, tok_ref.shape[0], ROWS):
            total = total + jnp.sum(gqn_ref[r : r + ROWS, cols].astype(F32), 0, keepdims=True)
        sum_ref[0:1, cols] += total

    @pl.when(step == pl.num_programs(0) - 1)
    def _():
        small_ref[2:3, :] = sum_ref[0:1, :width]
        small_ref[3:4, :] = sum_ref[0:1, 2 * width :]
        bias = small_ref[8:16, :].astype(BF16)
        flat = dot_nt(bias, mix_matrix())
        for q in range(4):
            small_ref[8 + q : 9 + q, :] = jnp.concatenate(
                [flat[c : c + 1, 128 * q : 128 * q + 128] for c in range(4)], axis=1
            )
        table = table_rows(gpos_a_ref[...] + gpos_b_ref[...], scratch_ref)
        extra = jnp.concatenate([jnp.zeros((UNIT, 16), F32), table, jnp.zeros((UNIT, 48), F32)], axis=1)
        small = jnp.transpose(small_ref[...])
        lane = iota((UNIT, 128), 1)
        for i in range(SHARDS):
            rows = slice(UNIT * i, UNIT * i + UNIT)
            weight = w_ref[rows, : 3 * width].astype(F32)
            gain = w_ref[rows, 3 * width : 3 * width + 1].astype(F32)
            bias = w_ref[rows, 3 * width + 1 : 3 * width + 2].astype(F32)
            product = acc_ref[rows, :]
            total = sum_ref[0:1, :]
            g_gain = jnp.sum(product * weight, 1, keepdims=True)
            g_bias = jnp.sum(total * weight, 1, keepdims=True)
            tail = jnp.where(lane == 0, g_gain, jnp.where(lane == 1, g_bias, small[rows, :] + extra))
            block = jnp.concatenate([gain * product + bias * total, tail], axis=1)
            put_block(send_refs, block_place(i, relative), block.astype(BF16))


def token_back_kernel(gqn_ref, tok_ref, gmid_ref, w_ref, vec_ref, gtok_ref, gact_ref):
    width = tok_ref.shape[1]
    gact_ref[...] = dot_nt(gqn_ref[...], w_ref[:, : 3 * width])
    for r in range(0, tok_ref.shape[0], ROWS):
        rows = slice(r, r + ROWS)
        normed, inv = norm_stats(tok_ref[rows, :].astype(F32))
        gtok_ref[rows, :] = gmid_ref[rows, :] + norm_back(gact_ref[rows, :], normed, inv, vec_ref[0:1, :])


def output_kernel(gelu_ref, ctx_ref, tok_ref, wp_ref, wd_ref, vec_ref, out_ref, acc_ref):
    acc_ref[...] = dot_nn(gelu_ref[...], wd_ref[...]) + dot_nn(ctx_ref[...], wp_ref[...])
    bias = vec_ref[6:7, :] + vec_ref[7:8, :]
    for r in range(0, tok_ref.shape[0], ROWS):
        rows = slice(r, r + ROWS)
        out_ref[rows, :] = (acc_ref[rows, :] + tok_ref[rows, :].astype(F32) + bias).astype(BF16)


SMEM_SPEC = pl.BlockSpec(memory_space=pltpu.SMEM)
ANY_SPEC = pl.BlockSpec(memory_space=pl.ANY)


def rows_spec(rows, cols):
    return pl.BlockSpec((rows, cols), lambda i: (i, 0))


def whole_spec(shape):
    return pl.BlockSpec(shape, lambda i: (0,) * len(shape))


def struct(shape, dtype):
    return jax.ShapeDtypeStruct(shape, dtype)


def cost(flops, nbytes):
    return pl.CostEstimate(flops=flops, bytes_accessed=nbytes, transcendentals=0)


def params():
    return pltpu.CompilerParams(vmem_limit_bytes=VMEM_BYTES, dimension_semantics=("arbitrary",))


def attend_scratch(width):
    return [
        pltpu.VMEM((PATCHES, PATCHES), BF16),
        pltpu.VMEM((PATCHES, width), F32),
        pltpu.VMEM((PATCHES, width), BF16),
        pltpu.VMEM((PATCHES, 256), F32),
        pltpu.VMEM((PATCHES, 256), BF16),
        pltpu.VMEM((PATCHES, width), BF16),
    ]


def clip_spec(cols, start):
    return pl.BlockSpec((PATCHES, cols), lambda i: (i + start, 0))


def attend(shifts, counts, tokens, table, pieces, masks, clips):
    n, width = tokens.shape
    cols = 3 * width + 128
    return pl.pallas_call(
        functools.partial(attend_kernel, masks, 0),
        grid=(clips,),
        in_specs=[SMEM_SPEC, SMEM_SPEC, rows_spec(PATCHES, width), whole_spec(table.shape)] + [ANY_SPEC] * len(pieces),
        out_specs=[
            rows_spec(PATCHES, 3 * width), rows_spec(PATCHES, 256), rows_spec(PATCHES, width),
            whole_spec((width, cols)), whole_spec((16, width)), whole_spec((BLOCK, 256)),
        ],
        out_shape=[
            struct((n, 3 * width), BF16), struct((n, 256), F32), struct((n, width), BF16),
            struct((width, cols), BF16), struct((16, width), F32), struct((BLOCK, 256), F32),
        ],
        scratch_shapes=attend_scratch(width) + [pltpu.SemaphoreType.DMA((SHARDS,))],
        compiler_params=params(),
        cost_estimate=cost(700000000 * clips, n * width),
        name="attend",
    )(shifts, counts, tokens, table, *pieces)


def attend_more(shifts, counts, tokens, pos, w_qkv, vec, into, start):
    n, width = tokens.shape
    return pl.pallas_call(
        functools.partial(attend_kernel, None, start),
        grid=(n // PATCHES - start,),
        in_specs=[SMEM_SPEC, SMEM_SPEC, clip_spec(width, start)]
        + [whole_spec(x.shape) for x in (pos, w_qkv, vec)]
        + [ANY_SPEC] * 3,
        out_specs=[clip_spec(3 * width, start), clip_spec(256, start), clip_spec(width, start)],
        out_shape=[struct((n, 3 * width), BF16), struct((n, 256), F32), struct((n, width), BF16)],
        scratch_shapes=attend_scratch(width),
        input_output_aliases={6: 0, 7: 1, 8: 2},
        compiler_params=params(),
        cost_estimate=cost(700000000, n * width),
        name="attend_more",
    )(shifts, counts, tokens, pos, w_qkv, vec, *into)


def send_shapes(cols, relative):
    rows = SHARDS * UNIT
    return [struct((rows // 2, cols), BF16)] * 2 if relative else [struct((rows, cols), BF16)]


def mlp(tokens, ctx, cot, vec, pieces, masks, relative, tile=512):
    n, width = tokens.shape
    cols = 9 * width
    ff = 4 * width
    sends = send_shapes(cols, relative)
    return pl.pallas_call(
        functools.partial(mlp_kernel, masks, relative),
        grid=(n // tile,),
        in_specs=[rows_spec(tile, width)] * 3 + [whole_spec(vec.shape)] + [ANY_SPEC] * len(pieces),
        out_specs=[rows_spec(tile, ff), rows_spec(tile, width), rows_spec(tile, width)]
        + [whole_spec(x.shape) for x in sends]
        + [whole_spec((16, width)), ANY_SPEC, ANY_SPEC],
        out_shape=[
            struct((n, ff), BF16), struct((n, width), F32), struct((n, width), BF16),
            *sends, struct((16, width), F32), struct((width, width), BF16), struct((ff, width), BF16),
        ],
        scratch_shapes=[
            pltpu.VMEM((width, cols), BF16),
            pltpu.VMEM((ff, width), BF16),
            pltpu.VMEM((width, width), F32),
            pltpu.VMEM((width, ff), F32),
            pltpu.VMEM((ff, width), F32),
            pltpu.VMEM((tile, width), F32),
            pltpu.VMEM((tile, width), BF16),
            pltpu.VMEM((tile, 512), F32),
            pltpu.VMEM((tile, 512), F32),
            pltpu.VMEM((tile, 512), BF16),
            pltpu.VMEM((tile, width), F32),
            pltpu.SemaphoreType.DMA((2 * SHARDS,)),
        ],
        compiler_params=params(),
        cost_estimate=cost(5000000000, n * width),
        name="mlp",
    )(tokens, ctx, cot, vec, *pieces)


def attend_back(shifts, qkv, prob, gctx, into, start, clips):
    n, width = gctx.shape

    def spec(cols):
        return pl.BlockSpec((PATCHES, cols), lambda i: (i + start, 0))

    return pl.pallas_call(
        functools.partial(attend_back_kernel, start),
        grid=(clips,),
        in_specs=[SMEM_SPEC, spec(3 * width), spec(256), spec(width), ANY_SPEC],
        out_specs=[spec(3 * width), whole_spec((BLOCK, 256))],
        out_shape=[struct((n, 3 * width), BF16), struct((BLOCK, 256), F32)],
        scratch_shapes=[
            pltpu.VMEM((PATCHES, PATCHES), BF16),
            pltpu.VMEM((PATCHES, width), BF16),
            pltpu.VMEM((PATCHES, 256), F32),
            pltpu.VMEM((PATCHES, 256), BF16),
            pltpu.VMEM((PATCHES, 256), BF16),
            pltpu.VMEM((256, PATCHES), BF16),
            pltpu.VMEM((256, PATCHES), BF16),
            pltpu.VMEM((PATCHES, 3 * width), BF16),
        ],
        input_output_aliases={} if into is None else {4: 0},
        compiler_params=params(),
        cost_estimate=cost(700000000 * clips, n * width),
        name="attend_back",
    )(shifts, qkv, prob, gctx, prob if into is None else into)


def project_back(gqn, tokens, w_qkv, small, gpos_a, gpos_b, relative, tile=512):
    n, width = tokens.shape
    sends = send_shapes(w_qkv.shape[1], relative)
    return pl.pallas_call(
        functools.partial(project_back_kernel, relative),
        grid=(n // tile,),
        in_specs=[rows_spec(tile, 3 * width), rows_spec(tile, width)]
        + [whole_spec(x.shape) for x in (w_qkv, small, gpos_a, gpos_b)],
        out_specs=[whole_spec(x.shape) for x in sends],
        out_shape=sends,
        scratch_shapes=[
            pltpu.VMEM((width, 3 * width), F32),
            pltpu.VMEM((tile, width), BF16),
            pltpu.VMEM((128, width), F32),
            pltpu.VMEM((8, 3 * width), F32),
            pltpu.VMEM((64, 256), F32),
        ],
        compiler_params=params(),
        cost_estimate=cost(1000000000, n * width),
        name="project_back",
    )(gqn, tokens, w_qkv, small, gpos_a, gpos_b)


def token_back(gqn, tokens, gmid, w_qkv, vec, tile=512):
    n, width = tokens.shape
    return pl.pallas_call(
        token_back_kernel,
        grid=(n // tile,),
        in_specs=[rows_spec(tile, 3 * width), rows_spec(tile, width), rows_spec(tile, width)]
        + [whole_spec(w_qkv.shape), whole_spec(vec.shape)],
        out_specs=rows_spec(tile, width),
        out_shape=struct((n, width), F32),
        scratch_shapes=[pltpu.VMEM((tile, width), F32)],
        compiler_params=params(),
        cost_estimate=cost(1000000000, n * width),
        name="token_back",
    )(gqn, tokens, gmid, w_qkv, vec)


def output(gelu, ctx, tokens, wp, wd, vec, tile=512):
    n, width = tokens.shape
    return pl.pallas_call(
        output_kernel,
        grid=(n // tile,),
        in_specs=[rows_spec(tile, gelu.shape[1]), rows_spec(tile, width), rows_spec(tile, width)]
        + [whole_spec(x.shape) for x in (wp, wd, vec)],
        out_specs=rows_spec(tile, width),
        out_shape=struct((n, width), BF16),
        scratch_shapes=[pltpu.VMEM((tile, width), F32)],
        compiler_params=params(),
        cost_estimate=cost(1000000000, n * width),
        name="output",
    )(gelu, ctx, tokens, wp, wd, vec)


def finish_kernel(*refs):
    first, second = refs[:4], refs[4:8]
    gqkv_ref, gproj_ref, gup_ref, gdown_ref, *vector_refs, table_ref = refs[8:]
    width = gproj_ref.shape[1]

    def total(parts, cols):
        a, b, c, d = (part[:, cols].astype(F32) for part in parts)
        return (a + b) + (c + d)

    gqkv_ref[...] = total(first, slice(0, 3 * width))
    gproj_ref[...] = total(second, slice(0, width))
    gup_ref[...] = total(second, slice(width, 5 * width))
    for q in range(4):
        gdown_ref[UNIT * q : UNIT * q + UNIT, :] = total(second, slice((5 + q) * width, (6 + q) * width))
    extra = total(first, slice(3 * width, 3 * width + 128))
    rows = jnp.transpose(extra)
    for i in range(8):
        vector_refs[i][...] = rows[i, :]
    vector_refs[8][...] = jnp.concatenate([rows[8 + q : 9 + q, :] for q in range(4)], axis=1)[0]
    table_ref[...] = rows[16 : 16 + RELS, :]


def finish(first, second):
    width = second[0].shape[1] // 9
    return pl.pallas_call(
        finish_kernel,
        out_shape=[
            struct((UNIT, 3 * width), F32), struct((UNIT, width), F32), struct((UNIT, 4 * width), F32),
            struct((4 * UNIT, width), F32),
            *[struct((UNIT,), F32)] * 8, struct((4 * UNIT,), F32), struct((RELS, HEADS), F32),
        ],
        compiler_params=pltpu.CompilerParams(vmem_limit_bytes=VMEM_BYTES),
        name="finish",
    )(*first, *second)


def exchange(x, mask):
    size = lax.axis_size(AXES)
    return lax.ppermute(x, AXES, [(i, i ^ mask) for i in range(size)])


def spread_near(own, masks):
    return jnp.concatenate([own] + [exchange(own, m) for m in masks], axis=0)


def spread_far(block, masks):
    return [block] + [exchange(block, m) for m in masks]


def spread_core(pieces):
    return pieces + [exchange(x, CORE[0]) for x in pieces]


def piece_masks(near, far, start):
    return tuple((start, tuple(n ^ f ^ core for n in (0,) + near)) for core in (0,) + CORE for f in (0,) + far)


def add(*parts):
    parts = [p.astype(F32) for p in parts]
    while len(parts) > 1:
        parts = [parts[i] + parts[i + 1] for i in range(0, len(parts), 2)]
    return parts[0].astype(BF16)


def meet_core(keep, send):
    got = exchange(send, CORE[0])
    quarter = keep.shape[0] // 4
    return [add(keep[quarter * k : quarter * (k + 1)], got[quarter * k : quarter * (k + 1)]) for k in range(4)]


def meet_far(groups, masks):
    return [groups[0]] + [exchange(group, mask) for group, mask in zip(groups[1:], masks)]


def add_blocks(parts):
    return [add(*[p[UNIT * k : UNIT * (k + 1)] for p in parts]) for k in range(4)]


def gather(x):
    return lax.all_gather(x, AXES, axis=0, tiled=True)


def scatter(x):
    return lax.psum_scatter(x, AXES, scatter_dimension=0, tiled=True)


def by_unit(x):
    return jnp.moveaxis(x.reshape((SHARDS, 4, UNIT) + x.shape[1:]), 1, 2).reshape((SHARDS * UNIT, 4) + x.shape[1:])


def by_row(x):
    return jnp.moveaxis(x.reshape((SHARDS, UNIT, 4) + x.shape[2:]), 2, 1).reshape((4 * SHARDS * UNIT,) + x.shape[2:])


def whole_weights(vectors, weights):
    columns = [gather(v)[:, None] for v in vectors[:8]] + [by_unit(gather(vectors[8]))]
    extra = jnp.concatenate(columns, axis=1)
    qkv, proj, up, down = (gather(w) for w in weights)
    first = jnp.concatenate([qkv, extra, jnp.zeros((qkv.shape[0], 128 - extra.shape[1]), BF16)], axis=1)
    second = jnp.concatenate([proj, up, by_unit(down).reshape(proj.shape[0], -1)], axis=1)
    return first, second


def whole_grads(first, second):
    width = second.shape[1] // 9
    mats = [first[:, : 3 * width], second[:, :width], second[:, width : 5 * width]]
    mats.append(by_row(second[:, 5 * width :].reshape(-1, 4, width)))
    extra = first[:, 3 * width :]
    vectors = [extra[:, k] for k in range(8)] + [by_row(extra[:, 8:12])]
    table = lax.psum(extra[:UNIT, 16 : 16 + RELS].astype(F32), AXES).T
    return [scatter(x).astype(F32) for x in mats] + [scatter(x.astype(F32)) for x in vectors] + [table]


def local_test(
    tokens, cotangent, counts, shifts, qkv, proj, up, down, vec1, vec2, ub, table,
):
    extra = jnp.concatenate([vec1, vec2], axis=0).T
    extra = jnp.concatenate([extra, by_unit(ub[0]), jnp.zeros((512, 116))], axis=1).astype(BF16)
    first = jnp.concatenate([qkv, extra], axis=1)
    second = jnp.concatenate([proj, up, by_unit(down).reshape(512, -1)], axis=1)
    *kept, w_qkv, vec, pos = attend(shifts, counts, tokens, table, [first], None, 3)
    q, prob, ctx = attend_more(shifts, counts, tokens, pos, w_qkv, vec, kept, 3)
    gelu, gmid, gctx, gsecond, small, wp, wd = mlp(tokens, ctx, cotangent, vec, [second], None, False)
    gqn, gpos_a = attend_back(shifts, q, prob, gctx, None, 0, 2)
    gqn, gpos_b = attend_back(shifts, q, prob, gctx, gqn, 2, 2)
    (gfirst,) = project_back(gqn, tokens, w_qkv, small, gpos_a, gpos_b, False)
    gtok = token_back(gqn, tokens, gmid, w_qkv, vec)
    out = output(gelu, ctx, tokens, wp, wd, vec)
    width = 512
    e = gfirst[:, 1536:]
    mats = [gfirst[:, :1536], gsecond[:, :width], gsecond[:, width : 5 * width], by_row(gsecond[:, 5 * width :].reshape(-1, 4, width))]
    v = [e[:, k] for k in range(8)]
    return [out, gtok] + mats + [v[0], v[1], v[4], v[5], v[2], v[3], v[6], by_row(e[:, 8:12]), v[7], e[:16, 16:65].T]


def on_device(
    tokens, cotangent, counts, shifts, qkv_weight, proj_weight, up_weight, down_weight,
    first_gain, first_bias, second_gain, second_bias, query_bias, value_bias, proj_bias, up_bias, down_bias,
    rel_table,
):
    vectors = [first_gain, first_bias, query_bias, value_bias, second_gain, second_bias, proj_bias, down_bias, up_bias]
    weights = [qkv_weight, proj_weight, up_weight, down_weight]
    stepped = lax.axis_size(AXES) == SHARDS
    if stepped:
        first, second, third = pack(vectors, weights)
        first_masks = piece_masks(COLUMN, PLANE, 0)
        second_masks = piece_masks(COLUMN, PLANE, 0) + piece_masks(PLANE, COLUMN, second.shape[1])
        first = spread_near(first, COLUMN)
        third = spread_near(third, PLANE)
        second = spread_near(second, COLUMN)
        first, second, third = lax.optimization_barrier((spread_far(first, PLANE), second, third))
        first = spread_core(first)
        third = spread_far(third, COLUMN)
        second = spread_far(second, PLANE)
    else:
        first, second = ([x] for x in whole_weights(vectors, weights))
        first_masks = second_masks = None
    clips = counts.shape[0]
    early = max(1, 3 * clips // 4)
    *kept, w_qkv, vec, pos = attend(shifts, counts, tokens, rel_table, first, first_masks, early)
    if stepped:
        kept, second, third = lax.optimization_barrier((kept, second, third))
        second = spread_core(second) + spread_core(third)
    qkv, prob, ctx = attend_more(shifts, counts, tokens, pos, w_qkv, vec, kept, early)
    gelu, gmid, gctx, *gsecond, small, wp, wd = mlp(tokens, ctx, cotangent, vec, second, second_masks, stepped)
    half = clips // 2
    gqn, gpos_a = attend_back(shifts, qkv, prob, gctx, None, 0, half)
    if stepped:
        gsecond = meet_core(*gsecond)
        gqn, gsecond = lax.optimization_barrier((gqn, gsecond))
        gsecond = meet_far(gsecond, PLANE)
    gqn, gpos_b = attend_back(shifts, qkv, prob, gctx, gqn, half, clips - half)
    gfirst = project_back(gqn, tokens, w_qkv, small, gpos_a, gpos_b, stepped)
    if stepped:
        gfirst, gsecond = lax.optimization_barrier((gfirst, gsecond))
        gsecond = meet_far(add_blocks(gsecond), COLUMN)
        gfirst = meet_core(*gfirst)
        gfirst, gqn = lax.optimization_barrier((gfirst, gqn))
        gfirst = meet_far(gfirst, PLANE)
    gtok = token_back(gqn, tokens, gmid, w_qkv, vec)
    if stepped:
        gfirst, gtok, gelu = lax.optimization_barrier((gfirst, gtok, gelu))
        gfirst = meet_far(add_blocks(gfirst), COLUMN)
    out = output(gelu, ctx, tokens, wp, wd, vec)
    if stepped:
        gfirst, gsecond, out = lax.optimization_barrier((gfirst, gsecond, out))
        grads = finish(gfirst, gsecond)
    else:
        grads = whole_grads(gfirst[0], gsecond[0])
    mats, vecs, table = grads[:4], grads[4:13], grads[13]
    return (
        out, gtok, *mats, vecs[0], vecs[1], vecs[4], vecs[5], vecs[2], vecs[3], vecs[6], vecs[8], vecs[7], table,
    )


def solution(mesh):
    sharded = P(AXES, None)
    line = P(AXES)
    in_specs = (sharded, sharded, line, sharded) + (sharded,) * 4 + (line,) * 9 + (P(),)
    out_specs = (sharded,) * 6 + (line,) * 9 + (P(),)
    return jax.shard_map(on_device, mesh=mesh, in_specs=in_specs, out_specs=out_specs, check_vma=False)
```

```python
import functools

import jax
import jax.numpy as jnp
import numpy as np
from jax import lax
from jax.experimental import pallas as pl
from jax.experimental.pallas import tpu as pltpu
from jax.sharding import PartitionSpec as P

HEADS = 16
GRID_T = 64
GRID_F = 8
WIN = 4
PLACES = WIN * WIN
PATCHES = GRID_T * GRID_F
BLOCK = 64
BLOCKS = PATCHES // BLOCK
AXES = ("dp", "pair")
UNIT = 16
SHARDS = 32
RELS = (2 * WIN - 1) ** 2
CORE = (2,)
PLANE = (4, 1, 5)
COLUMN = (8, 16, 24)

EPS = 1e-06
HIGH = lax.Precision.HIGHEST
NEGATIVE = -1e30
F32 = jnp.float32
BF16 = jnp.bfloat16
LOG2_E = float(np.log2(np.e))
LOG_BELL = float(np.log2(2.0 / np.sqrt(2.0 * np.pi)))
VMEM_BYTES = 60 * 1024 * 1024
ROWS = 32


def dot_nn(a, b):
    return lax.dot_general(a, b, (((1,), (0,)), ((), ())), preferred_element_type=F32)


def dot_nt(a, b):
    return lax.dot_general(a, b, (((1,), (1,)), ((), ())), preferred_element_type=F32)


def dot_tn(a, b):
    return lax.dot_general(a, b, (((0,), (0,)), ((), ())), preferred_element_type=F32)


def norm_stats(values):
    row_mean = jnp.mean(values, -1, keepdims=True)
    centred = values - row_mean
    inv_std = lax.rsqrt(jnp.mean(centred * centred, -1, keepdims=True) + EPS)
    return centred * inv_std, inv_std


def norm_back(grad_out, normed, inv_std, gain):
    grad_normed = grad_out * gain
    return inv_std * (
        grad_normed
        - jnp.mean(grad_normed, -1, keepdims=True)
        - normed * jnp.mean(grad_normed * normed, -1, keepdims=True)
    )


def iota(shape, dim):
    return lax.broadcasted_iota(jnp.int32, shape, dim)


def fill_perm(perm_ref, s, u, to_windows):
    for r0 in range(0, PATCHES, BLOCK):
        row = iota((BLOCK, 128), 0) + r0
        if to_windows:
            a = (row >> 2) & 3
            b = row & 3
            t = (4 * (row >> 5) + a + s) & (GRID_T - 1)
            f = (4 * ((row >> 4) & 1) + b + u) & (GRID_F - 1)
            source = t * GRID_F + f
        else:
            r = ((row >> 3) - s) & (GRID_T - 1)
            q = ((row & 7) - u) & (GRID_F - 1)
            source = (r >> 2) * 32 + (q >> 2) * 16 + (r & 3) * 4 + (q & 3)
        lane = iota((BLOCK, 128), 1)
        for c0 in range(0, PATCHES, 128):
            perm_ref[r0 : r0 + BLOCK, c0 : c0 + 128] = jnp.where(
                source == lane + c0, 1.0, 0.0
            ).astype(BF16)


def compact_code(rows):
    row = iota((rows, 128), 0)
    lane = iota((rows, 128), 1)
    return ((lane >> 4) - (row >> 4) - (lane >> 6)) & 3


def head_lanes(dtype):
    lane = iota((16, 128), 1) >> 5
    return [jnp.where(lane == hh, 1.0, 0.0).astype(dtype) for hh in range(4)]


def expand_rows(tile, g, lanes):
    parts = []
    for hh in range(4):
        half, ab = hh & 1, hh >> 1
        for slot in range(4):
            w = (slot - half - g - 2 * ab) % 4
            parts.append(tile[16 * w : 16 * w + 16, :] * lanes[hh])
    return jnp.concatenate(parts, axis=0)


def compact(code, s0, s1):
    return jnp.where(
        code == 0,
        s0[:, :128],
        jnp.where(code == 1, s1[:, :128], jnp.where(code == 2, s0[:, 128:], s1[:, 128:])),
    )


def parts_of(x, count):
    parts = []
    for _ in range(count):
        parts.append(x.astype(BF16))
        x = x - parts[-1].astype(F32)
    return parts


def group_matrix(count, first_only):
    row = iota((128 * count, 128), 0) & 127
    same = (row >> 4) == (iota((128 * count, 128), 1) >> 4)
    if first_only:
        same = same & ((row & 15) == 0)
    return jnp.where(same, 1.0, 0.0).astype(BF16)


def put_parts(part_ref, rows, x, count):
    for i, part in enumerate(parts_of(x, count)):
        part_ref[rows, 128 * i : 128 * i + 128] = part


def allowed_tile(block, s, u, count):
    row = iota((BLOCK, 128), 0)
    key = iota((BLOCK, 128), 1) & 15
    band = 4 * (2 * block + (row >> 5))
    side = 4 * ((row >> 4) & 1)
    r_i = band + ((row >> 2) & 3) + s
    q_i = side + (row & 3) + u
    r_j = band + (key >> 2) + s
    q_j = side + (key & 3) + u
    wrap_i = (r_i >> 6) * 2 + (q_i >> 3)
    wrap_j = (r_j >> 6) * 2 + (q_j >> 3)
    visible = ((r_j & (GRID_T - 1)) < count) | ((row & 15) == key)
    return (wrap_i == wrap_j) & visible


def device_id():
    return lax.axis_index("dp") * lax.axis_size("pair") + lax.axis_index("pair")


def place_code():
    row = iota((PLACES, 256), 0)
    key = iota((PLACES, 256), 1) & 15
    return ((row >> 2) - (key >> 2) + WIN - 1) * (2 * WIN - 1) + ((row & 3) - (key & 3) + WIN - 1)


def head_select(w):
    row = iota((256, 256), 0)
    lane = iota((256, 256), 1)
    half = (lane >> 6) & 1
    e = ((lane >> 4) - w - half) & 3
    head = 8 * (lane >> 7) + 4 * (e & 1) + 2 * (e >> 1) + half
    return jnp.where((row & 15 == lane & 15) & (row >> 4 == head), 1.0, 0.0).astype(BF16)


def head_repeat():
    return jnp.where(iota((HEADS, 256), 0) == iota((HEADS, 256), 1) >> 4, 1.0, 0.0).astype(BF16)


def fill_positions(pos_ref, table_ref):
    spread = dot_tn(table_ref[...], head_repeat())
    code = place_code()
    rows = jnp.zeros((PLACES, 256), F32)
    for e in range(RELS):
        rows = jnp.where(code == e, spread[e : e + 1, :], rows)
    rows = rows.astype(BF16)
    for w in range(4):
        pos_ref[16 * w : 16 * w + 16, :] = dot_nn(rows, head_select(w))


def table_rows(gpos, scratch_ref):
    rows = jnp.zeros((PLACES, 256), F32)
    for w in range(4):
        select = head_select(w)
        for part in parts_of(gpos[16 * w : 16 * w + 16, :], 2):
            rows = rows + dot_nt(part, select)
    code = place_code()
    scratch_ref[...] = jnp.zeros_like(scratch_ref)
    for e in range(RELS):
        scratch_ref[e : e + 1, :] = jnp.sum(jnp.where(code == e, rows, 0.0), 0, keepdims=True)
    repeat = head_repeat()
    high, low = parts_of(scratch_ref[...], 2)
    return dot_nt(repeat, high) + dot_nt(repeat, low)


def mix_matrix():
    row = iota((512, 512), 0)
    lane = iota((512, 512), 1)
    return jnp.where(row == 128 * ((lane >> 4) & 3) + 16 * (lane >> 6) + (lane & 15), 1.0, 0.0).astype(BF16)


def fetch_blocks(piece_refs, masks, full_ref, sems):
    if masks is None:
        copies = [pltpu.make_async_copy(piece_refs[0], full_ref, sems.at[0])]
    else:
        me = device_id()
        copies = []
        for piece, (start, piece_masks) in zip(piece_refs, masks):
            cols = pl.ds(start, piece.shape[1])
            for j, mask in enumerate(piece_masks):
                at = pl.multiple_of((me ^ mask) * UNIT, UNIT)
                copies.append(
                    pltpu.make_async_copy(
                        piece.at[pl.ds(j * UNIT, UNIT), :], full_ref.at[pl.ds(at, UNIT), cols], sems.at[len(copies)]
                    )
                )
    for copy in copies:
        copy.start()
    return copies


def block_device(place, relative):
    if not relative:
        return place
    plane = (place >> 2) & 3
    return device_id() ^ (2 * (place >> 4) + 4 * (plane & 1) + (plane >> 1) + 8 * (place & 3))


def block_rows(place, relative):
    return pl.ds(pl.multiple_of(block_device(place, relative) * UNIT, UNIT), UNIT)


def put_block(send_refs, place, block):
    rows = send_refs[0].shape[0]
    at = place * UNIT
    send_refs[at // rows][at % rows : at % rows + UNIT, :] = block


def pack_kernel(*refs):
    vectors, (qkv_ref, proj_ref, up_ref, down_ref, first_ref, second_ref) = refs[:9], refs[9:]
    width = proj_ref.shape[1]
    first_ref[:, : 3 * width] = qkv_ref[...]
    rows = [v[...].astype(F32).reshape(1, UNIT) for v in vectors[:8]]
    bias = vectors[8][...].astype(F32).reshape(1, 4 * UNIT)
    rows += [bias[:, UNIT * q : UNIT * q + UNIT] for q in range(4)]
    rows = jnp.concatenate(rows + [jnp.zeros((116, UNIT), F32)], axis=0)
    first_ref[:, 3 * width :] = jnp.transpose(rows).astype(BF16)
    second_ref[:, :width] = proj_ref[...]
    second_ref[:, width : 5 * width] = up_ref[...]
    for q in range(4):
        second_ref[:, (5 + q) * width : (6 + q) * width] = down_ref[UNIT * q : UNIT * q + UNIT, :]


def pack(vectors, weights):
    width = weights[1].shape[1]
    return pl.pallas_call(
        pack_kernel,
        out_shape=[struct((UNIT, cols * width + more), BF16) for cols, more in ((3, 128), (9, 0))],
        compiler_params=pltpu.CompilerParams(vmem_limit_bytes=VMEM_BYTES),
        name="pack",
    )(*vectors, *weights)


def attend_kernel(
    masks, shift_ref, count_ref, tok_ref, table_ref, *refs
):
    pieces = refs[: 1 if masks is None else len(masks)]
    (
        qkv_ref, prob_ref, ctx_ref, w_ref, vec_ref,
        perm_ref, rows_ref, act_ref, score_ref, low_ref, ctxw_ref, pos_ref, group_ref, *part_refs, sems,
    ) = refs[len(pieces) :]
    width = tok_ref.shape[1]
    scale = (width // HEADS) ** (-0.5)
    clip = pl.program_id(0)
    s = shift_ref[0, clip]
    u = shift_ref[1, clip]
    count = count_ref[clip]

    @pl.when(clip == 0)
    def _():
        copies = fetch_blocks(pieces, masks, w_ref, sems)
        fill_positions(pos_ref, table_ref)
        for copy in copies:
            copy.wait()
        vec_ref[...] = jnp.transpose(w_ref[:, 3 * width :].astype(F32))[:16, :]
        flat = vec_ref[8:16, :].astype(BF16)
        flat = jnp.concatenate(
            [
                jnp.concatenate([flat[q : q + 1, 128 * c : 128 * c + 128] for q in range(4)], axis=1)
                for c in range(4)
            ]
            + [jnp.zeros((12, width), BF16)],
            axis=0,
        )
        vec_ref[8:16, :] = dot_nn(flat, mix_matrix())[:8, :]

    fill_perm(perm_ref, s, u, True)
    rows_ref[...] = dot_nn(perm_ref[...], tok_ref[...])
    for r in range(0, PATCHES, ROWS):
        normed, _ = norm_stats(rows_ref[r : r + ROWS, :])
        act_ref[r : r + ROWS, :] = (normed * vec_ref[0:1, :] + vec_ref[1:2, :]).astype(BF16)
    for c in range(3):
        cols = slice(c * width, (c + 1) * width)
        out = dot_nn(act_ref[...], w_ref[:, cols])
        if c == 0:
            out = out + vec_ref[2:3, :]
        if c == 2:
            out = out + vec_ref[3:4, :]
        qkv_ref[:, cols] = out.astype(BF16)
    lanes = head_lanes(BF16)
    code = compact_code(BLOCK)
    for b in range(BLOCKS):
        rows = slice(b * BLOCK, (b + 1) * BLOCK)
        for p in range(2):
            parts = []
            for g in range(2):
                c0 = 128 * (2 * p + g)
                keys = expand_rows(qkv_ref[rows, width + c0 : width + c0 + 128], g, lanes)
                parts.append(dot_nt(qkv_ref[rows, c0 : c0 + 128], keys))
            score_ref[rows, 128 * p : 128 * p + 128] = compact(code, *parts)
    first_lane = group_matrix(3, True)
    all_lanes = group_matrix(2, False)
    blocks = [slice(b * BLOCK, (b + 1) * BLOCK) for b in range(BLOCKS)]
    pairs = [slice(128 * p, 128 * p + 128) for p in range(2)]
    for b, rows in enumerate(blocks):
        allowed = allowed_tile(b, s, u, count)
        for p, cols in enumerate(pairs):
            logits = score_ref[rows, cols] * scale + pos_ref[:, cols]
            logits = jnp.where(allowed, logits, NEGATIVE)
            score_ref[rows, cols] = logits
            for k in (1, 2, 4, 8):
                logits = jnp.maximum(logits, pltpu.roll(logits, 128 - k, 1))
            put_parts(part_refs[p], rows, logits, 3)
    for p, cols in enumerate(pairs):
        group_ref[:, cols] = dot_nn(part_refs[p][...], first_lane)
    for p, cols in enumerate(pairs):
        for rows in blocks:
            e = jnp.exp(score_ref[rows, cols] - group_ref[rows, cols])
            score_ref[rows, cols] = e
            put_parts(part_refs[p], rows, e, 2)
    for p, cols in enumerate(pairs):
        group_ref[:, cols] = dot_nn(part_refs[p][:, :256], all_lanes)
    for p, cols in enumerate(pairs):
        for rows in blocks:
            prob = score_ref[rows, cols] * pl.reciprocal(group_ref[rows, cols])
            prob_ref[rows, cols] = prob
            low_ref[rows, cols] = prob.astype(BF16)
    spread = [jnp.where(code == e, 1.0, 0.0).astype(BF16) for e in range(4)]
    for b in range(BLOCKS):
        rows = slice(b * BLOCK, (b + 1) * BLOCK)
        for p in range(2):
            low = low_ref[rows, 128 * p : 128 * p + 128]
            for g in range(2):
                c0 = 128 * (2 * p + g)
                values = expand_rows(qkv_ref[rows, 2 * width + c0 : 2 * width + c0 + 128], g, lanes)
                wide = jnp.concatenate([low * spread[g], low * spread[2 + g]], axis=1)
                ctxw_ref[rows, c0 : c0 + 128] = dot_nn(wide, values).astype(BF16)
    fill_perm(perm_ref, s, u, False)
    ctx_ref[...] = dot_nn(perm_ref[...], ctxw_ref[...]).astype(BF16)


def weave(first, second):
    done = 0
    for i, step in enumerate(first):
        step()
        upto = (i + 1) * len(second) // len(first)
        for other in second[done:upto]:
            other()
        done = upto
    for other in second[done:]:
        other()


def mlp_kernel(
    masks, relative, tok_ref, ctx_ref, cot_ref, vec_ref, *refs
):
    pieces = refs[: 1 if masks is None else len(masks)]
    (
        *gelu_refs, gmid_ref, gctx_ref, small_ref, wp_out_ref, wd_out_ref,
    ) = refs[len(pieces) : len(pieces) + 9]
    *send_refs, w_ref, wd_ref, accp_ref, accu_ref, accd_ref, mid_ref, act_ref, branch_ref, gact_ref = refs[
        len(pieces) + 9 : -13
    ]
    hid_refs, gg_refs, gh_refs, sems = refs[-13:-9], refs[-9:-5], refs[-5:-1], refs[-1]
    keeps = [
        pltpu.make_async_copy(w_ref.at[:, : tok_ref.shape[1]], wp_out_ref, sems.at[0]),
        pltpu.make_async_copy(wd_ref, wd_out_ref, sems.at[1]),
    ]
    step = pl.program_id(0)
    tile, width = tok_ref.shape
    ff = 4 * width
    chunk = 512

    @pl.when(step == 0)
    def _():
        copies = fetch_blocks(pieces, masks, w_ref, sems)
        accp_ref[...] = jnp.zeros_like(accp_ref)
        accu_ref[...] = jnp.zeros_like(accu_ref)
        accd_ref[...] = jnp.zeros_like(accd_ref)
        small_ref[...] = jnp.zeros_like(small_ref)
        for copy in copies:
            copy.wait()
        for i in range(SHARDS):
            for q in range(4):
                at = UNIT * (4 * i + q)
                weight = w_ref[UNIT * i : UNIT * i + UNIT, (5 + q) * width : (6 + q) * width]
                wd_ref[at : at + UNIT, :] = weight * jnp.asarray(0.5, BF16)
        for keep in keeps:
            keep.start()

    gain = vec_ref[4:5, :]
    bias = vec_ref[5:6, :]
    half = chunk // 2
    count = ff // chunk
    sums = [jnp.zeros((1, width), F32) for _ in range(4)]

    def norm_rows(r):
        rows = slice(r, r + ROWS)
        mid = mid_ref[rows, :] + tok_ref[rows, :].astype(F32) + vec_ref[6:7, :]
        mid_ref[rows, :] = mid
        normed, _ = norm_stats(mid)
        act_ref[rows, :] = (normed * gain + bias).astype(BF16)

    def back_rows(r):
        rows = slice(r, r + ROWS)
        normed, inv = norm_stats(mid_ref[rows, :])
        g_act = gact_ref[rows, :]
        cot = cot_ref[rows, :].astype(F32)
        g_mid = cot + norm_back(g_act, normed, inv, gain)
        gmid_ref[rows, :] = g_mid
        g_branch = g_mid.astype(BF16)
        branch_ref[rows, :] = g_branch
        for i, part in enumerate((g_act * normed, g_act, g_branch.astype(F32), cot)):
            sums[i] = sums[i] + jnp.sum(part, 0, keepdims=True)

    totals = {}

    def bend(c, k, r):
        lanes = slice(k, k + 128)
        rows = slice(r, r + 64)
        h = hid_refs[c][rows, lanes] + vec_ref[8 + c : 9 + c, lanes]
        z = h * (0.5**0.5)
        double_phi = 1.0 + lax.erf(z)
        double_bell = jnp.exp2(LOG_BELL - (z * z) * LOG2_E)
        gelu_refs[c][rows, lanes] = (h * double_phi).astype(BF16)
        g_hidden = gg_refs[c][rows, lanes] * (double_phi + h * double_bell)
        gh_refs[c][rows, lanes] = g_hidden.astype(BF16)
        part = jnp.sum(g_hidden.reshape(8, 8, 128), 0)
        totals[c, k] = part if r == 0 else totals[c, k] + part
        if r + 64 == tile:
            small_ref[8 + c : 9 + c, lanes] += jnp.sum(totals[c, k], 0, keepdims=True)

    def up(c, m, k):
        at = width + c * chunk + k
        hid_refs[c][m : m + half, k : k + half] = dot_nn(act_ref[m : m + half, :], w_ref[:, at : at + half])

    def down_back(c, m, k):
        at = c * chunk + k
        gg_refs[c][m : m + half, k : k + half] = dot_nt(cot_ref[m : m + half, :], wd_ref[at : at + half, :])

    def up_back(c, m, k):
        weight = w_ref[k : k + half, width + c * chunk : width + (c + 1) * chunk]
        part = dot_nt(gh_refs[c][m : m + half, :], weight)
        if c == 0:
            gact_ref[m : m + half, k : k + half] = part
        else:
            gact_ref[m : m + half, k : k + half] += part

    def down_grad(c, m, k):
        at = c * chunk + m
        accd_ref[at : at + half, k : k + half] += dot_tn(gelu_refs[c][:, m : m + half], cot_ref[:, k : k + half])

    def up_grad(c, m, k):
        at = c * chunk + k
        accu_ref[m : m + half, at : at + half] += dot_tn(act_ref[:, m : m + half], gh_refs[c][:, k : k + half])

    def all_of(fn, c):
        return [functools.partial(fn, c, m, k) for k in (0, half) for m in (0, half)]

    always = step >= 0

    @pl.when(always)
    def _():
        mid_ref[...] = dot_nn(ctx_ref[...], w_ref[:, :width])
        weave(
            all_of(down_back, 0) + all_of(down_back, 1),
            [functools.partial(norm_rows, r) for r in range(0, tile, ROWS)],
        )
        weave(all_of(up, 0), [])

    for c in range(count):

        @pl.when(always)
        def _(c=c):
            products = []
            if c + 1 < count:
                products += all_of(up, c + 1)
            if c > 0:
                products += all_of(up_back, c - 1)
            if c + 2 < count:
                products += all_of(down_back, c + 2)
            if c > 1:
                products += all_of(down_grad, c - 2) + all_of(up_grad, c - 2)
            weave(products, [functools.partial(bend, c, k, r) for k in range(0, chunk, 128) for r in range(0, tile, 64)])

    @pl.when(always)
    def _():
        weave(all_of(up_back, count - 1), [])
        weave(
            all_of(down_grad, count - 2)
            + all_of(up_grad, count - 2)
            + all_of(down_grad, count - 1)
            + all_of(up_grad, count - 1),
            [functools.partial(back_rows, r) for r in range(0, tile, ROWS)],
        )
        for i in range(4):
            small_ref[4 + i : 5 + i, :] += sums[i]
        gctx_ref[...] = dot_nt(branch_ref[...], w_ref[:, :width]).astype(BF16)
        accp_ref[...] += dot_tn(ctx_ref[...], branch_ref[...])

    @pl.when(step == pl.num_programs(0) - 1)
    def _():
        for place in range(SHARDS):
            rows = block_rows(place, relative)
            block = [accp_ref[rows, :], accu_ref[rows, :]]
            down = pl.multiple_of(block_device(place, relative) * (4 * UNIT), 4 * UNIT)
            block += [accd_ref[pl.ds(down + UNIT * q, UNIT), :] * 0.5 for q in range(4)]
            put_block(send_refs, place, jnp.concatenate(block, axis=1).astype(BF16))
        for keep in keeps:
            keep.wait()


def attend_back_kernel(
    start, shift_ref, qkv_ref, prob_ref, gctx_ref, _, gqn_ref, gpos_ref,
    perm_ref, do_ref, dp_ref, low_ref, gs_ref, lowt_ref, gst_ref, gqw_ref, group_ref, *part_refs,
):
    width = gctx_ref.shape[1]
    scale = (width // HEADS) ** (-0.5)
    step = pl.program_id(0)
    s = shift_ref[0, step + start]
    u = shift_ref[1, step + start]

    @pl.when(step == 0)
    def _():
        gpos_ref[...] = jnp.zeros_like(gpos_ref)

    fill_perm(perm_ref, s, u, True)
    do_ref[...] = dot_nn(perm_ref[...], gctx_ref[...]).astype(BF16)
    lanes = head_lanes(BF16)
    code = compact_code(BLOCK)
    for b in range(BLOCKS):
        rows = slice(b * BLOCK, (b + 1) * BLOCK)
        for p in range(2):
            parts = []
            for g in range(2):
                c0 = 128 * (2 * p + g)
                values = expand_rows(qkv_ref[rows, 2 * width + c0 : 2 * width + c0 + 128], g, lanes)
                parts.append(dot_nt(do_ref[rows, c0 : c0 + 128], values))
            dp_ref[rows, 128 * p : 128 * p + 128] = compact(code, *parts)
    all_lanes = group_matrix(2, False)
    blocks = [slice(b * BLOCK, (b + 1) * BLOCK) for b in range(BLOCKS)]
    pairs = [slice(128 * p, 128 * p + 128) for p in range(2)]
    for p, cols in enumerate(pairs):
        for rows in blocks:
            put_parts(part_refs[p], rows, prob_ref[rows, cols] * dp_ref[rows, cols], 2)
    for p, cols in enumerate(pairs):
        group_ref[:, cols] = dot_nn(part_refs[p][...], all_lanes)
    for p, cols in enumerate(pairs):
        total = jnp.zeros((BLOCK, 128), F32)
        for rows in blocks:
            prob = prob_ref[rows, cols]
            g_scores = (prob * (dp_ref[rows, cols] - group_ref[rows, cols])).astype(BF16)
            gs_ref[rows, cols] = g_scores
            low_ref[rows, cols] = prob.astype(BF16)
            total = total + g_scores.astype(F32)
        gpos_ref[:, cols] += total
    spread = [jnp.where(code == e, 1.0, 0.0).astype(BF16) for e in range(4)]
    for b in range(BLOCKS):
        rows = slice(b * BLOCK, (b + 1) * BLOCK)
        for p in range(2):
            low = gs_ref[rows, 128 * p : 128 * p + 128]
            for g in range(2):
                c0 = 128 * (2 * p + g)
                keys = expand_rows(qkv_ref[rows, width + c0 : width + c0 + 128], g, lanes)
                wide = jnp.concatenate([low * spread[g], low * spread[2 + g]], axis=1)
                gqw_ref[rows, c0 : c0 + 128] = (dot_nn(wide, keys) * scale).astype(BF16)
    lowt_ref[...] = jnp.transpose(low_ref[...])
    gst_ref[...] = jnp.transpose(gs_ref[...])
    row_t = iota((BLOCK, 128), 0)
    lane_t = iota((BLOCK, 128), 1)
    code_t = ((row_t >> 4) - (lane_t >> 4)) & 3
    spread_t = [
        [jnp.where((code_t == d) & ((lane_t >> 6) == blk), 1.0, 0.0).astype(BF16) for d in range(4)]
        for blk in range(2)
    ]
    lane16 = iota((16, 128), 1) >> 5
    for source_ref, other_ref, other_at, out_at, factor in (
        (gst_ref, qkv_ref, 0, width, scale),
        (lowt_ref, do_ref, 0, 2 * width, 1.0),
    ):
        for two in range(BLOCKS // 2):
            places = slice(128 * two, 128 * two + 128)
            for p in range(2):
                halves = [source_ref[128 * p + 64 * h : 128 * p + 64 * h + 64, places] for h in range(2)]
                for g in range(2):
                    c0 = 128 * (2 * p + g)
                    parts = []
                    for blk in range(2):
                        for hh in range(4):
                            half, ab = hh & 1, hh >> 1
                            d = (g + 2 * ab + half) & 3
                            parts.append(halves[half] * spread_t[blk][d])
                    wide = dot_nn(
                        jnp.concatenate(parts, axis=0), other_ref[places, other_at + c0 : other_at + c0 + 128]
                    )
                    for blk in range(2):
                        for w in range(4):
                            pieces = []
                            for hh in range(4):
                                half, ab = hh & 1, hh >> 1
                                slot = (w + half + g + 2 * ab) & 3
                                at = 256 * blk + 64 * hh + 16 * slot
                                pieces.append(wide[at : at + 16, :])
                            total = jnp.where(
                                lane16 == 0,
                                pieces[0],
                                jnp.where(lane16 == 1, pieces[1], jnp.where(lane16 == 2, pieces[2], pieces[3])),
                            )
                            at = 128 * two + 64 * blk + 16 * w
                            gqw_ref[at : at + 16, out_at + c0 : out_at + c0 + 128] = (total * factor).astype(BF16)
    fill_perm(perm_ref, s, u, False)
    for c in range(3):
        cols = slice(c * width, (c + 1) * width)
        gqn_ref[:, cols] = dot_nn(perm_ref[...], gqw_ref[:, cols]).astype(BF16)


def project_back_kernel(
    relative, gqn_ref, tok_ref, w_ref, small_in_ref, gpos_a_ref, gpos_b_ref, *refs
):
    *send_refs, acc_ref, norm_ref, small_ref, sum_ref, scratch_ref, column_ref = refs
    width = tok_ref.shape[1]
    step = pl.program_id(0)

    @pl.when(step == 0)
    def _():
        acc_ref[...] = jnp.zeros_like(acc_ref)
        sum_ref[...] = jnp.zeros_like(sum_ref)
        small_ref[...] = jnp.zeros_like(small_ref)
        small_ref[:16, :] = small_in_ref[...]

    tile = tok_ref.shape[0]
    half = width // 2

    def norm_rows(r):
        rows = slice(r, r + ROWS)
        normed, _ = norm_stats(tok_ref[rows, :].astype(F32))
        norm_ref[rows, :] = normed.astype(BF16)

    def column_sums(c):
        total = jnp.zeros((8, 128), F32)
        for r in range(0, tile, 64):
            part = gqn_ref[r : r + 64, c : c + 128].astype(F32)
            total = total + jnp.sum(part.reshape(8, 8, 128), 0)
        sum_ref[0:1, c : c + 128] += jnp.sum(total, 0, keepdims=True)

    def product(m, n):
        acc_ref[m : m + half, n : n + half] += dot_tn(norm_ref[:, m : m + half], gqn_ref[:, n : n + half])

    weave([], [functools.partial(norm_rows, r) for r in range(0, tile, ROWS)])
    weave(
        [functools.partial(product, m, n) for n in range(0, 3 * width, half) for m in (0, half)],
        [functools.partial(column_sums, c) for c in range(0, 3 * width, 128)],
    )

    @pl.when(step == pl.num_programs(0) - 1)
    def _():
        small_ref[2:3, :] = sum_ref[0:1, :width]
        small_ref[3:4, :] = sum_ref[0:1, 2 * width :]
        bias = small_ref[8:16, :].astype(BF16)
        flat = dot_nt(bias, mix_matrix())
        for q in range(4):
            small_ref[8 + q : 9 + q, :] = jnp.concatenate(
                [flat[c : c + 1, 128 * q : 128 * q + 128] for c in range(4)], axis=1
            )
        table = table_rows(gpos_a_ref[...] + gpos_b_ref[...], scratch_ref)
        extra = jnp.concatenate([jnp.zeros((UNIT, 16), F32), table, jnp.zeros((UNIT, 48), F32)], axis=1)
        column_ref[...] = jnp.transpose(small_ref[...])
        lane = iota((UNIT, 128), 1)
        for place in range(SHARDS):
            rows = block_rows(place, relative)
            weight = w_ref[rows, : 3 * width].astype(F32)
            gain = w_ref[rows, 3 * width : 3 * width + 1].astype(F32)
            bias = w_ref[rows, 3 * width + 1 : 3 * width + 2].astype(F32)
            product = acc_ref[rows, :]
            total = sum_ref[0:1, :]
            g_gain = jnp.sum(product * weight, 1, keepdims=True)
            g_bias = jnp.sum(total * weight, 1, keepdims=True)
            tail = jnp.where(lane == 0, g_gain, jnp.where(lane == 1, g_bias, column_ref[rows, :] + extra))
            block = jnp.concatenate([gain * product + bias * total, tail], axis=1)
            put_block(send_refs, place, block.astype(BF16))


def token_back_kernel(gqn_ref, tok_ref, gmid_ref, w_ref, vec_ref, gtok_ref, *gact_refs):
    tile, width = tok_ref.shape
    half = tile // 2

    def product(h, n):
        rows = slice(h * half, (h + 1) * half)
        gact_refs[h][:, n : n + half] = dot_nt(gqn_ref[rows, :], w_ref[n : n + half, : 3 * width])

    def back_rows(h, r):
        rows = slice(h * half + r, h * half + r + ROWS)
        normed, inv = norm_stats(tok_ref[rows, :].astype(F32))
        g_act = gact_refs[h][r : r + ROWS, :]
        gtok_ref[rows, :] = gmid_ref[rows, :] + norm_back(g_act, normed, inv, vec_ref[0:1, :])

    steps = [[functools.partial(back_rows, h, r) for r in range(0, half, ROWS)] for h in range(2)]
    products = [[functools.partial(product, h, n) for n in range(0, width, half)] for h in range(2)]
    weave(products[0], [])
    weave(products[1], steps[0])
    weave([], steps[1])


def output_kernel(*refs):
    gelu_refs, (ctx_ref, tok_ref, wp_ref, wd_ref, vec_ref, out_ref) = refs[:4], refs[4:]
    tile, width = tok_ref.shape
    half = width // 2
    bias = vec_ref[6:7, :] + vec_ref[7:8, :]
    for n in (0, half):
        cols = slice(n, n + half)
        for m in range(0, tile, half):
            rows = slice(m, m + half)
            gelu = jnp.concatenate([ref[rows, :] for ref in gelu_refs], axis=1)
            total = dot_nn(gelu, wd_ref[:, cols]) + dot_nn(ctx_ref[rows, :], wp_ref[:, cols])
            out_ref[rows, cols] = (total + tok_ref[rows, cols].astype(F32) + bias[:, cols]).astype(BF16)


SMEM_SPEC = pl.BlockSpec(memory_space=pltpu.SMEM)
ANY_SPEC = pl.BlockSpec(memory_space=pl.ANY)


def rows_spec(rows, cols):
    return pl.BlockSpec((rows, cols), lambda i: (i, 0))


def whole_spec(shape):
    return pl.BlockSpec(shape, lambda i: (0,) * len(shape))


def struct(shape, dtype):
    return jax.ShapeDtypeStruct(shape, dtype)


def cost(flops, nbytes):
    return pl.CostEstimate(flops=flops, bytes_accessed=nbytes, transcendentals=0)


def params():
    return pltpu.CompilerParams(vmem_limit_bytes=VMEM_BYTES, dimension_semantics=("arbitrary",))


def clip_spec(cols, start):
    return pl.BlockSpec((PATCHES, cols), lambda i: (i + start, 0))


def attend(shifts, counts, tokens, table, pieces, masks):
    n, width = tokens.shape
    cols = 3 * width + 128
    return pl.pallas_call(
        functools.partial(attend_kernel, masks),
        grid=(n // PATCHES,),
        in_specs=[SMEM_SPEC, SMEM_SPEC, rows_spec(PATCHES, width), whole_spec(table.shape)] + [ANY_SPEC] * len(pieces),
        out_specs=[
            rows_spec(PATCHES, 3 * width), rows_spec(PATCHES, 256), rows_spec(PATCHES, width),
            whole_spec((width, cols)), whole_spec((16, width)),
        ],
        out_shape=[
            struct((n, 3 * width), BF16), struct((n, 256), F32), struct((n, width), BF16),
            struct((width, cols), BF16), struct((16, width), F32),
        ],
        scratch_shapes=[
            pltpu.VMEM((PATCHES, PATCHES), BF16),
            pltpu.VMEM((PATCHES, width), F32),
            pltpu.VMEM((PATCHES, width), BF16),
            pltpu.VMEM((PATCHES, 256), F32),
            pltpu.VMEM((PATCHES, 256), BF16),
            pltpu.VMEM((PATCHES, width), BF16),
            pltpu.VMEM((BLOCK, 256), F32),
            pltpu.VMEM((PATCHES, 256), F32),
            *[pltpu.VMEM((PATCHES, 384), BF16)] * 2,
            pltpu.SemaphoreType.DMA((SHARDS,)),
        ],
        compiler_params=params(),
        cost_estimate=cost(2800000000, n * width),
        name="attend",
    )(shifts, counts, tokens, table, *pieces)


def send_shapes(cols, relative):
    rows = SHARDS * UNIT
    return [struct((rows // 2, cols), BF16)] * 2 if relative else [struct((rows, cols), BF16)]


def mlp(tokens, ctx, cot, vec, pieces, masks, relative, tile=512):
    n, width = tokens.shape
    cols = 9 * width
    ff = 4 * width
    sends = send_shapes(cols, relative)
    return pl.pallas_call(
        functools.partial(mlp_kernel, masks, relative),
        grid=(n // tile,),
        in_specs=[rows_spec(tile, width)] * 3 + [whole_spec(vec.shape)] + [ANY_SPEC] * len(pieces),
        out_specs=[rows_spec(tile, width)] * 6
        + [whole_spec((16, width)), ANY_SPEC, ANY_SPEC]
        + [whole_spec(x.shape) for x in sends],
        out_shape=[struct((n, width), BF16)] * 4
        + [
            struct((n, width), F32), struct((n, width), BF16),
            struct((16, width), F32), struct((width, width), BF16), struct((ff, width), BF16),
        ]
        + sends,
        scratch_shapes=[
            pltpu.VMEM((width, cols), BF16),
            pltpu.VMEM((ff, width), BF16),
            pltpu.VMEM((width, width), F32),
            pltpu.VMEM((width, ff), F32),
            pltpu.VMEM((ff, width), F32),
            pltpu.VMEM((tile, width), F32),
            pltpu.VMEM((tile, width), BF16),
            pltpu.VMEM((tile, width), BF16),
            pltpu.VMEM((tile, width), F32),
            *[pltpu.VMEM((tile, width), F32)] * 8,
            *[pltpu.VMEM((tile, width), BF16)] * 4,
            pltpu.SemaphoreType.DMA((SHARDS,)),
        ],
        compiler_params=params(),
        cost_estimate=cost(5000000000, n * width),
        name="mlp",
    )(tokens, ctx, cot, vec, *pieces)


def attend_back(shifts, qkv, prob, gctx, into, start, clips):
    n, width = gctx.shape

    def spec(cols):
        return pl.BlockSpec((PATCHES, cols), lambda i: (i + start, 0))

    return pl.pallas_call(
        functools.partial(attend_back_kernel, start),
        grid=(clips,),
        in_specs=[SMEM_SPEC, spec(3 * width), spec(256), spec(width), ANY_SPEC],
        out_specs=[spec(3 * width), whole_spec((BLOCK, 256))],
        out_shape=[struct((n, 3 * width), BF16), struct((BLOCK, 256), F32)],
        scratch_shapes=[
            pltpu.VMEM((PATCHES, PATCHES), BF16),
            pltpu.VMEM((PATCHES, width), BF16),
            pltpu.VMEM((PATCHES, 256), F32),
            pltpu.VMEM((PATCHES, 256), BF16),
            pltpu.VMEM((PATCHES, 256), BF16),
            pltpu.VMEM((256, PATCHES), BF16),
            pltpu.VMEM((256, PATCHES), BF16),
            pltpu.VMEM((PATCHES, 3 * width), BF16),
            pltpu.VMEM((PATCHES, 256), F32),
            *[pltpu.VMEM((PATCHES, 256), BF16)] * 2,
        ],
        input_output_aliases={} if into is None else {4: 0},
        compiler_params=params(),
        cost_estimate=cost(700000000 * clips, n * width),
        name="attend_back",
    )(shifts, qkv, prob, gctx, prob if into is None else into)


def project_back(gqn, tokens, w_qkv, small, gpos_a, gpos_b, relative, tile=512):
    n, width = tokens.shape
    sends = send_shapes(w_qkv.shape[1], relative)
    return pl.pallas_call(
        functools.partial(project_back_kernel, relative),
        grid=(n // tile,),
        in_specs=[rows_spec(tile, 3 * width), rows_spec(tile, width)]
        + [whole_spec(x.shape) for x in (w_qkv, small, gpos_a, gpos_b)],
        out_specs=[whole_spec(x.shape) for x in sends],
        out_shape=sends,
        scratch_shapes=[
            pltpu.VMEM((width, 3 * width), F32),
            pltpu.VMEM((tile, width), BF16),
            pltpu.VMEM((128, width), F32),
            pltpu.VMEM((8, 3 * width), F32),
            pltpu.VMEM((64, 256), F32),
            pltpu.VMEM((width, 128), F32),
        ],
        compiler_params=params(),
        cost_estimate=cost(1000000000, n * width),
        name="project_back",
    )(gqn, tokens, w_qkv, small, gpos_a, gpos_b)


def token_back(gqn, tokens, gmid, w_qkv, vec, tile=512):
    n, width = tokens.shape
    return pl.pallas_call(
        token_back_kernel,
        grid=(n // tile,),
        in_specs=[rows_spec(tile, 3 * width), rows_spec(tile, width), rows_spec(tile, width)]
        + [whole_spec(w_qkv.shape), whole_spec(vec.shape)],
        out_specs=rows_spec(tile, width),
        out_shape=struct((n, width), F32),
        scratch_shapes=[pltpu.VMEM((tile // 2, width), F32)] * 2,
        compiler_params=params(),
        cost_estimate=cost(1000000000, n * width),
        name="token_back",
    )(gqn, tokens, gmid, w_qkv, vec)


def output(gelu, ctx, tokens, wp, wd, vec, tile=512):
    n, width = tokens.shape
    return pl.pallas_call(
        output_kernel,
        grid=(n // tile,),
        in_specs=[rows_spec(tile, width)] * 6
        + [whole_spec(x.shape) for x in (wp, wd, vec)],
        out_specs=rows_spec(tile, width),
        out_shape=struct((n, width), BF16),
        compiler_params=params(),
        cost_estimate=cost(1000000000, n * width),
        name="output",
    )(*gelu, ctx, tokens, wp, wd, vec)


def finish_kernel(*refs):
    first, second = refs[:4], refs[4:8]
    gqkv_ref, gproj_ref, gup_ref, gdown_ref, *vector_refs, table_ref = refs[8:]
    width = gproj_ref.shape[1]

    def total(parts, cols):
        a, b, c, d = (part[:, cols].astype(F32) for part in parts)
        return (a + b) + (c + d)

    gqkv_ref[...] = total(first, slice(0, 3 * width))
    gproj_ref[...] = total(second, slice(0, width))
    gup_ref[...] = total(second, slice(width, 5 * width))
    for q in range(4):
        gdown_ref[UNIT * q : UNIT * q + UNIT, :] = total(second, slice((5 + q) * width, (6 + q) * width))
    extra = total(first, slice(3 * width, 3 * width + 128))
    rows = jnp.transpose(extra)
    for i in range(8):
        vector_refs[i][...] = rows[i, :]
    vector_refs[8][...] = jnp.concatenate([rows[8 + q : 9 + q, :] for q in range(4)], axis=1)[0]
    table_ref[...] = extra[:, 16 : 16 + RELS]


def finish(first, second):
    width = second[0].shape[1] // 9
    return pl.pallas_call(
        finish_kernel,
        out_shape=[
            struct((UNIT, 3 * width), F32), struct((UNIT, width), F32), struct((UNIT, 4 * width), F32),
            struct((4 * UNIT, width), F32),
            *[struct((UNIT,), F32)] * 8, struct((4 * UNIT,), F32), struct((HEADS, RELS), F32),
        ],
        compiler_params=pltpu.CompilerParams(vmem_limit_bytes=VMEM_BYTES),
        name="finish",
    )(*first, *second)


def exchange(x, mask):
    size = lax.axis_size(AXES)
    return lax.ppermute(x, AXES, [(i, i ^ mask) for i in range(size)])


def spread_far(block, masks):
    return [block] + [exchange(block, m) for m in masks]


def spread_core(pieces):
    return pieces + [exchange(x, CORE[0]) for x in pieces]


def piece_masks(near, far, start):
    return tuple((start, tuple(n ^ f ^ core for n in (0,) + near)) for core in (0,) + CORE for f in (0,) + far)


def add(*parts):
    parts = [p.astype(F32) for p in parts]
    while len(parts) > 1:
        parts = [parts[i] + parts[i + 1] for i in range(0, len(parts), 2)]
    return parts[0].astype(BF16)


def meet_core(keep, send):
    got = exchange(send, CORE[0])
    quarter = keep.shape[0] // 4
    return [add(keep[quarter * k : quarter * (k + 1)], got[quarter * k : quarter * (k + 1)]) for k in range(4)]


def meet_far(groups, masks):
    return [groups[0]] + [exchange(group, mask) for group, mask in zip(groups[1:], masks)]


def add_blocks(parts):
    return [add(*[p[UNIT * k : UNIT * (k + 1)] for p in parts]) for k in range(4)]


def gather(x):
    return lax.all_gather(x, AXES, axis=0, tiled=True)


def scatter(x):
    return lax.psum_scatter(x, AXES, scatter_dimension=0, tiled=True)


def by_unit(x):
    return jnp.moveaxis(x.reshape((SHARDS, 4, UNIT) + x.shape[1:]), 1, 2).reshape((SHARDS * UNIT, 4) + x.shape[1:])


def by_row(x):
    return jnp.moveaxis(x.reshape((SHARDS, UNIT, 4) + x.shape[2:]), 2, 1).reshape((4 * SHARDS * UNIT,) + x.shape[2:])


def whole_weights(vectors, weights):
    columns = [gather(v)[:, None] for v in vectors[:8]] + [by_unit(gather(vectors[8]))]
    extra = jnp.concatenate(columns, axis=1)
    qkv, proj, up, down = (gather(w) for w in weights)
    first = jnp.concatenate([qkv, extra, jnp.zeros((qkv.shape[0], 128 - extra.shape[1]), BF16)], axis=1)
    second = jnp.concatenate([proj, up, by_unit(down).reshape(proj.shape[0], -1)], axis=1)
    return first, second


def whole_grads(first, second):
    width = second.shape[1] // 9
    mats = [first[:, : 3 * width], second[:, :width], second[:, width : 5 * width]]
    mats.append(by_row(second[:, 5 * width :].reshape(-1, 4, width)))
    extra = first[:, 3 * width :]
    vectors = [extra[:, k] for k in range(8)] + [by_row(extra[:, 8:12])]
    table = lax.psum(extra[:UNIT, 16 : 16 + RELS].astype(F32), AXES).T
    return [scatter(x).astype(F32) for x in mats] + [scatter(x.astype(F32)) for x in vectors] + [table]


def local_test(
    tokens, cotangent, counts, shifts, qkv, proj, up, down, vec1, vec2, ub, table,
):
    shifts, table = shifts.T, table.T
    extra = jnp.concatenate([vec1, vec2], axis=0).T
    extra = jnp.concatenate([extra, by_unit(ub[0]), jnp.zeros((512, 116))], axis=1).astype(BF16)
    first = jnp.concatenate([qkv, extra], axis=1)
    second = jnp.concatenate([proj, up, by_unit(down).reshape(512, -1)], axis=1)
    q, prob, ctx, w_qkv, vec = attend(shifts, counts, tokens, table, [first], None)
    *gelu, gmid, gctx, small, wp, wd, gsecond = mlp(tokens, ctx, cotangent, vec, [second], None, False)
    gqn, gpos_a = attend_back(shifts, q, prob, gctx, None, 0, 2)
    gqn, gpos_b = attend_back(shifts, q, prob, gctx, gqn, 2, 2)
    (gfirst,) = project_back(gqn, tokens, w_qkv, small, gpos_a, gpos_b, False)
    gtok = token_back(gqn, tokens, gmid, w_qkv, vec)
    out = output(gelu, ctx, tokens, wp, wd, vec)
    width = 512
    e = gfirst[:, 1536:]
    mats = [gfirst[:, :1536], gsecond[:, :width], gsecond[:, width : 5 * width], by_row(gsecond[:, 5 * width :].reshape(-1, 4, width))]
    v = [e[:, k] for k in range(8)]
    return [out, gtok] + mats + [v[0], v[1], v[4], v[5], v[2], v[3], v[6], by_row(e[:, 8:12]), v[7], e[:16, 16:65].T]


def on_device(
    tokens, cotangent, counts, shifts, qkv_weight, proj_weight, up_weight, down_weight,
    first_gain, first_bias, second_gain, second_bias, query_bias, value_bias, proj_bias, up_bias, down_bias,
    rel_table,
):
    shifts, rel_table = shifts.T, rel_table.T
    vectors = [first_gain, first_bias, query_bias, value_bias, second_gain, second_bias, proj_bias, down_bias, up_bias]
    weights = [qkv_weight, proj_weight, up_weight, down_weight]
    stepped = lax.axis_size(AXES) == SHARDS
    if stepped:
        first, second = pack(vectors, weights)
        masks = piece_masks(COLUMN, PLANE, 0)
        first = spread_far(first, COLUMN)
        second = spread_far(second, COLUMN)
        first = spread_far(jnp.concatenate(first), PLANE)
        first, second = lax.optimization_barrier((first, second))
        first, second = lax.optimization_barrier((spread_core(first), jnp.concatenate(second)))
        second = spread_far(second, PLANE)
    else:
        first, second = ([x] for x in whole_weights(vectors, weights))
        masks = None
    clips = counts.shape[0]
    qkv, prob, ctx, w_qkv, vec = attend(shifts, counts, tokens, rel_table, first, masks)
    if stepped:
        ctx, far = lax.optimization_barrier((ctx, second[1:]))
        second = spread_core(second[:1] + list(far))
    parts = mlp(tokens, ctx, cotangent, vec, second, masks, stepped)
    gelu, (gmid, gctx, small, wp, wd), gsecond = parts[:4], parts[4:9], parts[9:]
    half = max(1, clips // 4)
    gqn, gpos_a = attend_back(shifts, qkv, prob, gctx, None, 0, half)
    if stepped:
        gsecond = meet_core(*gsecond)
        gqn, gsecond = lax.optimization_barrier((gqn, gsecond))
        gsecond = meet_far(gsecond, PLANE)
    gqn, gpos_b = attend_back(shifts, qkv, prob, gctx, gqn, half, clips - half)
    gfirst = project_back(gqn, tokens, w_qkv, small, gpos_a, gpos_b, stepped)
    if stepped:
        gfirst, gsecond = lax.optimization_barrier((gfirst, gsecond))
        gsecond = meet_far(add_blocks(gsecond), COLUMN)
        gfirst = meet_core(*gfirst)
        gfirst, gqn = lax.optimization_barrier((gfirst, gqn))
        gfirst = meet_far(gfirst, PLANE)
    gtok = token_back(gqn, tokens, gmid, w_qkv, vec)
    if stepped:
        gfirst, gtok, gelu = lax.optimization_barrier((gfirst, gtok, gelu))
        gfirst = meet_far(add_blocks(gfirst), COLUMN)
    out = output(gelu, ctx, tokens, wp, wd, vec)
    if stepped:
        gfirst, gsecond, out = lax.optimization_barrier((gfirst, gsecond, out))
        grads = finish(gfirst, gsecond)
        grads = (*grads[:13], grads[13].T)
    else:
        grads = whole_grads(gfirst[0], gsecond[0])
    mats, vecs, table = grads[:4], grads[4:13], grads[13]
    return (
        out, gtok, *mats, vecs[0], vecs[1], vecs[4], vecs[5], vecs[2], vecs[3], vecs[6], vecs[8], vecs[7], table,
    )


def solution(mesh):
    sharded = P(AXES, None)
    line = P(AXES)
    in_specs = (sharded, sharded, line, sharded) + (sharded,) * 4 + (line,) * 9 + (P(),)
    out_specs = (sharded,) * 6 + (line,) * 9 + (P(),)
    return jax.shard_map(on_device, mesh=mesh, in_specs=in_specs, out_specs=out_specs, check_vma=False)
```

```python
import functools

import jax
import jax.numpy as jnp
import numpy as np
from jax import lax
from jax.experimental import pallas as pl
from jax.experimental.pallas import tpu as pltpu
from jax.sharding import PartitionSpec as P

HEADS = 16
GRID_T = 64
GRID_F = 8
WIN = 4
PLACES = WIN * WIN
PATCHES = GRID_T * GRID_F
BLOCK = 64
BLOCKS = PATCHES // BLOCK
AXES = ("dp", "pair")
UNIT = 16
SHARDS = 32
RELS = (2 * WIN - 1) ** 2
CORE = (2,)
PLANE = (4, 1, 5)
COLUMN = (8, 16, 24)

EPS = 1e-06
HIGH = lax.Precision.HIGHEST
NEGATIVE = -1e30
F32 = jnp.float32
BF16 = jnp.bfloat16
LOG2_E = float(np.log2(np.e))
LOG_BELL = float(np.log2(2.0 / np.sqrt(2.0 * np.pi)))
ROWS = 32


def dot_nn(a, b):
    return lax.dot_general(a, b, (((1,), (0,)), ((), ())), preferred_element_type=F32)


def dot_nt(a, b):
    return lax.dot_general(a, b, (((1,), (1,)), ((), ())), preferred_element_type=F32)


def dot_tn(a, b):
    return lax.dot_general(a, b, (((0,), (0,)), ((), ())), preferred_element_type=F32)


def norm_stats(values):
    row_mean = jnp.mean(values, -1, keepdims=True)
    centred = values - row_mean
    inv_std = lax.rsqrt(jnp.mean(centred * centred, -1, keepdims=True) + EPS)
    return centred * inv_std, inv_std


def norm_back(grad_out, normed, inv_std, gain):
    grad_normed = grad_out * gain
    return inv_std * (
        grad_normed
        - jnp.mean(grad_normed, -1, keepdims=True)
        - normed * jnp.mean(grad_normed * normed, -1, keepdims=True)
    )


def iota(shape, dim):
    return lax.broadcasted_iota(jnp.int32, shape, dim)


def fill_perm(perm_ref, s, u):
    for r0 in range(0, PATCHES, BLOCK):
        row = iota((BLOCK, 128), 0) + r0
        t = (4 * (row >> 5) + ((row >> 2) & 3) + s) & (GRID_T - 1)
        f = (4 * ((row >> 4) & 1) + (row & 3) + u) & (GRID_F - 1)
        source = t * GRID_F + f - iota((BLOCK, 128), 1)
        for c0 in range(0, PATCHES, 128):
            perm_ref[r0 : r0 + BLOCK, c0 : c0 + 128] = jnp.where(source == c0, 1.0, 0.0).astype(BF16)


def compact_code(rows):
    row = iota((rows, 128), 0)
    lane = iota((rows, 128), 1)
    return ((lane >> 4) - (row >> 4) - (lane >> 6)) & 3


def head_lanes(dtype):
    lane = iota((16, 128), 1) >> 5
    return [jnp.where(lane == hh, 1.0, 0.0).astype(dtype) for hh in range(4)]


def expand_rows(tile, g, lanes):
    parts = []
    for hh in range(4):
        half, ab = hh & 1, hh >> 1
        for slot in range(4):
            w = (slot - half - g - 2 * ab) % 4
            parts.append(tile[16 * w : 16 * w + 16, :] * lanes[hh])
    return jnp.concatenate(parts, axis=0)


def compact(code, s0, s1):
    return jnp.where(
        code == 0,
        s0[:, :128],
        jnp.where(code == 1, s1[:, :128], jnp.where(code == 2, s0[:, 128:], s1[:, 128:])),
    )


def parts_of(x, count):
    parts = []
    for _ in range(count):
        parts.append(x.astype(BF16))
        x = x - parts[-1].astype(F32)
    return parts


def group_matrix(count, first_only):
    row = iota((128 * count, 128), 0) & 127
    same = (row >> 4) == (iota((128 * count, 128), 1) >> 4)
    if first_only:
        same = same & ((row & 15) == 0)
    return jnp.where(same, 1.0, 0.0).astype(BF16)


def put_parts(part_ref, rows, x, count):
    for i, part in enumerate(parts_of(x, count)):
        part_ref[rows, 128 * i : 128 * i + 128] = part


def allowed_tile(block, s, u, count):
    row = iota((BLOCK, 128), 0)
    key = iota((BLOCK, 128), 1) & 15
    band = 4 * (2 * block + (row >> 5))
    side = 4 * ((row >> 4) & 1)
    r_i = band + ((row >> 2) & 3) + s
    q_i = side + (row & 3) + u
    r_j = band + (key >> 2) + s
    q_j = side + (key & 3) + u
    wrap_i = (r_i >> 6) * 2 + (q_i >> 3)
    wrap_j = (r_j >> 6) * 2 + (q_j >> 3)
    visible = ((r_j & (GRID_T - 1)) < count) | ((row & 15) == key)
    return (wrap_i == wrap_j) & visible


def device_id():
    return lax.axis_index("dp") * lax.axis_size("pair") + lax.axis_index("pair")


def place_code():
    row = iota((PLACES, 256), 0)
    key = iota((PLACES, 256), 1) & 15
    return ((row >> 2) - (key >> 2) + WIN - 1) * (2 * WIN - 1) + ((row & 3) - (key & 3) + WIN - 1)


def head_select(w):
    row = iota((256, 256), 0)
    lane = iota((256, 256), 1)
    half = (lane >> 6) & 1
    e = ((lane >> 4) - w - half) & 3
    head = 8 * (lane >> 7) + 4 * (e & 1) + 2 * (e >> 1) + half
    return jnp.where((row & 15 == lane & 15) & (row >> 4 == head), 1.0, 0.0).astype(BF16)


def head_repeat():
    return jnp.where(iota((HEADS, 256), 0) == iota((HEADS, 256), 1) >> 4, 1.0, 0.0).astype(BF16)


def fill_positions(pos_ref, table_ref):
    spread = dot_tn(table_ref[...], head_repeat())
    code = place_code()
    rows = jnp.zeros((PLACES, 256), F32)
    for e in range(RELS):
        rows = jnp.where(code == e, spread[e : e + 1, :], rows)
    rows = rows.astype(BF16)
    for w in range(4):
        pos_ref[16 * w : 16 * w + 16, :] = dot_nn(rows, head_select(w))


def table_rows(gpos, scratch_ref):
    rows = jnp.zeros((PLACES, 256), F32)
    for w in range(4):
        select = head_select(w)
        for part in parts_of(gpos[16 * w : 16 * w + 16, :], 2):
            rows = rows + dot_nt(part, select)
    code = place_code()
    scratch_ref[...] = jnp.zeros_like(scratch_ref)
    for e in range(RELS):
        scratch_ref[e : e + 1, :] = jnp.sum(jnp.where(code == e, rows, 0.0), 0, keepdims=True)
    repeat = head_repeat()
    high, low = parts_of(scratch_ref[...], 2)
    return dot_nt(repeat, high) + dot_nt(repeat, low)


def mix_matrix():
    row = iota((512, 512), 0)
    lane = iota((512, 512), 1)
    return jnp.where(row == 128 * ((lane >> 4) & 3) + 16 * (lane >> 6) + (lane & 15), 1.0, 0.0).astype(BF16)


def fetch_blocks(piece_refs, masks, full_ref, sems):
    if masks is None:
        copies = [pltpu.make_async_copy(piece_refs[0], full_ref, sems.at[0])]
    else:
        me = device_id()
        copies = []
        for piece, (start, piece_masks) in zip(piece_refs, masks):
            cols = pl.ds(start, piece.shape[1])
            for j, mask in enumerate(piece_masks):
                at = pl.multiple_of((me ^ mask) * UNIT, UNIT)
                copies.append(
                    pltpu.make_async_copy(
                        piece.at[pl.ds(j * UNIT, UNIT), :], full_ref.at[pl.ds(at, UNIT), cols], sems.at[len(copies)]
                    )
                )
    for copy in copies:
        copy.start()
    return copies


def block_device(place, relative):
    if not relative:
        return place
    plane = (place >> 2) & 3
    return device_id() ^ (2 * (place >> 4) + 4 * (plane & 1) + (plane >> 1) + 8 * (place & 3))


def block_rows(place, relative):
    return pl.ds(pl.multiple_of(block_device(place, relative) * UNIT, UNIT), UNIT)


def put_block(send_refs, place, block):
    rows = send_refs[0].shape[0]
    at = place * UNIT
    send_refs[at // rows][at % rows : at % rows + UNIT, :] = block


def pack_kernel(*refs):
    vectors, (qkv_ref, proj_ref, up_ref, down_ref, first_ref, second_ref) = refs[:9], refs[9:]
    width = proj_ref.shape[1]
    first_ref[:, : 3 * width] = qkv_ref[...]
    rows = [v[...].astype(F32).reshape(1, UNIT) for v in vectors[:8]]
    bias = vectors[8][...].astype(F32).reshape(1, 4 * UNIT)
    rows += [bias[:, UNIT * q : UNIT * q + UNIT] for q in range(4)]
    rows = jnp.concatenate(rows + [jnp.zeros((116, UNIT), F32)], axis=0)
    first_ref[:, 3 * width :] = jnp.transpose(rows).astype(BF16)
    second_ref[:, :width] = proj_ref[...]
    second_ref[:, width : 5 * width] = up_ref[...]
    for q in range(4):
        second_ref[:, (5 + q) * width : (6 + q) * width] = down_ref[UNIT * q : UNIT * q + UNIT, :]


def pack(vectors, weights):
    width = weights[1].shape[1]
    return pl.pallas_call(
        pack_kernel,
        out_shape=[struct((UNIT, cols * width + more), BF16) for cols, more in ((3, 128), (9, 0))],
        compiler_params=pltpu.CompilerParams(vmem_limit_bytes=60 * 1024 * 1024),
        name="pack",
    )(*vectors, *weights)


def attend_kernel(
    masks, shift_ref, count_ref, tok_ref, table_ref, *refs
):
    pieces = refs[: 1 if masks is None else len(masks)]
    (
        qkv_ref, prob_ref, ctx_ref, w_ref, vec_ref,
        perm_ref, rows_ref, act_ref, score_ref, low_ref, ctxw_ref, pos_ref, group_ref, *part_refs, sems,
    ) = refs[len(pieces) :]
    width = tok_ref.shape[1]
    scale = (width // HEADS) ** (-0.5)
    clip = pl.program_id(0)
    s = shift_ref[0, clip]
    u = shift_ref[1, clip]
    count = count_ref[clip]

    @pl.when(clip == 0)
    def _():
        copies = fetch_blocks(pieces, masks, w_ref, sems)
        fill_positions(pos_ref, table_ref)
        for copy in copies:
            copy.wait()
        vec_ref[...] = jnp.transpose(w_ref[:, 3 * width :].astype(F32))[:16, :]
        flat = vec_ref[8:16, :].astype(BF16)
        flat = jnp.concatenate(
            [
                jnp.concatenate([flat[q : q + 1, 128 * c : 128 * c + 128] for q in range(4)], axis=1)
                for c in range(4)
            ]
            + [jnp.zeros((12, width), BF16)],
            axis=0,
        )
        vec_ref[8:16, :] = dot_nn(flat, mix_matrix())[:8, :]

    fill_perm(perm_ref, s, u)
    rows_ref[...] = dot_nn(perm_ref[...], tok_ref[...])
    for r in range(0, PATCHES, ROWS):
        normed, _ = norm_stats(rows_ref[r : r + ROWS, :])
        act_ref[r : r + ROWS, :] = (normed * vec_ref[0:1, :] + vec_ref[1:2, :]).astype(BF16)
    for c in range(3):
        cols = slice(c * width, (c + 1) * width)
        out = dot_nn(act_ref[...], w_ref[:, cols])
        if c == 0:
            out = out + vec_ref[2:3, :]
        if c == 2:
            out = out + vec_ref[3:4, :]
        qkv_ref[:, cols] = out.astype(BF16)
    lanes = head_lanes(BF16)
    code = compact_code(BLOCK)
    for b in range(BLOCKS):
        rows = slice(b * BLOCK, (b + 1) * BLOCK)
        for p in range(2):
            parts = []
            for g in range(2):
                c0 = 128 * (2 * p + g)
                keys = expand_rows(qkv_ref[rows, width + c0 : width + c0 + 128], g, lanes)
                parts.append(dot_nt(qkv_ref[rows, c0 : c0 + 128], keys))
            score_ref[rows, 128 * p : 128 * p + 128] = compact(code, *parts)
    first_lane = group_matrix(3, True)
    all_lanes = group_matrix(2, False)
    blocks = [slice(b * BLOCK, (b + 1) * BLOCK) for b in range(BLOCKS)]
    pairs = [slice(128 * p, 128 * p + 128) for p in range(2)]
    for b, rows in enumerate(blocks):
        allowed = allowed_tile(b, s, u, count)
        for p, cols in enumerate(pairs):
            logits = score_ref[rows, cols] * scale + pos_ref[:, cols]
            logits = jnp.where(allowed, logits, NEGATIVE)
            score_ref[rows, cols] = logits
            for k in (1, 2, 4, 8):
                logits = jnp.maximum(logits, pltpu.roll(logits, 128 - k, 1))
            put_parts(part_refs[p], rows, logits, 3)
    for p, cols in enumerate(pairs):
        group_ref[:, cols] = dot_nn(part_refs[p][...], first_lane)
    for p, cols in enumerate(pairs):
        for rows in blocks:
            e = jnp.exp(score_ref[rows, cols] - group_ref[rows, cols])
            score_ref[rows, cols] = e
            put_parts(part_refs[p], rows, e, 2)
    for p, cols in enumerate(pairs):
        group_ref[:, cols] = dot_nn(part_refs[p][:, :256], all_lanes)
    for p, cols in enumerate(pairs):
        for rows in blocks:
            prob = score_ref[rows, cols] * pl.reciprocal(group_ref[rows, cols])
            prob_ref[rows, cols] = prob
            low_ref[rows, cols] = prob.astype(BF16)
    spread = [jnp.where(code == e, 1.0, 0.0).astype(BF16) for e in range(4)]
    for b in range(BLOCKS):
        rows = slice(b * BLOCK, (b + 1) * BLOCK)
        for p in range(2):
            low = low_ref[rows, 128 * p : 128 * p + 128]
            for g in range(2):
                c0 = 128 * (2 * p + g)
                values = expand_rows(qkv_ref[rows, 2 * width + c0 : 2 * width + c0 + 128], g, lanes)
                wide = jnp.concatenate([low * spread[g], low * spread[2 + g]], axis=1)
                ctxw_ref[rows, c0 : c0 + 128] = dot_nn(wide, values).astype(BF16)
    ctx_ref[...] = dot_tn(perm_ref[...], ctxw_ref[...]).astype(BF16)


def weave(first, second):
    done = 0
    for i, step in enumerate(first):
        step()
        upto = (i + 1) * len(second) // len(first)
        for other in second[done:upto]:
            other()
        done = upto
    for other in second[done:]:
        other()


def mlp_kernel(
    masks, relative, tok_ref, ctx_ref, cot_ref, vec_ref, *refs
):
    pieces = refs[: 1 if masks is None else len(masks)]
    (
        *gelu_refs, gmid_ref, gctx_ref, small_ref, wp_out_ref, wd_out_ref,
    ) = refs[len(pieces) : len(pieces) + 9]
    *send_refs, w_ref, wd_ref, accp_ref, accu_ref, accd_ref, mid_ref, act_ref, branch_ref, gact_ref = refs[
        len(pieces) + 9 : -13
    ]
    hid_refs, gg_refs, gh_refs, sems = refs[-13:-9], refs[-9:-5], refs[-5:-1], refs[-1]
    keeps = [
        pltpu.make_async_copy(w_ref.at[:, : tok_ref.shape[1]], wp_out_ref, sems.at[0]),
        pltpu.make_async_copy(wd_ref, wd_out_ref, sems.at[1]),
    ]
    step = pl.program_id(0)
    tile, width = tok_ref.shape
    ff = 4 * width
    chunk = 512

    @pl.when(step == 0)
    def _():
        copies = fetch_blocks(pieces, masks, w_ref, sems)
        accp_ref[...] = jnp.zeros_like(accp_ref)
        accu_ref[...] = jnp.zeros_like(accu_ref)
        accd_ref[...] = jnp.zeros_like(accd_ref)
        small_ref[...] = jnp.zeros_like(small_ref)
        for copy in copies:
            copy.wait()
        for i in range(SHARDS):
            for q in range(4):
                at = UNIT * (4 * i + q)
                weight = w_ref[UNIT * i : UNIT * i + UNIT, (5 + q) * width : (6 + q) * width]
                wd_ref[at : at + UNIT, :] = weight * jnp.asarray(0.5, BF16)
        for keep in keeps:
            keep.start()

    gain = vec_ref[4:5, :]
    bias = vec_ref[5:6, :]
    half = chunk // 2
    count = ff // chunk
    sums = [jnp.zeros((1, width), F32) for _ in range(4)]

    def norm_rows(r):
        rows = slice(r, r + ROWS)
        mid = mid_ref[rows, :] + tok_ref[rows, :].astype(F32) + vec_ref[6:7, :]
        mid_ref[rows, :] = mid
        normed, _ = norm_stats(mid)
        act_ref[rows, :] = (normed * gain + bias).astype(BF16)

    def back_rows(r):
        rows = slice(r, r + ROWS)
        normed, inv = norm_stats(mid_ref[rows, :])
        g_act = gact_ref[rows, :]
        cot = cot_ref[rows, :].astype(F32)
        g_mid = cot + norm_back(g_act, normed, inv, gain)
        gmid_ref[rows, :] = g_mid
        g_branch = g_mid.astype(BF16)
        branch_ref[rows, :] = g_branch
        for i, part in enumerate((g_act * normed, g_act, g_branch.astype(F32), cot)):
            sums[i] = sums[i] + jnp.sum(part, 0, keepdims=True)

    totals = {}

    def bend(c, k, r):
        lanes = slice(k, k + 128)
        rows = slice(r, r + 64)
        h = hid_refs[c][rows, lanes] + vec_ref[8 + c : 9 + c, lanes]
        z = h * (0.5**0.5)
        double_phi = 1.0 + lax.erf(z)
        double_bell = jnp.exp2(LOG_BELL - (z * z) * LOG2_E)
        gelu_refs[c][rows, lanes] = (h * double_phi).astype(BF16)
        g_hidden = gg_refs[c][rows, lanes] * (double_phi + h * double_bell)
        gh_refs[c][rows, lanes] = g_hidden.astype(BF16)
        part = jnp.sum(g_hidden.reshape(8, 8, 128), 0)
        totals[c, k] = part if r == 0 else totals[c, k] + part
        if r + 64 == tile:
            small_ref[8 + c : 9 + c, lanes] += jnp.sum(totals[c, k], 0, keepdims=True)

    def up(c, m, k):
        at = width + c * chunk + k
        hid_refs[c][m : m + half, k : k + half] = dot_nn(act_ref[m : m + half, :], w_ref[:, at : at + half])

    def down_back(c, m, k):
        at = c * chunk + k
        gg_refs[c][m : m + half, k : k + half] = dot_nt(cot_ref[m : m + half, :], wd_ref[at : at + half, :])

    def up_back(c, m, k):
        weight = w_ref[k : k + half, width + c * chunk : width + (c + 1) * chunk]
        part = dot_nt(gh_refs[c][m : m + half, :], weight)
        if c == 0:
            gact_ref[m : m + half, k : k + half] = part
        else:
            gact_ref[m : m + half, k : k + half] += part

    def down_grad(c, m, k):
        at = c * chunk + m
        accd_ref[at : at + half, k : k + half] += dot_tn(gelu_refs[c][:, m : m + half], cot_ref[:, k : k + half])

    def up_grad(c, m, k):
        at = c * chunk + k
        accu_ref[m : m + half, at : at + half] += dot_tn(act_ref[:, m : m + half], gh_refs[c][:, k : k + half])

    def all_of(fn, c):
        return [functools.partial(fn, c, m, k) for k in (0, half) for m in (0, half)]

    always = step >= 0

    @pl.when(always)
    def _():
        mid_ref[...] = dot_nn(ctx_ref[...], w_ref[:, :width])
        weave(
            all_of(down_back, 0) + all_of(down_back, 1),
            [functools.partial(norm_rows, r) for r in range(0, tile, ROWS)],
        )
        weave(all_of(up, 0), [])

    for c in range(count):

        @pl.when(always)
        def _(c=c):
            products = []
            if c + 1 < count:
                products += all_of(up, c + 1)
            if c > 0:
                products += all_of(up_back, c - 1)
            if c + 2 < count:
                products += all_of(down_back, c + 2)
            if c > 1:
                products += all_of(down_grad, c - 2) + all_of(up_grad, c - 2)
            weave(products, [functools.partial(bend, c, k, r) for k in range(0, chunk, 128) for r in range(0, tile, 64)])

    @pl.when(always)
    def _():
        weave(all_of(up_back, count - 1), [])
        weave(
            all_of(down_grad, count - 2)
            + all_of(up_grad, count - 2)
            + all_of(down_grad, count - 1)
            + all_of(up_grad, count - 1),
            [functools.partial(back_rows, r) for r in range(0, tile, ROWS)],
        )
        for i in range(4):
            small_ref[4 + i : 5 + i, :] += sums[i]
        gctx_ref[...] = dot_nt(branch_ref[...], w_ref[:, :width]).astype(BF16)
        accp_ref[...] += dot_tn(ctx_ref[...], branch_ref[...])

    @pl.when(step == pl.num_programs(0) - 1)
    def _():
        for place in range(SHARDS):
            rows = block_rows(place, relative)
            block = [accp_ref[rows, :], accu_ref[rows, :]]
            down = pl.multiple_of(block_device(place, relative) * (4 * UNIT), 4 * UNIT)
            block += [accd_ref[pl.ds(down + UNIT * q, UNIT), :] * 0.5 for q in range(4)]
            put_block(send_refs, place, jnp.concatenate(block, axis=1).astype(BF16))
        for keep in keeps:
            keep.wait()


def attend_back_kernel(
    start, shift_ref, qkv_ref, prob_ref, gctx_ref, _, gqn_ref, gpos_ref,
    perm_ref, do_ref, dp_ref, low_ref, gs_ref, lowt_ref, gst_ref, gqw_ref, group_ref, *part_refs,
):
    width = gctx_ref.shape[1]
    scale = (width // HEADS) ** (-0.5)
    step = pl.program_id(0)
    s = shift_ref[0, step + start]
    u = shift_ref[1, step + start]

    @pl.when(step == 0)
    def _():
        gpos_ref[...] = jnp.zeros_like(gpos_ref)

    fill_perm(perm_ref, s, u)
    do_ref[...] = dot_nn(perm_ref[...], gctx_ref[...]).astype(BF16)
    lanes = head_lanes(BF16)
    code = compact_code(BLOCK)
    for b in range(BLOCKS):
        rows = slice(b * BLOCK, (b + 1) * BLOCK)
        for p in range(2):
            parts = []
            for g in range(2):
                c0 = 128 * (2 * p + g)
                values = expand_rows(qkv_ref[rows, 2 * width + c0 : 2 * width + c0 + 128], g, lanes)
                parts.append(dot_nt(do_ref[rows, c0 : c0 + 128], values))
            dp_ref[rows, 128 * p : 128 * p + 128] = compact(code, *parts)
    all_lanes = group_matrix(2, False)
    blocks = [slice(b * BLOCK, (b + 1) * BLOCK) for b in range(BLOCKS)]
    pairs = [slice(128 * p, 128 * p + 128) for p in range(2)]
    for p, cols in enumerate(pairs):
        for rows in blocks:
            put_parts(part_refs[p], rows, prob_ref[rows, cols] * dp_ref[rows, cols], 2)
    for p, cols in enumerate(pairs):
        group_ref[:, cols] = dot_nn(part_refs[p][...], all_lanes)
    for p, cols in enumerate(pairs):
        total = jnp.zeros((BLOCK, 128), F32)
        for rows in blocks:
            prob = prob_ref[rows, cols]
            g_scores = (prob * (dp_ref[rows, cols] - group_ref[rows, cols])).astype(BF16)
            gs_ref[rows, cols] = g_scores
            low_ref[rows, cols] = prob.astype(BF16)
            total = total + g_scores.astype(F32)
        gpos_ref[:, cols] += total
    spread = [jnp.where(code == e, 1.0, 0.0).astype(BF16) for e in range(4)]
    for b in range(BLOCKS):
        rows = slice(b * BLOCK, (b + 1) * BLOCK)
        for p in range(2):
            low = gs_ref[rows, 128 * p : 128 * p + 128]
            for g in range(2):
                c0 = 128 * (2 * p + g)
                keys = expand_rows(qkv_ref[rows, width + c0 : width + c0 + 128], g, lanes)
                wide = jnp.concatenate([low * spread[g], low * spread[2 + g]], axis=1)
                gqw_ref[rows, c0 : c0 + 128] = (dot_nn(wide, keys) * scale).astype(BF16)
    lowt_ref[...] = jnp.transpose(low_ref[...])
    gst_ref[...] = jnp.transpose(gs_ref[...])
    row_t = iota((BLOCK, 128), 0)
    lane_t = iota((BLOCK, 128), 1)
    code_t = ((row_t >> 4) - (lane_t >> 4)) & 3
    spread_t = [
        [jnp.where((code_t == d) & ((lane_t >> 6) == blk), 1.0, 0.0).astype(BF16) for d in range(4)]
        for blk in range(2)
    ]
    lane16 = iota((16, 128), 1) >> 5
    for source_ref, other_ref, other_at, out_at, factor in (
        (gst_ref, qkv_ref, 0, width, scale),
        (lowt_ref, do_ref, 0, 2 * width, 1.0),
    ):
        for two in range(BLOCKS // 2):
            places = slice(128 * two, 128 * two + 128)
            for p in range(2):
                halves = [source_ref[128 * p + 64 * h : 128 * p + 64 * h + 64, places] for h in range(2)]
                for g in range(2):
                    c0 = 128 * (2 * p + g)
                    parts = []
                    for blk in range(2):
                        for hh in range(4):
                            half, ab = hh & 1, hh >> 1
                            d = (g + 2 * ab + half) & 3
                            parts.append(halves[half] * spread_t[blk][d])
                    wide = dot_nn(
                        jnp.concatenate(parts, axis=0), other_ref[places, other_at + c0 : other_at + c0 + 128]
                    )
                    for blk in range(2):
                        for w in range(4):
                            pieces = []
                            for hh in range(4):
                                half, ab = hh & 1, hh >> 1
                                slot = (w + half + g + 2 * ab) & 3
                                at = 256 * blk + 64 * hh + 16 * slot
                                pieces.append(wide[at : at + 16, :])
                            total = jnp.where(
                                lane16 == 0,
                                pieces[0],
                                jnp.where(lane16 == 1, pieces[1], jnp.where(lane16 == 2, pieces[2], pieces[3])),
                            )
                            at = 128 * two + 64 * blk + 16 * w
                            gqw_ref[at : at + 16, out_at + c0 : out_at + c0 + 128] = (total * factor).astype(BF16)
    gqn_ref[...] = dot_tn(perm_ref[...], gqw_ref[...]).astype(BF16)


def project_back_kernel(
    relative, gqn_ref, tok_ref, w_ref, small_in_ref, gpos_a_ref, gpos_b_ref, *refs
):
    *send_refs, acc_ref, norm_ref, small_ref, sum_ref, scratch_ref, column_ref = refs
    width = tok_ref.shape[1]
    step = pl.program_id(0)

    @pl.when(step == 0)
    def _():
        acc_ref[...] = jnp.zeros_like(acc_ref)
        sum_ref[...] = jnp.zeros_like(sum_ref)
        small_ref[...] = jnp.zeros_like(small_ref)
        small_ref[:16, :] = small_in_ref[...]

    tile = tok_ref.shape[0]
    half = width // 2

    def norm_rows(r):
        rows = slice(r, r + ROWS)
        normed, _ = norm_stats(tok_ref[rows, :].astype(F32))
        norm_ref[rows, :] = normed.astype(BF16)

    def column_sums(c):
        total = jnp.zeros((8, 128), F32)
        for r in range(0, tile, 64):
            part = gqn_ref[r : r + 64, c : c + 128].astype(F32)
            total = total + jnp.sum(part.reshape(8, 8, 128), 0)
        sum_ref[0:1, c : c + 128] += jnp.sum(total, 0, keepdims=True)

    def product(m, n):
        acc_ref[m : m + half, n : n + half] += dot_tn(norm_ref[:, m : m + half], gqn_ref[:, n : n + half])

    weave([], [functools.partial(norm_rows, r) for r in range(0, tile, ROWS)])
    weave(
        [functools.partial(product, m, n) for n in range(0, 3 * width, half) for m in (0, half)],
        [functools.partial(column_sums, c) for c in range(0, 3 * width, 128)],
    )

    @pl.when(step == pl.num_programs(0) - 1)
    def _():
        small_ref[2:3, :] = sum_ref[0:1, :width]
        small_ref[3:4, :] = sum_ref[0:1, 2 * width :]
        bias = small_ref[8:16, :].astype(BF16)
        flat = dot_nt(bias, mix_matrix())
        for q in range(4):
            small_ref[8 + q : 9 + q, :] = jnp.concatenate(
                [flat[c : c + 1, 128 * q : 128 * q + 128] for c in range(4)], axis=1
            )
        table = table_rows(gpos_a_ref[...] + gpos_b_ref[...], scratch_ref)
        extra = jnp.concatenate([jnp.zeros((UNIT, 16), F32), table, jnp.zeros((UNIT, 48), F32)], axis=1)
        column_ref[...] = jnp.transpose(small_ref[...])
        lane = iota((UNIT, 128), 1)
        for place in range(SHARDS):
            rows = block_rows(place, relative)
            weight = w_ref[rows, : 3 * width].astype(F32)
            gain = w_ref[rows, 3 * width : 3 * width + 1].astype(F32)
            bias = w_ref[rows, 3 * width + 1 : 3 * width + 2].astype(F32)
            product = acc_ref[rows, :]
            total = sum_ref[0:1, :]
            g_gain = jnp.sum(product * weight, 1, keepdims=True)
            g_bias = jnp.sum(total * weight, 1, keepdims=True)
            tail = jnp.where(lane == 0, g_gain, jnp.where(lane == 1, g_bias, column_ref[rows, :] + extra))
            block = jnp.concatenate([gain * product + bias * total, tail], axis=1)
            put_block(send_refs, place, block.astype(BF16))


def token_back_kernel(gqn_ref, tok_ref, gmid_ref, w_ref, vec_ref, gtok_ref, *gact_refs):
    tile, width = tok_ref.shape
    half = tile // 2

    def product(h, n):
        rows = slice(h * half, (h + 1) * half)
        gact_refs[h][:, n : n + half] = dot_nt(gqn_ref[rows, :], w_ref[n : n + half, : 3 * width])

    def back_rows(h, r):
        rows = slice(h * half + r, h * half + r + ROWS)
        normed, inv = norm_stats(tok_ref[rows, :].astype(F32))
        g_act = gact_refs[h][r : r + ROWS, :]
        gtok_ref[rows, :] = gmid_ref[rows, :] + norm_back(g_act, normed, inv, vec_ref[0:1, :])

    steps = [[functools.partial(back_rows, h, r) for r in range(0, half, ROWS)] for h in range(2)]
    products = [[functools.partial(product, h, n) for n in range(0, width, half)] for h in range(2)]
    weave(products[0], [])
    weave(products[1], steps[0])
    weave([], steps[1])


def output_kernel(*refs):
    gelu_refs, (ctx_ref, tok_ref, wp_ref, wd_ref, vec_ref, out_ref) = refs[:4], refs[4:]
    tile, width = tok_ref.shape
    half = width // 2
    bias = vec_ref[6:7, :] + vec_ref[7:8, :]
    for n in (0, half):
        cols = slice(n, n + half)
        for m in range(0, tile, half):
            rows = slice(m, m + half)
            gelu = jnp.concatenate([ref[rows, :] for ref in gelu_refs], axis=1)
            total = dot_nn(gelu, wd_ref[:, cols]) + dot_nn(ctx_ref[rows, :], wp_ref[:, cols])
            out_ref[rows, cols] = (total + tok_ref[rows, cols].astype(F32) + bias[:, cols]).astype(BF16)


SMEM_SPEC = pl.BlockSpec(memory_space=pltpu.SMEM)
ANY_SPEC = pl.BlockSpec(memory_space=pl.ANY)


def rows_spec(rows, cols):
    return pl.BlockSpec((rows, cols), lambda i: (i, 0))


def whole_spec(shape):
    return pl.BlockSpec(shape, lambda i: (0,) * len(shape))


def struct(shape, dtype):
    return jax.ShapeDtypeStruct(shape, dtype)


def cost(flops, nbytes):
    return pl.CostEstimate(flops=flops, bytes_accessed=nbytes, transcendentals=0)


def params(mib):
    return pltpu.CompilerParams(vmem_limit_bytes=mib * 1024 * 1024, dimension_semantics=("arbitrary",))


def clip_spec(cols, start):
    return pl.BlockSpec((PATCHES, cols), lambda i: (i + start, 0))


def attend(shifts, counts, tokens, table, pieces, masks):
    n, width = tokens.shape
    cols = 3 * width + 128
    return pl.pallas_call(
        functools.partial(attend_kernel, masks),
        grid=(n // PATCHES,),
        in_specs=[SMEM_SPEC, SMEM_SPEC, rows_spec(PATCHES, width), whole_spec(table.shape)] + [ANY_SPEC] * len(pieces),
        out_specs=[
            rows_spec(PATCHES, 3 * width), rows_spec(PATCHES, 256), rows_spec(PATCHES, width),
            whole_spec((width, cols)), whole_spec((16, width)),
        ],
        out_shape=[
            struct((n, 3 * width), BF16), struct((n, 256), F32), struct((n, width), BF16),
            struct((width, cols), BF16), struct((16, width), F32),
        ],
        scratch_shapes=[
            pltpu.VMEM((PATCHES, PATCHES), BF16),
            pltpu.VMEM((PATCHES, width), F32),
            pltpu.VMEM((PATCHES, width), BF16),
            pltpu.VMEM((PATCHES, 256), F32),
            pltpu.VMEM((PATCHES, 256), BF16),
            pltpu.VMEM((PATCHES, width), BF16),
            pltpu.VMEM((BLOCK, 256), F32),
            pltpu.VMEM((PATCHES, 256), F32),
            *[pltpu.VMEM((PATCHES, 384), BF16)] * 2,
            pltpu.SemaphoreType.DMA((SHARDS,)),
        ],
        compiler_params=params(60),
        cost_estimate=cost(2800000000, n * width),
        name="attend",
    )(shifts, counts, tokens, table, *pieces)


def send_shapes(cols, relative):
    rows = SHARDS * UNIT
    return [struct((rows // 2, cols), BF16)] * 2 if relative else [struct((rows, cols), BF16)]


def mlp(tokens, ctx, cot, vec, pieces, masks, relative, tile=512):
    n, width = tokens.shape
    cols = 9 * width
    ff = 4 * width
    sends = send_shapes(cols, relative)
    return pl.pallas_call(
        functools.partial(mlp_kernel, masks, relative),
        grid=(n // tile,),
        in_specs=[rows_spec(tile, width)] * 3 + [whole_spec(vec.shape)] + [ANY_SPEC] * len(pieces),
        out_specs=[rows_spec(tile, width)] * 6
        + [whole_spec((16, width)), ANY_SPEC, ANY_SPEC]
        + [whole_spec(x.shape) for x in sends],
        out_shape=[struct((n, width), BF16)] * 4
        + [
            struct((n, width), F32), struct((n, width), BF16),
            struct((16, width), F32), struct((width, width), BF16), struct((ff, width), BF16),
        ]
        + sends,
        scratch_shapes=[
            pltpu.VMEM((width, cols), BF16),
            pltpu.VMEM((ff, width), BF16),
            pltpu.VMEM((width, width), F32),
            pltpu.VMEM((width, ff), F32),
            pltpu.VMEM((ff, width), F32),
            pltpu.VMEM((tile, width), F32),
            pltpu.VMEM((tile, width), BF16),
            pltpu.VMEM((tile, width), BF16),
            pltpu.VMEM((tile, width), F32),
            *[pltpu.VMEM((tile, width), F32)] * 8,
            *[pltpu.VMEM((tile, width), BF16)] * 4,
            pltpu.SemaphoreType.DMA((SHARDS,)),
        ],
        compiler_params=params(54),
        cost_estimate=cost(5000000000, n * width),
        name="mlp",
    )(tokens, ctx, cot, vec, *pieces)


def attend_back(shifts, qkv, prob, gctx, into, start, clips):
    n, width = gctx.shape

    def spec(cols):
        return pl.BlockSpec((PATCHES, cols), lambda i: (i + start, 0))

    return pl.pallas_call(
        functools.partial(attend_back_kernel, start),
        grid=(clips,),
        in_specs=[SMEM_SPEC, spec(3 * width), spec(256), spec(width), ANY_SPEC],
        out_specs=[spec(3 * width), whole_spec((BLOCK, 256))],
        out_shape=[struct((n, 3 * width), BF16), struct((BLOCK, 256), F32)],
        scratch_shapes=[
            pltpu.VMEM((PATCHES, PATCHES), BF16),
            pltpu.VMEM((PATCHES, width), BF16),
            pltpu.VMEM((PATCHES, 256), F32),
            pltpu.VMEM((PATCHES, 256), BF16),
            pltpu.VMEM((PATCHES, 256), BF16),
            pltpu.VMEM((256, PATCHES), BF16),
            pltpu.VMEM((256, PATCHES), BF16),
            pltpu.VMEM((PATCHES, 3 * width), BF16),
            pltpu.VMEM((PATCHES, 256), F32),
            *[pltpu.VMEM((PATCHES, 256), BF16)] * 2,
        ],
        input_output_aliases={} if into is None else {4: 0},
        compiler_params=params(24),
        cost_estimate=cost(700000000 * clips, n * width),
        name="attend_back",
    )(shifts, qkv, prob, gctx, prob if into is None else into)


def project_back(gqn, tokens, w_qkv, small, gpos_a, gpos_b, relative, tile=512):
    n, width = tokens.shape
    sends = send_shapes(w_qkv.shape[1], relative)
    return pl.pallas_call(
        functools.partial(project_back_kernel, relative),
        grid=(n // tile,),
        in_specs=[rows_spec(tile, 3 * width), rows_spec(tile, width)]
        + [whole_spec(x.shape) for x in (w_qkv, small, gpos_a, gpos_b)],
        out_specs=[whole_spec(x.shape) for x in sends],
        out_shape=sends,
        scratch_shapes=[
            pltpu.VMEM((width, 3 * width), F32),
            pltpu.VMEM((tile, width), BF16),
            pltpu.VMEM((128, width), F32),
            pltpu.VMEM((8, 3 * width), F32),
            pltpu.VMEM((64, 256), F32),
            pltpu.VMEM((width, 128), F32),
        ],
        compiler_params=params(24),
        cost_estimate=cost(1000000000, n * width),
        name="project_back",
    )(gqn, tokens, w_qkv, small, gpos_a, gpos_b)


def token_back(gqn, tokens, gmid, w_qkv, vec, tile=512):
    n, width = tokens.shape
    return pl.pallas_call(
        token_back_kernel,
        grid=(n // tile,),
        in_specs=[rows_spec(tile, 3 * width), rows_spec(tile, width), rows_spec(tile, width)]
        + [whole_spec(w_qkv.shape), whole_spec(vec.shape)],
        out_specs=rows_spec(tile, width),
        out_shape=struct((n, width), F32),
        scratch_shapes=[pltpu.VMEM((tile // 2, width), F32)] * 2,
        compiler_params=params(24),
        cost_estimate=cost(1000000000, n * width),
        name="token_back",
    )(gqn, tokens, gmid, w_qkv, vec)


def output(gelu, ctx, tokens, wp, wd, vec, tile=512):
    n, width = tokens.shape
    return pl.pallas_call(
        output_kernel,
        grid=(n // tile,),
        in_specs=[rows_spec(tile, width)] * 6
        + [whole_spec(x.shape) for x in (wp, wd, vec)],
        out_specs=rows_spec(tile, width),
        out_shape=struct((n, width), BF16),
        compiler_params=params(24),
        cost_estimate=cost(1000000000, n * width),
        name="output",
    )(*gelu, ctx, tokens, wp, wd, vec)


def finish_kernel(*refs):
    first, second = refs[:4], refs[4:8]
    gqkv_ref, gproj_ref, gup_ref, gdown_ref, *vector_refs, table_ref = refs[8:]
    width = gproj_ref.shape[1]

    def total(parts, cols):
        a, b, c, d = (part[:, cols].astype(F32) for part in parts)
        return (a + b) + (c + d)

    gqkv_ref[...] = total(first, slice(0, 3 * width))
    gproj_ref[...] = total(second, slice(0, width))
    gup_ref[...] = total(second, slice(width, 5 * width))
    for q in range(4):
        gdown_ref[UNIT * q : UNIT * q + UNIT, :] = total(second, slice((5 + q) * width, (6 + q) * width))
    extra = total(first, slice(3 * width, 3 * width + 128))
    rows = jnp.transpose(extra)
    for i in range(8):
        vector_refs[i][...] = rows[i, :]
    vector_refs[8][...] = jnp.concatenate([rows[8 + q : 9 + q, :] for q in range(4)], axis=1)[0]
    table_ref[...] = extra[:, 16 : 16 + RELS]


def finish(first, second):
    width = second[0].shape[1] // 9
    return pl.pallas_call(
        finish_kernel,
        out_shape=[
            struct((UNIT, 3 * width), F32), struct((UNIT, width), F32), struct((UNIT, 4 * width), F32),
            struct((4 * UNIT, width), F32),
            *[struct((UNIT,), F32)] * 8, struct((4 * UNIT,), F32), struct((HEADS, RELS), F32),
        ],
        compiler_params=pltpu.CompilerParams(vmem_limit_bytes=60 * 1024 * 1024),
        name="finish",
    )(*first, *second)


def exchange(x, mask):
    size = lax.axis_size(AXES)
    return lax.ppermute(x, AXES, [(i, i ^ mask) for i in range(size)])


def spread_far(block, masks):
    return [block] + [exchange(block, m) for m in masks]


def spread_core(pieces):
    return pieces + [exchange(x, CORE[0]) for x in pieces]


def piece_masks(near, far, start):
    return tuple((start, tuple(n ^ f ^ core for n in (0,) + near)) for core in (0,) + CORE for f in (0,) + far)


def add(*parts):
    parts = [p.astype(F32) for p in parts]
    while len(parts) > 1:
        parts = [parts[i] + parts[i + 1] for i in range(0, len(parts), 2)]
    return parts[0].astype(BF16)


def meet_core(keep, send):
    got = exchange(send, CORE[0])
    quarter = keep.shape[0] // 4
    return [add(keep[quarter * k : quarter * (k + 1)], got[quarter * k : quarter * (k + 1)]) for k in range(4)]


def meet_far(groups, masks):
    return [groups[0]] + [exchange(group, mask) for group, mask in zip(groups[1:], masks)]


def add_blocks(parts):
    return [add(*[p[UNIT * k : UNIT * (k + 1)] for p in parts]) for k in range(4)]


def gather(x):
    return lax.all_gather(x, AXES, axis=0, tiled=True)


def scatter(x):
    return lax.psum_scatter(x, AXES, scatter_dimension=0, tiled=True)


def by_unit(x):
    return jnp.moveaxis(x.reshape((SHARDS, 4, UNIT) + x.shape[1:]), 1, 2).reshape((SHARDS * UNIT, 4) + x.shape[1:])


def by_row(x):
    return jnp.moveaxis(x.reshape((SHARDS, UNIT, 4) + x.shape[2:]), 2, 1).reshape((4 * SHARDS * UNIT,) + x.shape[2:])


def whole_weights(vectors, weights):
    columns = [gather(v)[:, None] for v in vectors[:8]] + [by_unit(gather(vectors[8]))]
    extra = jnp.concatenate(columns, axis=1)
    qkv, proj, up, down = (gather(w) for w in weights)
    first = jnp.concatenate([qkv, extra, jnp.zeros((qkv.shape[0], 128 - extra.shape[1]), BF16)], axis=1)
    second = jnp.concatenate([proj, up, by_unit(down).reshape(proj.shape[0], -1)], axis=1)
    return first, second


def whole_grads(first, second):
    width = second.shape[1] // 9
    mats = [first[:, : 3 * width], second[:, :width], second[:, width : 5 * width]]
    mats.append(by_row(second[:, 5 * width :].reshape(-1, 4, width)))
    extra = first[:, 3 * width :]
    vectors = [extra[:, k] for k in range(8)] + [by_row(extra[:, 8:12])]
    table = lax.psum(extra[:UNIT, 16 : 16 + RELS].astype(F32), AXES).T
    return [scatter(x).astype(F32) for x in mats] + [scatter(x.astype(F32)) for x in vectors] + [table]


def local_test(
    tokens, cotangent, counts, shifts, qkv, proj, up, down, vec1, vec2, ub, table,
):
    shifts, table = shifts.T, table.T
    extra = jnp.concatenate([vec1, vec2], axis=0).T
    extra = jnp.concatenate([extra, by_unit(ub[0]), jnp.zeros((512, 116))], axis=1).astype(BF16)
    first = jnp.concatenate([qkv, extra], axis=1)
    second = jnp.concatenate([proj, up, by_unit(down).reshape(512, -1)], axis=1)
    q, prob, ctx, w_qkv, vec = attend(shifts, counts, tokens, table, [first], None)
    *gelu, gmid, gctx, small, wp, wd, gsecond = mlp(tokens, ctx, cotangent, vec, [second], None, False)
    gqn, gpos_a = attend_back(shifts, q, prob, gctx, None, 0, 2)
    gqn, gpos_b = attend_back(shifts, q, prob, gctx, gqn, 2, 2)
    (gfirst,) = project_back(gqn, tokens, w_qkv, small, gpos_a, gpos_b, False)
    gtok = token_back(gqn, tokens, gmid, w_qkv, vec)
    out = output(gelu, ctx, tokens, wp, wd, vec)
    width = 512
    e = gfirst[:, 1536:]
    mats = [gfirst[:, :1536], gsecond[:, :width], gsecond[:, width : 5 * width], by_row(gsecond[:, 5 * width :].reshape(-1, 4, width))]
    v = [e[:, k] for k in range(8)]
    return [out, gtok] + mats + [v[0], v[1], v[4], v[5], v[2], v[3], v[6], by_row(e[:, 8:12]), v[7], e[:16, 16:65].T]


def on_device(
    tokens, cotangent, counts, shifts, qkv_weight, proj_weight, up_weight, down_weight,
    first_gain, first_bias, second_gain, second_bias, query_bias, value_bias, proj_bias, up_bias, down_bias,
    rel_table,
):
    shifts, rel_table = shifts.T, rel_table.T
    vectors = [first_gain, first_bias, query_bias, value_bias, second_gain, second_bias, proj_bias, down_bias, up_bias]
    weights = [qkv_weight, proj_weight, up_weight, down_weight]
    stepped = lax.axis_size(AXES) == SHARDS
    if stepped:
        first, second = pack(vectors, weights)
        masks = piece_masks(COLUMN, PLANE, 0)
        first = spread_far(first, COLUMN)
        second = spread_far(second, COLUMN)
        first = spread_far(jnp.concatenate(first), PLANE)
        first, second = lax.optimization_barrier((first, second))
        first, second = lax.optimization_barrier((first, jnp.concatenate(second)))
        second = spread_far(second, PLANE)
        first = spread_core(first)
    else:
        first, second = ([x] for x in whole_weights(vectors, weights))
        masks = None
    clips = counts.shape[0]
    qkv, prob, ctx, w_qkv, vec = attend(shifts, counts, tokens, rel_table, first, masks)
    if stepped:
        ctx, far = lax.optimization_barrier((ctx, second[1:]))
        second = spread_core(second[:1] + list(far))
    parts = mlp(tokens, ctx, cotangent, vec, second, masks, stepped)
    gelu, (gmid, gctx, small, wp, wd), gsecond = parts[:4], parts[4:9], parts[9:]
    half = max(1, clips // 4)
    gqn, gpos_a = attend_back(shifts, qkv, prob, gctx, None, 0, half)
    if stepped:
        gsecond = meet_core(*gsecond)
        gqn, gsecond = lax.optimization_barrier((gqn, gsecond))
        gsecond = meet_far(gsecond, PLANE)
    gqn, gpos_b = attend_back(shifts, qkv, prob, gctx, gqn, half, clips - half)
    gtok = token_back(gqn, tokens, gmid, w_qkv, vec)
    gqn, gtok = lax.optimization_barrier((gqn, gtok))
    gfirst = project_back(gqn, tokens, w_qkv, small, gpos_a, gpos_b, stepped)
    if stepped:
        gfirst, gsecond = lax.optimization_barrier((gfirst, gsecond))
        gsecond = meet_far(add_blocks(gsecond), COLUMN)
        gfirst = meet_far(meet_core(*gfirst), PLANE)
        gfirst, gelu = lax.optimization_barrier((add_blocks(gfirst), gelu))
        gfirst = meet_far(gfirst, COLUMN)
    out = output(gelu, ctx, tokens, wp, wd, vec)
    if stepped:
        gfirst, gsecond, out = lax.optimization_barrier((gfirst, gsecond, out))
        grads = finish(gfirst, gsecond)
        grads = (*grads[:13], grads[13].T)
    else:
        grads = whole_grads(gfirst[0], gsecond[0])
    mats, vecs, table = grads[:4], grads[4:13], grads[13]
    return (
        out, gtok, *mats, vecs[0], vecs[1], vecs[4], vecs[5], vecs[2], vecs[3], vecs[6], vecs[8], vecs[7], table,
    )


def solution(mesh):
    sharded = P(AXES, None)
    line = P(AXES)
    in_specs = (sharded, sharded, line, sharded) + (sharded,) * 4 + (line,) * 9 + (P(),)
    out_specs = (sharded,) * 6 + (line,) * 9 + (P(),)
    return jax.shard_map(on_device, mesh=mesh, in_specs=in_specs, out_specs=out_specs, check_vma=False)
```

```python
import functools

import jax
import jax.numpy as jnp
import numpy as np
from jax import lax
from jax.experimental import pallas as pl
from jax.experimental.pallas import tpu as pltpu
from jax.sharding import PartitionSpec as P

HEADS = 16
GRID_T = 64
GRID_F = 8
WIN = 4
PLACES = WIN * WIN
PATCHES = GRID_T * GRID_F
BLOCK = 64
BLOCKS = PATCHES // BLOCK
AXES = ("dp", "pair")
UNIT = 16
SHARDS = 32
RELS = (2 * WIN - 1) ** 2
CORE = (2,)
PLANE = (4, 1, 5)
COLUMN = (8, 16, 24)

EPS = 1e-06
HIGH = lax.Precision.HIGHEST
NEGATIVE = -1e30
F32 = jnp.float32
BF16 = jnp.bfloat16
LOG2_E = float(np.log2(np.e))
LOG_BELL = float(np.log2(2.0 / np.sqrt(2.0 * np.pi)))
ROWS = 32


def dot_nn(a, b):
    return lax.dot_general(a, b, (((1,), (0,)), ((), ())), preferred_element_type=F32)


def dot_nt(a, b):
    return lax.dot_general(a, b, (((1,), (1,)), ((), ())), preferred_element_type=F32)


def dot_tn(a, b):
    return lax.dot_general(a, b, (((0,), (0,)), ((), ())), preferred_element_type=F32)


def norm_stats(values):
    row_mean = jnp.mean(values, -1, keepdims=True)
    centred = values - row_mean
    inv_std = lax.rsqrt(jnp.mean(centred * centred, -1, keepdims=True) + EPS)
    return centred * inv_std, inv_std


def norm_back(grad_out, normed, inv_std, gain):
    grad_normed = grad_out * gain
    return inv_std * (
        grad_normed
        - jnp.mean(grad_normed, -1, keepdims=True)
        - normed * jnp.mean(grad_normed * normed, -1, keepdims=True)
    )


def iota(shape, dim):
    return lax.broadcasted_iota(jnp.int32, shape, dim)


def fill_perm(perm_ref, s, u):
    for r0 in range(0, PATCHES, BLOCK):
        row = iota((BLOCK, 128), 0) + r0
        t = (4 * (row >> 5) + ((row >> 2) & 3) + s) & (GRID_T - 1)
        f = (4 * ((row >> 4) & 1) + (row & 3) + u) & (GRID_F - 1)
        source = t * GRID_F + f - iota((BLOCK, 128), 1)
        for c0 in range(0, PATCHES, 128):
            perm_ref[r0 : r0 + BLOCK, c0 : c0 + 128] = jnp.where(source == c0, 1.0, 0.0).astype(BF16)


def compact_code(rows):
    row = iota((rows, 128), 0)
    lane = iota((rows, 128), 1)
    return ((lane >> 4) - (row >> 4) - (lane >> 6)) & 3


def head_lanes(dtype):
    lane = iota((16, 128), 1) >> 5
    return [jnp.where(lane == hh, 1.0, 0.0).astype(dtype) for hh in range(4)]


def expand_rows(tile, g, lanes):
    parts = []
    for hh in range(4):
        half, ab = hh & 1, hh >> 1
        for slot in range(4):
            w = (slot - half - g - 2 * ab) % 4
            parts.append(tile[16 * w : 16 * w + 16, :] * lanes[hh])
    return jnp.concatenate(parts, axis=0)


def compact(code, s0, s1):
    return jnp.where(
        code == 0,
        s0[:, :128],
        jnp.where(code == 1, s1[:, :128], jnp.where(code == 2, s0[:, 128:], s1[:, 128:])),
    )


def parts_of(x, count):
    parts = []
    for _ in range(count):
        parts.append(x.astype(BF16))
        x = x - parts[-1].astype(F32)
    return parts


def group_matrix(count, first_only):
    row = iota((128 * count, 128), 0) & 127
    same = (row >> 4) == (iota((128 * count, 128), 1) >> 4)
    if first_only:
        same = same & ((row & 15) == 0)
    return jnp.where(same, 1.0, 0.0).astype(BF16)


def put_parts(part_ref, rows, x, count):
    for i, part in enumerate(parts_of(x, count)):
        part_ref[rows, 128 * i : 128 * i + 128] = part


def allowed_tile(block, s, u, count):
    row = iota((BLOCK, 128), 0)
    key = iota((BLOCK, 128), 1) & 15
    band = 4 * (2 * block + (row >> 5))
    side = 4 * ((row >> 4) & 1)
    r_i = band + ((row >> 2) & 3) + s
    q_i = side + (row & 3) + u
    r_j = band + (key >> 2) + s
    q_j = side + (key & 3) + u
    wrap_i = (r_i >> 6) * 2 + (q_i >> 3)
    wrap_j = (r_j >> 6) * 2 + (q_j >> 3)
    visible = ((r_j & (GRID_T - 1)) < count) | ((row & 15) == key)
    return (wrap_i == wrap_j) & visible


def device_id():
    return lax.axis_index("dp") * lax.axis_size("pair") + lax.axis_index("pair")


def place_code():
    row = iota((PLACES, 256), 0)
    key = iota((PLACES, 256), 1) & 15
    return ((row >> 2) - (key >> 2) + WIN - 1) * (2 * WIN - 1) + ((row & 3) - (key & 3) + WIN - 1)


def head_select(w):
    row = iota((256, 256), 0)
    lane = iota((256, 256), 1)
    half = (lane >> 6) & 1
    e = ((lane >> 4) - w - half) & 3
    head = 8 * (lane >> 7) + 4 * (e & 1) + 2 * (e >> 1) + half
    return jnp.where((row & 15 == lane & 15) & (row >> 4 == head), 1.0, 0.0).astype(BF16)


def head_repeat():
    return jnp.where(iota((HEADS, 256), 0) == iota((HEADS, 256), 1) >> 4, 1.0, 0.0).astype(BF16)


def fill_positions(pos_ref, table_ref):
    spread = dot_tn(table_ref[...], head_repeat())
    code = place_code()
    rows = jnp.zeros((PLACES, 256), F32)
    for e in range(RELS):
        rows = jnp.where(code == e, spread[e : e + 1, :], rows)
    rows = rows.astype(BF16)
    for w in range(4):
        pos_ref[16 * w : 16 * w + 16, :] = dot_nn(rows, head_select(w))


def table_rows(gpos, scratch_ref):
    rows = jnp.zeros((PLACES, 256), F32)
    for w in range(4):
        select = head_select(w)
        for part in parts_of(gpos[16 * w : 16 * w + 16, :], 2):
            rows = rows + dot_nt(part, select)
    code = place_code()
    scratch_ref[...] = jnp.zeros_like(scratch_ref)
    for e in range(RELS):
        scratch_ref[e : e + 1, :] = jnp.sum(jnp.where(code == e, rows, 0.0), 0, keepdims=True)
    repeat = head_repeat()
    high, low = parts_of(scratch_ref[...], 2)
    return dot_nt(repeat, high) + dot_nt(repeat, low)


def mix_matrix():
    row = iota((512, 512), 0)
    lane = iota((512, 512), 1)
    return jnp.where(row == 128 * ((lane >> 4) & 3) + 16 * (lane >> 6) + (lane & 15), 1.0, 0.0).astype(BF16)


def fetch_blocks(piece_refs, masks, full_ref, sems):
    if masks is None:
        copies = [pltpu.make_async_copy(piece_refs[0], full_ref, sems.at[0])]
    else:
        me = device_id()
        copies = []
        for piece, (start, piece_masks) in zip(piece_refs, masks):
            cols = pl.ds(start, piece.shape[1])
            for j, mask in enumerate(piece_masks):
                at = pl.multiple_of((me ^ mask) * UNIT, UNIT)
                copies.append(
                    pltpu.make_async_copy(
                        piece.at[pl.ds(j * UNIT, UNIT), :], full_ref.at[pl.ds(at, UNIT), cols], sems.at[len(copies)]
                    )
                )
    for copy in copies:
        copy.start()
    return copies


def block_device(place, relative):
    if not relative:
        return place
    plane = (place >> 2) & 3
    return device_id() ^ (2 * (place >> 4) + 4 * (plane & 1) + (plane >> 1) + 8 * (place & 3))


def block_rows(place, relative):
    return pl.ds(pl.multiple_of(block_device(place, relative) * UNIT, UNIT), UNIT)


def put_block(send_refs, place, block):
    rows = send_refs[0].shape[0]
    at = place * UNIT
    send_refs[at // rows][at % rows : at % rows + UNIT, :] = block


def pack_kernel(*refs):
    vectors, (qkv_ref, proj_ref, up_ref, down_ref, first_ref, second_ref) = refs[:9], refs[9:]
    width = proj_ref.shape[1]
    first_ref[:, : 3 * width] = qkv_ref[...]
    rows = [v[...].astype(F32).reshape(1, UNIT) for v in vectors[:8]]
    bias = vectors[8][...].astype(F32).reshape(1, 4 * UNIT)
    rows += [bias[:, UNIT * q : UNIT * q + UNIT] for q in range(4)]
    rows = jnp.concatenate(rows + [jnp.zeros((116, UNIT), F32)], axis=0)
    first_ref[:, 3 * width :] = jnp.transpose(rows).astype(BF16)
    second_ref[:, :width] = proj_ref[...]
    second_ref[:, width : 5 * width] = up_ref[...]
    for q in range(4):
        second_ref[:, (5 + q) * width : (6 + q) * width] = down_ref[UNIT * q : UNIT * q + UNIT, :]


def pack(vectors, weights):
    width = weights[1].shape[1]
    return pl.pallas_call(
        pack_kernel,
        out_shape=[struct((UNIT, cols * width + more), BF16) for cols, more in ((3, 128), (9, 0))],
        compiler_params=pltpu.CompilerParams(vmem_limit_bytes=60 * 1024 * 1024),
        name="pack",
    )(*vectors, *weights)


def attend_kernel(
    masks, shift_ref, count_ref, tok_ref, table_ref, *refs
):
    pieces = refs[: 1 if masks is None else len(masks)]
    (
        qkv_ref, prob_ref, ctx_ref, w_ref, vec_ref,
        perm_ref, rows_ref, act_ref, score_ref, low_ref, ctxw_ref, pos_ref, group_ref, *part_refs, sems,
    ) = refs[len(pieces) :]
    width = tok_ref.shape[1]
    scale = (width // HEADS) ** (-0.5)
    clip = pl.program_id(0)
    s = shift_ref[0, clip]
    u = shift_ref[1, clip]
    count = count_ref[clip]

    @pl.when(clip == 0)
    def _():
        copies = fetch_blocks(pieces, masks, w_ref, sems)
        fill_positions(pos_ref, table_ref)
        for copy in copies:
            copy.wait()
        vec_ref[...] = jnp.transpose(w_ref[:, 3 * width :].astype(F32))[:16, :]
        flat = vec_ref[8:16, :].astype(BF16)
        flat = jnp.concatenate(
            [
                jnp.concatenate([flat[q : q + 1, 128 * c : 128 * c + 128] for q in range(4)], axis=1)
                for c in range(4)
            ]
            + [jnp.zeros((12, width), BF16)],
            axis=0,
        )
        vec_ref[8:16, :] = dot_nn(flat, mix_matrix())[:8, :]

    fill_perm(perm_ref, s, u)
    rows_ref[...] = dot_nn(perm_ref[...], tok_ref[...])
    for r in range(0, PATCHES, ROWS):
        normed, _ = norm_stats(rows_ref[r : r + ROWS, :])
        act_ref[r : r + ROWS, :] = (normed * vec_ref[0:1, :] + vec_ref[1:2, :]).astype(BF16)
    for c in range(3):
        cols = slice(c * width, (c + 1) * width)
        out = dot_nn(act_ref[...], w_ref[:, cols])
        if c == 0:
            out = out + vec_ref[2:3, :]
        if c == 2:
            out = out + vec_ref[3:4, :]
        qkv_ref[:, cols] = out.astype(BF16)
    lanes = head_lanes(BF16)
    code = compact_code(BLOCK)
    for b in range(BLOCKS):
        rows = slice(b * BLOCK, (b + 1) * BLOCK)
        for p in range(2):
            parts = []
            for g in range(2):
                c0 = 128 * (2 * p + g)
                keys = expand_rows(qkv_ref[rows, width + c0 : width + c0 + 128], g, lanes)
                parts.append(dot_nt(qkv_ref[rows, c0 : c0 + 128], keys))
            score_ref[rows, 128 * p : 128 * p + 128] = compact(code, *parts)
    first_lane = group_matrix(3, True)
    all_lanes = group_matrix(2, False)
    blocks = [slice(b * BLOCK, (b + 1) * BLOCK) for b in range(BLOCKS)]
    pairs = [slice(128 * p, 128 * p + 128) for p in range(2)]
    for b, rows in enumerate(blocks):
        allowed = allowed_tile(b, s, u, count)
        for p, cols in enumerate(pairs):
            logits = score_ref[rows, cols] * scale + pos_ref[:, cols]
            logits = jnp.where(allowed, logits, NEGATIVE)
            score_ref[rows, cols] = logits
            for k in (1, 2, 4, 8):
                logits = jnp.maximum(logits, pltpu.roll(logits, 128 - k, 1))
            put_parts(part_refs[p], rows, logits, 3)
    for p, cols in enumerate(pairs):
        group_ref[:, cols] = dot_nn(part_refs[p][...], first_lane)
    for p, cols in enumerate(pairs):
        for rows in blocks:
            e = jnp.exp(score_ref[rows, cols] - group_ref[rows, cols])
            score_ref[rows, cols] = e
            put_parts(part_refs[p], rows, e, 2)
    for p, cols in enumerate(pairs):
        group_ref[:, cols] = dot_nn(part_refs[p][:, :256], all_lanes)
    for p, cols in enumerate(pairs):
        for rows in blocks:
            prob = score_ref[rows, cols] * pl.reciprocal(group_ref[rows, cols])
            prob_ref[rows, cols] = prob
            low_ref[rows, cols] = prob.astype(BF16)
    spread = [jnp.where(code == e, 1.0, 0.0).astype(BF16) for e in range(4)]
    for b in range(BLOCKS):
        rows = slice(b * BLOCK, (b + 1) * BLOCK)
        for p in range(2):
            low = low_ref[rows, 128 * p : 128 * p + 128]
            for g in range(2):
                c0 = 128 * (2 * p + g)
                values = expand_rows(qkv_ref[rows, 2 * width + c0 : 2 * width + c0 + 128], g, lanes)
                wide = jnp.concatenate([low * spread[g], low * spread[2 + g]], axis=1)
                ctxw_ref[rows, c0 : c0 + 128] = dot_nn(wide, values).astype(BF16)
    ctx_ref[...] = dot_tn(perm_ref[...], ctxw_ref[...]).astype(BF16)


def weave(first, second):
    done = 0
    for i, step in enumerate(first):
        step()
        upto = (i + 1) * len(second) // len(first)
        for other in second[done:upto]:
            other()
        done = upto
    for other in second[done:]:
        other()


def mlp_kernel(
    masks, relative, tok_ref, ctx_ref, cot_ref, vec_ref, *refs
):
    pieces = refs[: 1 if masks is None else len(masks)]
    (
        *gelu_refs, gmid_ref, gctx_ref, small_ref, wp_out_ref, wd_out_ref,
    ) = refs[len(pieces) : len(pieces) + 9]
    *send_refs, w_ref, wd_ref, accp_ref, accu_ref, accd_ref, mid_ref, act_ref, branch_ref, gact_ref = refs[
        len(pieces) + 9 : -13
    ]
    hid_refs, gg_refs, gh_refs, sems = refs[-13:-9], refs[-9:-5], refs[-5:-1], refs[-1]
    keeps = [
        pltpu.make_async_copy(w_ref.at[:, : tok_ref.shape[1]], wp_out_ref, sems.at[0]),
        pltpu.make_async_copy(wd_ref, wd_out_ref, sems.at[1]),
    ]
    step = pl.program_id(0)
    tile, width = tok_ref.shape
    ff = 4 * width
    chunk = 512

    @pl.when(step == 0)
    def _():
        copies = fetch_blocks(pieces, masks, w_ref, sems)
        accp_ref[...] = jnp.zeros_like(accp_ref)
        accu_ref[...] = jnp.zeros_like(accu_ref)
        accd_ref[...] = jnp.zeros_like(accd_ref)
        small_ref[...] = jnp.zeros_like(small_ref)
        for copy in copies:
            copy.wait()
        for i in range(SHARDS):
            for q in range(4):
                at = UNIT * (4 * i + q)
                weight = w_ref[UNIT * i : UNIT * i + UNIT, (5 + q) * width : (6 + q) * width]
                wd_ref[at : at + UNIT, :] = weight * jnp.asarray(0.5, BF16)
        for keep in keeps:
            keep.start()

    gain = vec_ref[4:5, :]
    bias = vec_ref[5:6, :]
    half = chunk // 2
    count = ff // chunk
    sums = [jnp.zeros((1, width), F32) for _ in range(4)]

    def norm_rows(r):
        rows = slice(r, r + ROWS)
        mid = mid_ref[rows, :] + tok_ref[rows, :].astype(F32) + vec_ref[6:7, :]
        mid_ref[rows, :] = mid
        normed, _ = norm_stats(mid)
        act_ref[rows, :] = (normed * gain + bias).astype(BF16)

    def back_rows(r):
        rows = slice(r, r + ROWS)
        normed, inv = norm_stats(mid_ref[rows, :])
        g_act = gact_ref[rows, :]
        cot = cot_ref[rows, :].astype(F32)
        g_mid = cot + norm_back(g_act, normed, inv, gain)
        gmid_ref[rows, :] = g_mid
        g_branch = g_mid.astype(BF16)
        branch_ref[rows, :] = g_branch
        for i, part in enumerate((g_act * normed, g_act, g_branch.astype(F32), cot)):
            sums[i] = sums[i] + jnp.sum(part, 0, keepdims=True)

    totals = {}

    def bend(c, k, r):
        lanes = slice(k, k + 128)
        rows = slice(r, r + 64)
        h = hid_refs[c][rows, lanes] + vec_ref[8 + c : 9 + c, lanes]
        z = h * (0.5**0.5)
        double_phi = 1.0 + lax.erf(z)
        double_bell = jnp.exp2(LOG_BELL - (z * z) * LOG2_E)
        gelu_refs[c][rows, lanes] = (h * double_phi).astype(BF16)
        g_hidden = gg_refs[c][rows, lanes] * (double_phi + h * double_bell)
        gh_refs[c][rows, lanes] = g_hidden.astype(BF16)
        part = jnp.sum(g_hidden.reshape(8, 8, 128), 0)
        totals[c, k] = part if r == 0 else totals[c, k] + part
        if r + 64 == tile:
            small_ref[8 + c : 9 + c, lanes] += jnp.sum(totals[c, k], 0, keepdims=True)

    def up(c, m, k):
        at = width + c * chunk + k
        hid_refs[c][m : m + half, k : k + half] = dot_nn(act_ref[m : m + half, :], w_ref[:, at : at + half])

    def down_back(c, m, k):
        at = c * chunk + k
        gg_refs[c][m : m + half, k : k + half] = dot_nt(cot_ref[m : m + half, :], wd_ref[at : at + half, :])

    def up_back(c, m, k):
        weight = w_ref[k : k + half, width + c * chunk : width + (c + 1) * chunk]
        part = dot_nt(gh_refs[c][m : m + half, :], weight)
        if c == 0:
            gact_ref[m : m + half, k : k + half] = part
        else:
            gact_ref[m : m + half, k : k + half] += part

    def down_grad(c, m, k):
        at = c * chunk + m
        accd_ref[at : at + half, k : k + half] += dot_tn(gelu_refs[c][:, m : m + half], cot_ref[:, k : k + half])

    def up_grad(c, m, k):
        at = c * chunk + k
        accu_ref[m : m + half, at : at + half] += dot_tn(act_ref[:, m : m + half], gh_refs[c][:, k : k + half])

    def all_of(fn, c):
        return [functools.partial(fn, c, m, k) for k in (0, half) for m in (0, half)]

    always = step >= 0

    @pl.when(always)
    def _():
        mid_ref[...] = dot_nn(ctx_ref[...], w_ref[:, :width])
        weave(
            all_of(down_back, 0) + all_of(down_back, 1),
            [functools.partial(norm_rows, r) for r in range(0, tile, ROWS)],
        )
        weave(all_of(up, 0), [])

    for c in range(count):

        @pl.when(always)
        def _(c=c):
            products = []
            if c + 1 < count:
                products += all_of(up, c + 1)
            if c > 0:
                products += all_of(up_back, c - 1)
            if c + 2 < count:
                products += all_of(down_back, c + 2)
            if c > 1:
                products += all_of(down_grad, c - 2) + all_of(up_grad, c - 2)
            weave(products, [functools.partial(bend, c, k, r) for k in range(0, chunk, 128) for r in range(0, tile, 64)])

    @pl.when(always)
    def _():
        weave(all_of(up_back, count - 1), [])
        weave(
            all_of(down_grad, count - 2)
            + all_of(up_grad, count - 2)
            + all_of(down_grad, count - 1)
            + all_of(up_grad, count - 1),
            [functools.partial(back_rows, r) for r in range(0, tile, ROWS)],
        )
        for i in range(4):
            small_ref[4 + i : 5 + i, :] += sums[i]
        gctx_ref[...] = dot_nt(branch_ref[...], w_ref[:, :width]).astype(BF16)
        accp_ref[...] += dot_tn(ctx_ref[...], branch_ref[...])

    @pl.when(step == pl.num_programs(0) - 1)
    def _():
        for place in range(SHARDS):
            rows = block_rows(place, relative)
            block = [accp_ref[rows, :], accu_ref[rows, :]]
            down = pl.multiple_of(block_device(place, relative) * (4 * UNIT), 4 * UNIT)
            block += [accd_ref[pl.ds(down + UNIT * q, UNIT), :] * 0.5 for q in range(4)]
            put_block(send_refs, place, jnp.concatenate(block, axis=1).astype(BF16))
        for keep in keeps:
            keep.wait()


def attend_back_kernel(
    start, shift_ref, qkv_ref, prob_ref, gctx_ref, _, gqn_ref, gpos_ref,
    perm_ref, do_ref, dp_ref, low_ref, gs_ref, lowt_ref, gst_ref, gqw_ref, group_ref, *part_refs,
):
    width = gctx_ref.shape[1]
    scale = (width // HEADS) ** (-0.5)
    step = pl.program_id(0)
    s = shift_ref[0, step + start]
    u = shift_ref[1, step + start]

    @pl.when(step == 0)
    def _():
        gpos_ref[...] = jnp.zeros_like(gpos_ref)

    fill_perm(perm_ref, s, u)
    do_ref[...] = dot_nn(perm_ref[...], gctx_ref[...]).astype(BF16)
    lanes = head_lanes(BF16)
    code = compact_code(BLOCK)
    for b in range(BLOCKS):
        rows = slice(b * BLOCK, (b + 1) * BLOCK)
        for p in range(2):
            parts = []
            for g in range(2):
                c0 = 128 * (2 * p + g)
                values = expand_rows(qkv_ref[rows, 2 * width + c0 : 2 * width + c0 + 128], g, lanes)
                parts.append(dot_nt(do_ref[rows, c0 : c0 + 128], values))
            dp_ref[rows, 128 * p : 128 * p + 128] = compact(code, *parts)
    all_lanes = group_matrix(2, False)
    blocks = [slice(b * BLOCK, (b + 1) * BLOCK) for b in range(BLOCKS)]
    pairs = [slice(128 * p, 128 * p + 128) for p in range(2)]
    for p, cols in enumerate(pairs):
        for rows in blocks:
            put_parts(part_refs[p], rows, prob_ref[rows, cols] * dp_ref[rows, cols], 2)
    for p, cols in enumerate(pairs):
        group_ref[:, cols] = dot_nn(part_refs[p][...], all_lanes)
    for p, cols in enumerate(pairs):
        total = jnp.zeros((BLOCK, 128), F32)
        for rows in blocks:
            prob = prob_ref[rows, cols]
            g_scores = (prob * (dp_ref[rows, cols] - group_ref[rows, cols])).astype(BF16)
            gs_ref[rows, cols] = g_scores
            low_ref[rows, cols] = prob.astype(BF16)
            total = total + g_scores.astype(F32)
        gpos_ref[:, cols] += total
    spread = [jnp.where(code == e, 1.0, 0.0).astype(BF16) for e in range(4)]
    for b in range(BLOCKS):
        rows = slice(b * BLOCK, (b + 1) * BLOCK)
        for p in range(2):
            low = gs_ref[rows, 128 * p : 128 * p + 128]
            for g in range(2):
                c0 = 128 * (2 * p + g)
                keys = expand_rows(qkv_ref[rows, width + c0 : width + c0 + 128], g, lanes)
                wide = jnp.concatenate([low * spread[g], low * spread[2 + g]], axis=1)
                gqw_ref[rows, c0 : c0 + 128] = (dot_nn(wide, keys) * scale).astype(BF16)
    lowt_ref[...] = jnp.transpose(low_ref[...])
    gst_ref[...] = jnp.transpose(gs_ref[...])
    row_t = iota((BLOCK, 128), 0)
    lane_t = iota((BLOCK, 128), 1)
    code_t = ((row_t >> 4) - (lane_t >> 4)) & 3
    spread_t = [
        [jnp.where((code_t == d) & ((lane_t >> 6) == blk), 1.0, 0.0).astype(BF16) for d in range(4)]
        for blk in range(2)
    ]
    lane16 = iota((16, 128), 1) >> 5
    for source_ref, other_ref, other_at, out_at, factor in (
        (gst_ref, qkv_ref, 0, width, scale),
        (lowt_ref, do_ref, 0, 2 * width, 1.0),
    ):
        for two in range(BLOCKS // 2):
            places = slice(128 * two, 128 * two + 128)
            for p in range(2):
                halves = [source_ref[128 * p + 64 * h : 128 * p + 64 * h + 64, places] for h in range(2)]
                for g in range(2):
                    c0 = 128 * (2 * p + g)
                    parts = []
                    for blk in range(2):
                        for hh in range(4):
                            half, ab = hh & 1, hh >> 1
                            d = (g + 2 * ab + half) & 3
                            parts.append(halves[half] * spread_t[blk][d])
                    wide = dot_nn(
                        jnp.concatenate(parts, axis=0), other_ref[places, other_at + c0 : other_at + c0 + 128]
                    )
                    for blk in range(2):
                        for w in range(4):
                            pieces = []
                            for hh in range(4):
                                half, ab = hh & 1, hh >> 1
                                slot = (w + half + g + 2 * ab) & 3
                                at = 256 * blk + 64 * hh + 16 * slot
                                pieces.append(wide[at : at + 16, :])
                            total = jnp.where(
                                lane16 == 0,
                                pieces[0],
                                jnp.where(lane16 == 1, pieces[1], jnp.where(lane16 == 2, pieces[2], pieces[3])),
                            )
                            at = 128 * two + 64 * blk + 16 * w
                            gqw_ref[at : at + 16, out_at + c0 : out_at + c0 + 128] = (total * factor).astype(BF16)
    gqn_ref[...] = dot_tn(perm_ref[...], gqw_ref[...]).astype(BF16)


def project_back_kernel(
    relative, gqn_ref, tok_ref, w_ref, small_in_ref, gpos_a_ref, gpos_b_ref, *refs
):
    *send_refs, acc_ref, norm_ref, small_ref, sum_ref, scratch_ref, column_ref = refs
    width = tok_ref.shape[1]
    step = pl.program_id(0)

    @pl.when(step == 0)
    def _():
        acc_ref[...] = jnp.zeros_like(acc_ref)
        sum_ref[...] = jnp.zeros_like(sum_ref)
        small_ref[...] = jnp.zeros_like(small_ref)
        small_ref[:16, :] = small_in_ref[...]

    tile = tok_ref.shape[0]
    half = width // 2

    def norm_rows(r):
        rows = slice(r, r + ROWS)
        normed, _ = norm_stats(tok_ref[rows, :].astype(F32))
        norm_ref[rows, :] = normed.astype(BF16)

    def column_sums(c):
        total = jnp.zeros((8, 128), F32)
        for r in range(0, tile, 64):
            part = gqn_ref[r : r + 64, c : c + 128].astype(F32)
            total = total + jnp.sum(part.reshape(8, 8, 128), 0)
        sum_ref[0:1, c : c + 128] += jnp.sum(total, 0, keepdims=True)

    def product(m, n):
        acc_ref[m : m + half, n : n + half] += dot_tn(norm_ref[:, m : m + half], gqn_ref[:, n : n + half])

    weave([], [functools.partial(norm_rows, r) for r in range(0, tile, ROWS)])
    weave(
        [functools.partial(product, m, n) for n in range(0, 3 * width, half) for m in (0, half)],
        [functools.partial(column_sums, c) for c in range(0, 3 * width, 128)],
    )

    @pl.when(step == pl.num_programs(0) - 1)
    def _():
        small_ref[2:3, :] = sum_ref[0:1, :width]
        small_ref[3:4, :] = sum_ref[0:1, 2 * width :]
        bias = small_ref[8:16, :].astype(BF16)
        flat = dot_nt(bias, mix_matrix())
        for q in range(4):
            small_ref[8 + q : 9 + q, :] = jnp.concatenate(
                [flat[c : c + 1, 128 * q : 128 * q + 128] for c in range(4)], axis=1
            )
        table = table_rows(gpos_a_ref[...] + gpos_b_ref[...], scratch_ref)
        extra = jnp.concatenate([jnp.zeros((UNIT, 16), F32), table, jnp.zeros((UNIT, 48), F32)], axis=1)
        column_ref[...] = jnp.transpose(small_ref[...])
        lane = iota((UNIT, 128), 1)
        for place in range(SHARDS):
            rows = block_rows(place, relative)
            weight = w_ref[rows, : 3 * width].astype(F32)
            gain = w_ref[rows, 3 * width : 3 * width + 1].astype(F32)
            bias = w_ref[rows, 3 * width + 1 : 3 * width + 2].astype(F32)
            product = acc_ref[rows, :]
            total = sum_ref[0:1, :]
            g_gain = jnp.sum(product * weight, 1, keepdims=True)
            g_bias = jnp.sum(total * weight, 1, keepdims=True)
            tail = jnp.where(lane == 0, g_gain, jnp.where(lane == 1, g_bias, column_ref[rows, :] + extra))
            block = jnp.concatenate([gain * product + bias * total, tail], axis=1)
            put_block(send_refs, place, block.astype(BF16))


def token_back_kernel(gqn_ref, tok_ref, gmid_ref, w_ref, vec_ref, gtok_ref, *gact_refs):
    tile, width = tok_ref.shape
    half = tile // 2

    def product(h, n):
        rows = slice(h * half, (h + 1) * half)
        gact_refs[h][:, n : n + half] = dot_nt(gqn_ref[rows, :], w_ref[n : n + half, : 3 * width])

    def back_rows(h, r):
        rows = slice(h * half + r, h * half + r + ROWS)
        normed, inv = norm_stats(tok_ref[rows, :].astype(F32))
        g_act = gact_refs[h][r : r + ROWS, :]
        gtok_ref[rows, :] = gmid_ref[rows, :] + norm_back(g_act, normed, inv, vec_ref[0:1, :])

    steps = [[functools.partial(back_rows, h, r) for r in range(0, half, ROWS)] for h in range(2)]
    products = [[functools.partial(product, h, n) for n in range(0, width, half)] for h in range(2)]
    weave(products[0], [])
    weave(products[1], steps[0])
    weave([], steps[1])


def output_kernel(*refs):
    gelu_refs, (ctx_ref, tok_ref, wp_ref, wd_ref, vec_ref, _, out_ref) = refs[:4], refs[4:]
    tile, width = tok_ref.shape
    half = width // 2
    bias = vec_ref[6:7, :] + vec_ref[7:8, :]
    for n in (0, half):
        cols = slice(n, n + half)
        for m in range(0, tile, half):
            rows = slice(m, m + half)
            gelu = jnp.concatenate([ref[rows, :] for ref in gelu_refs], axis=1)
            total = dot_nn(gelu, wd_ref[:, cols]) + dot_nn(ctx_ref[rows, :], wp_ref[:, cols])
            out_ref[rows, cols] = (total + tok_ref[rows, cols].astype(F32) + bias[:, cols]).astype(BF16)


SMEM_SPEC = pl.BlockSpec(memory_space=pltpu.SMEM)
ANY_SPEC = pl.BlockSpec(memory_space=pl.ANY)


def rows_spec(rows, cols):
    return pl.BlockSpec((rows, cols), lambda i: (i, 0))


def whole_spec(shape):
    return pl.BlockSpec(shape, lambda i: (0,) * len(shape))


def struct(shape, dtype):
    return jax.ShapeDtypeStruct(shape, dtype)


def cost(flops, nbytes):
    return pl.CostEstimate(flops=flops, bytes_accessed=nbytes, transcendentals=0)


def params(mib):
    return pltpu.CompilerParams(vmem_limit_bytes=mib * 1024 * 1024, dimension_semantics=("arbitrary",))


def clip_spec(cols, start):
    return pl.BlockSpec((PATCHES, cols), lambda i: (i + start, 0))


def attend(shifts, counts, tokens, table, pieces, masks):
    n, width = tokens.shape
    cols = 3 * width + 128
    return pl.pallas_call(
        functools.partial(attend_kernel, masks),
        grid=(n // PATCHES,),
        in_specs=[SMEM_SPEC, SMEM_SPEC, rows_spec(PATCHES, width), whole_spec(table.shape)] + [ANY_SPEC] * len(pieces),
        out_specs=[
            rows_spec(PATCHES, 3 * width), rows_spec(PATCHES, 256), rows_spec(PATCHES, width),
            whole_spec((width, cols)), whole_spec((16, width)),
        ],
        out_shape=[
            struct((n, 3 * width), BF16), struct((n, 256), F32), struct((n, width), BF16),
            struct((width, cols), BF16), struct((16, width), F32),
        ],
        scratch_shapes=[
            pltpu.VMEM((PATCHES, PATCHES), BF16),
            pltpu.VMEM((PATCHES, width), F32),
            pltpu.VMEM((PATCHES, width), BF16),
            pltpu.VMEM((PATCHES, 256), F32),
            pltpu.VMEM((PATCHES, 256), BF16),
            pltpu.VMEM((PATCHES, width), BF16),
            pltpu.VMEM((BLOCK, 256), F32),
            pltpu.VMEM((PATCHES, 256), F32),
            *[pltpu.VMEM((PATCHES, 384), BF16)] * 2,
            pltpu.SemaphoreType.DMA((SHARDS,)),
        ],
        compiler_params=params(60),
        cost_estimate=cost(2800000000, n * width),
        name="attend",
    )(shifts, counts, tokens, table, *pieces)


def send_shapes(cols, relative):
    rows = SHARDS * UNIT
    return [struct((rows // 2, cols), BF16)] * 2 if relative else [struct((rows, cols), BF16)]


def mlp(tokens, ctx, cot, vec, pieces, masks, relative, tile=512):
    n, width = tokens.shape
    cols = 9 * width
    ff = 4 * width
    sends = send_shapes(cols, relative)
    return pl.pallas_call(
        functools.partial(mlp_kernel, masks, relative),
        grid=(n // tile,),
        in_specs=[rows_spec(tile, width)] * 3 + [whole_spec(vec.shape)] + [ANY_SPEC] * len(pieces),
        out_specs=[rows_spec(tile, width)] * 6
        + [whole_spec((16, width)), ANY_SPEC, ANY_SPEC]
        + [whole_spec(x.shape) for x in sends],
        out_shape=[struct((n, width), BF16)] * 4
        + [
            struct((n, width), F32), struct((n, width), BF16),
            struct((16, width), F32), struct((width, width), BF16), struct((ff, width), BF16),
        ]
        + sends,
        scratch_shapes=[
            pltpu.VMEM((width, cols), BF16),
            pltpu.VMEM((ff, width), BF16),
            pltpu.VMEM((width, width), F32),
            pltpu.VMEM((width, ff), F32),
            pltpu.VMEM((ff, width), F32),
            pltpu.VMEM((tile, width), F32),
            pltpu.VMEM((tile, width), BF16),
            pltpu.VMEM((tile, width), BF16),
            pltpu.VMEM((tile, width), F32),
            *[pltpu.VMEM((tile, width), F32)] * 8,
            *[pltpu.VMEM((tile, width), BF16)] * 4,
            pltpu.SemaphoreType.DMA((SHARDS,)),
        ],
        compiler_params=params(54),
        cost_estimate=cost(5000000000, n * width),
        name="mlp",
    )(tokens, ctx, cot, vec, *pieces)


def attend_back(shifts, qkv, prob, gctx, into, start, clips):
    n, width = gctx.shape

    def spec(cols):
        return pl.BlockSpec((PATCHES, cols), lambda i: (i + start, 0))

    return pl.pallas_call(
        functools.partial(attend_back_kernel, start),
        grid=(clips,),
        in_specs=[SMEM_SPEC, spec(3 * width), spec(256), spec(width), ANY_SPEC],
        out_specs=[spec(3 * width), whole_spec((BLOCK, 256))],
        out_shape=[struct((n, 3 * width), BF16), struct((BLOCK, 256), F32)],
        scratch_shapes=[
            pltpu.VMEM((PATCHES, PATCHES), BF16),
            pltpu.VMEM((PATCHES, width), BF16),
            pltpu.VMEM((PATCHES, 256), F32),
            pltpu.VMEM((PATCHES, 256), BF16),
            pltpu.VMEM((PATCHES, 256), BF16),
            pltpu.VMEM((256, PATCHES), BF16),
            pltpu.VMEM((256, PATCHES), BF16),
            pltpu.VMEM((PATCHES, 3 * width), BF16),
            pltpu.VMEM((PATCHES, 256), F32),
            *[pltpu.VMEM((PATCHES, 256), BF16)] * 2,
        ],
        input_output_aliases={} if into is None else {4: 0},
        compiler_params=params(24),
        cost_estimate=cost(700000000 * clips, n * width),
        name="attend_back",
    )(shifts, qkv, prob, gctx, prob if into is None else into)


def project_back(gqn, tokens, w_qkv, small, gpos_a, gpos_b, relative, tile=512):
    n, width = tokens.shape
    sends = send_shapes(w_qkv.shape[1], relative)
    return pl.pallas_call(
        functools.partial(project_back_kernel, relative),
        grid=(n // tile,),
        in_specs=[rows_spec(tile, 3 * width), rows_spec(tile, width)]
        + [whole_spec(x.shape) for x in (w_qkv, small, gpos_a, gpos_b)],
        out_specs=[whole_spec(x.shape) for x in sends],
        out_shape=sends,
        scratch_shapes=[
            pltpu.VMEM((width, 3 * width), F32),
            pltpu.VMEM((tile, width), BF16),
            pltpu.VMEM((128, width), F32),
            pltpu.VMEM((8, 3 * width), F32),
            pltpu.VMEM((64, 256), F32),
            pltpu.VMEM((width, 128), F32),
        ],
        compiler_params=params(24),
        cost_estimate=cost(1000000000, n * width),
        name="project_back",
    )(gqn, tokens, w_qkv, small, gpos_a, gpos_b)


def token_back(gqn, tokens, gmid, w_qkv, vec, tile=512):
    n, width = tokens.shape
    return pl.pallas_call(
        token_back_kernel,
        grid=(n // tile,),
        in_specs=[rows_spec(tile, 3 * width), rows_spec(tile, width), rows_spec(tile, width)]
        + [whole_spec(w_qkv.shape), whole_spec(vec.shape)],
        out_specs=rows_spec(tile, width),
        out_shape=struct((n, width), F32),
        scratch_shapes=[pltpu.VMEM((tile // 2, width), F32)] * 2,
        compiler_params=params(24),
        cost_estimate=cost(1000000000, n * width),
        name="token_back",
    )(gqn, tokens, gmid, w_qkv, vec)


def output(gelu, ctx, tokens, wp, wd, vec, into, start, count, tile=512):
    n, width = tokens.shape

    def spec(cols):
        return pl.BlockSpec((tile, cols), lambda i: (i + start, 0))

    return pl.pallas_call(
        output_kernel,
        grid=(count,),
        in_specs=[spec(width)] * 6 + [whole_spec(x.shape) for x in (wp, wd, vec)] + [ANY_SPEC],
        out_specs=spec(width),
        out_shape=struct((n, width), BF16),
        input_output_aliases={} if into is None else {9: 0},
        compiler_params=params(24),
        cost_estimate=cost(1000000000, n * width),
        name="output",
    )(*gelu, ctx, tokens, wp, wd, vec, ctx if into is None else into)


def finish_kernel(*refs):
    first, second = refs[:4], refs[4:8]
    gqkv_ref, gproj_ref, gup_ref, gdown_ref, *vector_refs, table_ref = refs[8:]
    width = gproj_ref.shape[1]

    def total(parts, cols):
        a, b, c, d = (part[:, cols].astype(F32) for part in parts)
        return (a + b) + (c + d)

    gqkv_ref[...] = total(first, slice(0, 3 * width))
    gproj_ref[...] = total(second, slice(0, width))
    gup_ref[...] = total(second, slice(width, 5 * width))
    for q in range(4):
        gdown_ref[UNIT * q : UNIT * q + UNIT, :] = total(second, slice((5 + q) * width, (6 + q) * width))
    extra = total(first, slice(3 * width, 3 * width + 128))
    rows = jnp.transpose(extra)
    for i in range(8):
        vector_refs[i][...] = rows[i, :]
    vector_refs[8][...] = jnp.concatenate([rows[8 + q : 9 + q, :] for q in range(4)], axis=1)[0]
    table_ref[...] = extra[:, 16 : 16 + RELS]


def finish(first, second):
    width = second[0].shape[1] // 9
    return pl.pallas_call(
        finish_kernel,
        out_shape=[
            struct((UNIT, 3 * width), F32), struct((UNIT, width), F32), struct((UNIT, 4 * width), F32),
            struct((4 * UNIT, width), F32),
            *[struct((UNIT,), F32)] * 8, struct((4 * UNIT,), F32), struct((HEADS, RELS), F32),
        ],
        compiler_params=pltpu.CompilerParams(vmem_limit_bytes=16 * 1024 * 1024),
        name="finish",
    )(*first, *second)


def exchange(x, mask):
    size = lax.axis_size(AXES)
    return lax.ppermute(x, AXES, [(i, i ^ mask) for i in range(size)])


def spread_far(block, masks):
    return [block] + [exchange(block, m) for m in masks]


def spread_core(pieces):
    return pieces + [exchange(x, CORE[0]) for x in pieces]


def piece_masks(near, far, start):
    return tuple((start, tuple(n ^ f ^ core for n in (0,) + near)) for core in (0,) + CORE for f in (0,) + far)


def add(*parts):
    parts = [p.astype(F32) for p in parts]
    while len(parts) > 1:
        parts = [parts[i] + parts[i + 1] for i in range(0, len(parts), 2)]
    return parts[0].astype(BF16)


def meet_core(keep, send):
    got = exchange(send, CORE[0])
    quarter = keep.shape[0] // 4
    return [add(keep[quarter * k : quarter * (k + 1)], got[quarter * k : quarter * (k + 1)]) for k in range(4)]


def meet_far(groups, masks):
    return [groups[0]] + [exchange(group, mask) for group, mask in zip(groups[1:], masks)]


def add_blocks(parts):
    return [add(*[p[UNIT * k : UNIT * (k + 1)] for p in parts]) for k in range(4)]


def gather(x):
    return lax.all_gather(x, AXES, axis=0, tiled=True)


def scatter(x):
    return lax.psum_scatter(x, AXES, scatter_dimension=0, tiled=True)


def by_unit(x):
    return jnp.moveaxis(x.reshape((SHARDS, 4, UNIT) + x.shape[1:]), 1, 2).reshape((SHARDS * UNIT, 4) + x.shape[1:])


def by_row(x):
    return jnp.moveaxis(x.reshape((SHARDS, UNIT, 4) + x.shape[2:]), 2, 1).reshape((4 * SHARDS * UNIT,) + x.shape[2:])


def whole_weights(vectors, weights):
    columns = [gather(v)[:, None] for v in vectors[:8]] + [by_unit(gather(vectors[8]))]
    extra = jnp.concatenate(columns, axis=1)
    qkv, proj, up, down = (gather(w) for w in weights)
    first = jnp.concatenate([qkv, extra, jnp.zeros((qkv.shape[0], 128 - extra.shape[1]), BF16)], axis=1)
    second = jnp.concatenate([proj, up, by_unit(down).reshape(proj.shape[0], -1)], axis=1)
    return first, second


def whole_grads(first, second):
    width = second.shape[1] // 9
    mats = [first[:, : 3 * width], second[:, :width], second[:, width : 5 * width]]
    mats.append(by_row(second[:, 5 * width :].reshape(-1, 4, width)))
    extra = first[:, 3 * width :]
    vectors = [extra[:, k] for k in range(8)] + [by_row(extra[:, 8:12])]
    table = lax.psum(extra[:UNIT, 16 : 16 + RELS].astype(F32), AXES).T
    return [scatter(x).astype(F32) for x in mats] + [scatter(x.astype(F32)) for x in vectors] + [table]


def local_test(
    tokens, cotangent, counts, shifts, qkv, proj, up, down, vec1, vec2, ub, table,
):
    shifts, table = shifts.T, table.T
    extra = jnp.concatenate([vec1, vec2], axis=0).T
    extra = jnp.concatenate([extra, by_unit(ub[0]), jnp.zeros((512, 116))], axis=1).astype(BF16)
    first = jnp.concatenate([qkv, extra], axis=1)
    second = jnp.concatenate([proj, up, by_unit(down).reshape(512, -1)], axis=1)
    q, prob, ctx, w_qkv, vec = attend(shifts, counts, tokens, table, [first], None)
    *gelu, gmid, gctx, small, wp, wd, gsecond = mlp(tokens, ctx, cotangent, vec, [second], None, False)
    gqn, gpos_a = attend_back(shifts, q, prob, gctx, None, 0, 2)
    gqn, gpos_b = attend_back(shifts, q, prob, gctx, gqn, 2, 2)
    (gfirst,) = project_back(gqn, tokens, w_qkv, small, gpos_a, gpos_b, False)
    gtok = token_back(gqn, tokens, gmid, w_qkv, vec)
    out = output(gelu, ctx, tokens, wp, wd, vec, None, 0, 2)
    out = output(gelu, ctx, tokens, wp, wd, vec, out, 2, 2)
    width = 512
    e = gfirst[:, 1536:]
    mats = [gfirst[:, :1536], gsecond[:, :width], gsecond[:, width : 5 * width], by_row(gsecond[:, 5 * width :].reshape(-1, 4, width))]
    v = [e[:, k] for k in range(8)]
    return [out, gtok] + mats + [v[0], v[1], v[4], v[5], v[2], v[3], v[6], by_row(e[:, 8:12]), v[7], e[:16, 16:65].T]


def on_device(
    tokens, cotangent, counts, shifts, qkv_weight, proj_weight, up_weight, down_weight,
    first_gain, first_bias, second_gain, second_bias, query_bias, value_bias, proj_bias, up_bias, down_bias,
    rel_table,
):
    shifts, rel_table = shifts.T, rel_table.T
    vectors = [first_gain, first_bias, query_bias, value_bias, second_gain, second_bias, proj_bias, down_bias, up_bias]
    weights = [qkv_weight, proj_weight, up_weight, down_weight]
    stepped = lax.axis_size(AXES) == SHARDS
    if stepped:
        first, second = pack(vectors, weights)
        masks = piece_masks(COLUMN, PLANE, 0)
        first = spread_far(first, COLUMN)
        second = spread_far(second, COLUMN)
        first = spread_far(jnp.concatenate(first), PLANE)
        first, second = lax.optimization_barrier((first, jnp.concatenate(second)))
        second = spread_far(second, PLANE)
        first = spread_core(first)
    else:
        first, second = ([x] for x in whole_weights(vectors, weights))
        masks = None
    clips = counts.shape[0]
    qkv, prob, ctx, w_qkv, vec = attend(shifts, counts, tokens, rel_table, first, masks)
    if stepped:
        ctx, far = lax.optimization_barrier((ctx, second[1:]))
        second = spread_core(second[:1] + list(far))
    parts = mlp(tokens, ctx, cotangent, vec, second, masks, stepped)
    gelu, (gmid, gctx, small, wp, wd), gsecond = parts[:4], parts[4:9], parts[9:]
    half = max(1, clips // 4)
    gqn, gpos_a = attend_back(shifts, qkv, prob, gctx, None, 0, half)
    if stepped:
        gsecond = meet_core(*gsecond)
        gqn, gsecond = lax.optimization_barrier((gqn, gsecond))
        gsecond = meet_far(gsecond, PLANE)
    gqn, gpos_b = attend_back(shifts, qkv, prob, gctx, gqn, half, clips - half)
    gtok = token_back(gqn, tokens, gmid, w_qkv, vec)
    gqn, gtok = lax.optimization_barrier((gqn, gtok))
    gfirst = project_back(gqn, tokens, w_qkv, small, gpos_a, gpos_b, stepped)
    if stepped:
        gfirst, gsecond = lax.optimization_barrier((gfirst, gsecond))
        gsecond = meet_far(add_blocks(gsecond), COLUMN)
        gfirst = meet_core(*gfirst)
        gfirst, gelu = lax.optimization_barrier((gfirst, gelu))
        gfirst = meet_far(gfirst, PLANE)
    tiles = tokens.shape[0] // 512
    out = output(gelu, ctx, tokens, wp, wd, vec, None, 0, tiles // 2)
    if stepped:
        gfirst, out = lax.optimization_barrier((gfirst, out))
        gfirst, out = lax.optimization_barrier((add_blocks(gfirst), out))
        gfirst = meet_far(gfirst, COLUMN)
    out = output(gelu, ctx, tokens, wp, wd, vec, out, tiles // 2, tiles - tiles // 2)
    if stepped:
        gfirst, gsecond, out = lax.optimization_barrier((gfirst, gsecond, out))
        grads = finish(gfirst, gsecond)
        grads = (*grads[:13], grads[13].T)
    else:
        grads = whole_grads(gfirst[0], gsecond[0])
    mats, vecs, table = grads[:4], grads[4:13], grads[13]
    return (
        out, gtok, *mats, vecs[0], vecs[1], vecs[4], vecs[5], vecs[2], vecs[3], vecs[6], vecs[8], vecs[7], table,
    )


def solution(mesh):
    sharded = P(AXES, None)
    line = P(AXES)
    in_specs = (sharded, sharded, line, sharded) + (sharded,) * 4 + (line,) * 9 + (P(),)
    out_specs = (sharded,) * 6 + (line,) * 9 + (P(),)
    return jax.shard_map(on_device, mesh=mesh, in_specs=in_specs, out_specs=out_specs, check_vma=False)
```

```python
import functools

import jax
import jax.numpy as jnp
import numpy as np
from jax import lax
from jax.experimental import pallas as pl
from jax.experimental.pallas import tpu as pltpu
from jax.sharding import PartitionSpec as P

HEADS = 16
GRID_T = 64
GRID_F = 8
WIN = 4
PLACES = WIN * WIN
PATCHES = GRID_T * GRID_F
BLOCK = 64
BLOCKS = PATCHES // BLOCK
AXES = ("dp", "pair")
UNIT = 16
SHARDS = 32
RELS = (2 * WIN - 1) ** 2
CORE = (2,)
PLANE = (4, 1, 5)
COLUMN = (8, 16, 24)

EPS = 1e-06
HIGH = lax.Precision.HIGHEST
NEGATIVE = -1e30
F32 = jnp.float32
BF16 = jnp.bfloat16
LOG2_E = float(np.log2(np.e))
LOG_BELL = float(np.log2(2.0 / np.sqrt(2.0 * np.pi)))
ROWS = 32


def dot_nn(a, b):
    return lax.dot_general(a, b, (((1,), (0,)), ((), ())), preferred_element_type=F32)


def dot_nt(a, b):
    return lax.dot_general(a, b, (((1,), (1,)), ((), ())), preferred_element_type=F32)


def dot_tn(a, b):
    return lax.dot_general(a, b, (((0,), (0,)), ((), ())), preferred_element_type=F32)


def norm_stats(values):
    row_mean = jnp.mean(values, -1, keepdims=True)
    centred = values - row_mean
    inv_std = lax.rsqrt(jnp.mean(centred * centred, -1, keepdims=True) + EPS)
    return centred * inv_std, inv_std


def norm_back(grad_out, normed, inv_std, gain):
    grad_normed = grad_out * gain
    return inv_std * (
        grad_normed
        - jnp.mean(grad_normed, -1, keepdims=True)
        - normed * jnp.mean(grad_normed * normed, -1, keepdims=True)
    )


def iota(shape, dim):
    return lax.broadcasted_iota(jnp.int32, shape, dim)


def fill_perm(perm_ref, s, u):
    for r0 in range(0, PATCHES, BLOCK):
        row = iota((BLOCK, 128), 0) + r0
        t = (4 * (row >> 5) + ((row >> 2) & 3) + s) & (GRID_T - 1)
        f = (4 * ((row >> 4) & 1) + (row & 3) + u) & (GRID_F - 1)
        source = t * GRID_F + f - iota((BLOCK, 128), 1)
        for c0 in range(0, PATCHES, 128):
            perm_ref[r0 : r0 + BLOCK, c0 : c0 + 128] = jnp.where(source == c0, 1.0, 0.0).astype(BF16)


def compact_code(rows):
    row = iota((rows, 128), 0)
    lane = iota((rows, 128), 1)
    return ((lane >> 4) - (row >> 4) - (lane >> 6)) & 3


def head_lanes(dtype):
    lane = iota((16, 128), 1) >> 5
    return [jnp.where(lane == hh, 1.0, 0.0).astype(dtype) for hh in range(4)]


def expand_rows(tile, g, lanes):
    parts = []
    for hh in range(4):
        half, ab = hh & 1, hh >> 1
        for slot in range(4):
            w = (slot - half - g - 2 * ab) % 4
            parts.append(tile[16 * w : 16 * w + 16, :] * lanes[hh])
    return jnp.concatenate(parts, axis=0)


def compact(code, s0, s1):
    return jnp.where(
        code == 0,
        s0[:, :128],
        jnp.where(code == 1, s1[:, :128], jnp.where(code == 2, s0[:, 128:], s1[:, 128:])),
    )


def parts_of(x, count):
    parts = []
    for _ in range(count):
        parts.append(x.astype(BF16))
        x = x - parts[-1].astype(F32)
    return parts


def group_matrix(count, first_only):
    row = iota((128 * count, 128), 0) & 127
    same = (row >> 4) == (iota((128 * count, 128), 1) >> 4)
    if first_only:
        same = same & ((row & 15) == 0)
    return jnp.where(same, 1.0, 0.0).astype(BF16)


def put_parts(part_ref, rows, x, count):
    for i, part in enumerate(parts_of(x, count)):
        part_ref[rows, 128 * i : 128 * i + 128] = part


def allowed_tile(block, s, u, count):
    row = iota((BLOCK, 128), 0)
    key = iota((BLOCK, 128), 1) & 15
    band = 4 * (2 * block + (row >> 5))
    side = 4 * ((row >> 4) & 1)
    r_i = band + ((row >> 2) & 3) + s
    q_i = side + (row & 3) + u
    r_j = band + (key >> 2) + s
    q_j = side + (key & 3) + u
    wrap_i = (r_i >> 6) * 2 + (q_i >> 3)
    wrap_j = (r_j >> 6) * 2 + (q_j >> 3)
    visible = ((r_j & (GRID_T - 1)) < count) | ((row & 15) == key)
    return (wrap_i == wrap_j) & visible


def device_id():
    return lax.axis_index("dp") * lax.axis_size("pair") + lax.axis_index("pair")


def place_code():
    row = iota((PLACES, 256), 0)
    key = iota((PLACES, 256), 1) & 15
    return ((row >> 2) - (key >> 2) + WIN - 1) * (2 * WIN - 1) + ((row & 3) - (key & 3) + WIN - 1)


def head_select(w):
    row = iota((256, 256), 0)
    lane = iota((256, 256), 1)
    half = (lane >> 6) & 1
    e = ((lane >> 4) - w - half) & 3
    head = 8 * (lane >> 7) + 4 * (e & 1) + 2 * (e >> 1) + half
    return jnp.where((row & 15 == lane & 15) & (row >> 4 == head), 1.0, 0.0).astype(BF16)


def head_repeat():
    return jnp.where(iota((HEADS, 256), 0) == iota((HEADS, 256), 1) >> 4, 1.0, 0.0).astype(BF16)


def fill_positions(pos_ref, table_ref):
    spread = dot_tn(table_ref[...], head_repeat())
    code = place_code()
    rows = jnp.zeros((PLACES, 256), F32)
    for e in range(RELS):
        rows = jnp.where(code == e, spread[e : e + 1, :], rows)
    rows = rows.astype(BF16)
    for w in range(4):
        pos_ref[16 * w : 16 * w + 16, :] = dot_nn(rows, head_select(w))


def table_rows(gpos, scratch_ref):
    rows = jnp.zeros((PLACES, 256), F32)
    for w in range(4):
        select = head_select(w)
        for part in parts_of(gpos[16 * w : 16 * w + 16, :], 2):
            rows = rows + dot_nt(part, select)
    code = place_code()
    scratch_ref[...] = jnp.zeros_like(scratch_ref)
    for e in range(RELS):
        scratch_ref[e : e + 1, :] = jnp.sum(jnp.where(code == e, rows, 0.0), 0, keepdims=True)
    repeat = head_repeat()
    high, low = parts_of(scratch_ref[...], 2)
    return dot_nt(repeat, high) + dot_nt(repeat, low)


def mix_matrix():
    row = iota((512, 512), 0)
    lane = iota((512, 512), 1)
    return jnp.where(row == 128 * ((lane >> 4) & 3) + 16 * (lane >> 6) + (lane & 15), 1.0, 0.0).astype(BF16)


def fetch_blocks(piece_refs, masks, full_ref, sems):
    if masks is None:
        copies = [pltpu.make_async_copy(piece_refs[0], full_ref, sems.at[0])]
    else:
        me = device_id()
        copies = []
        for piece, (start, piece_masks) in zip(piece_refs, masks):
            cols = pl.ds(start, piece.shape[1])
            for j, mask in enumerate(piece_masks):
                at = pl.multiple_of((me ^ mask) * UNIT, UNIT)
                copies.append(
                    pltpu.make_async_copy(
                        piece.at[pl.ds(j * UNIT, UNIT), :], full_ref.at[pl.ds(at, UNIT), cols], sems.at[len(copies)]
                    )
                )
    for copy in copies:
        copy.start()
    return copies


def block_device(place, relative):
    if not relative:
        return place
    plane = (place >> 2) & 3
    return device_id() ^ (2 * (place >> 4) + 4 * (plane & 1) + (plane >> 1) + 8 * (place & 3))


def block_rows(place, relative):
    return pl.ds(pl.multiple_of(block_device(place, relative) * UNIT, UNIT), UNIT)


def put_block(send_refs, place, block):
    rows = send_refs[0].shape[0]
    at = place * UNIT
    send_refs[at // rows][at % rows : at % rows + UNIT, :] = block


def pack_kernel(*refs):
    vectors, (qkv_ref, proj_ref, up_ref, down_ref, first_ref, second_ref) = refs[:9], refs[9:]
    width = proj_ref.shape[1]
    first_ref[:, : 3 * width] = qkv_ref[...]
    rows = [v[...].astype(F32).reshape(1, UNIT) for v in vectors[:8]]
    bias = vectors[8][...].astype(F32).reshape(1, 4 * UNIT)
    rows += [bias[:, UNIT * q : UNIT * q + UNIT] for q in range(4)]
    rows = jnp.concatenate(rows + [jnp.zeros((116, UNIT), F32)], axis=0)
    first_ref[:, 3 * width :] = jnp.transpose(rows).astype(BF16)
    second_ref[:, :width] = proj_ref[...]
    second_ref[:, width : 5 * width] = up_ref[...]
    for q in range(4):
        second_ref[:, (5 + q) * width : (6 + q) * width] = down_ref[UNIT * q : UNIT * q + UNIT, :]


def pack(vectors, weights):
    width = weights[1].shape[1]
    return pl.pallas_call(
        pack_kernel,
        out_shape=[struct((UNIT, cols * width + more), BF16) for cols, more in ((3, 128), (9, 0))],
        compiler_params=pltpu.CompilerParams(vmem_limit_bytes=60 * 1024 * 1024),
        name="pack",
    )(*vectors, *weights)


def attend_kernel(
    masks, shift_ref, count_ref, tok_ref, table_ref, *refs
):
    pieces = refs[: 1 if masks is None else len(masks)]
    (
        qkv_ref, prob_ref, ctx_ref, w_ref, vec_ref,
        perm_ref, rows_ref, act_ref, score_ref, low_ref, ctxw_ref, pos_ref, group_ref, *part_refs, sems,
    ) = refs[len(pieces) :]
    width = tok_ref.shape[1]
    scale = (width // HEADS) ** (-0.5)
    clip = pl.program_id(0)
    s = shift_ref[0, clip]
    u = shift_ref[1, clip]
    count = count_ref[clip]

    @pl.when(clip == 0)
    def _():
        copies = fetch_blocks(pieces, masks, w_ref, sems)
        fill_positions(pos_ref, table_ref)
        for copy in copies:
            copy.wait()
        vec_ref[...] = jnp.transpose(w_ref[:, 3 * width :].astype(F32))[:16, :]
        flat = vec_ref[8:16, :].astype(BF16)
        flat = jnp.concatenate(
            [
                jnp.concatenate([flat[q : q + 1, 128 * c : 128 * c + 128] for q in range(4)], axis=1)
                for c in range(4)
            ]
            + [jnp.zeros((12, width), BF16)],
            axis=0,
        )
        vec_ref[8:16, :] = dot_nn(flat, mix_matrix())[:8, :]

    fill_perm(perm_ref, s, u)
    rows_ref[...] = dot_nn(perm_ref[...], tok_ref[...])
    for r in range(0, PATCHES, ROWS):
        normed, _ = norm_stats(rows_ref[r : r + ROWS, :])
        act_ref[r : r + ROWS, :] = (normed * vec_ref[0:1, :] + vec_ref[1:2, :]).astype(BF16)
    for c in range(3):
        cols = slice(c * width, (c + 1) * width)
        out = dot_nn(act_ref[...], w_ref[:, cols])
        if c == 0:
            out = out + vec_ref[2:3, :]
        if c == 2:
            out = out + vec_ref[3:4, :]
        qkv_ref[:, cols] = out.astype(BF16)
    lanes = head_lanes(BF16)
    code = compact_code(BLOCK)
    for b in range(BLOCKS):
        rows = slice(b * BLOCK, (b + 1) * BLOCK)
        for p in range(2):
            parts = []
            for g in range(2):
                c0 = 128 * (2 * p + g)
                keys = expand_rows(qkv_ref[rows, width + c0 : width + c0 + 128], g, lanes)
                parts.append(dot_nt(qkv_ref[rows, c0 : c0 + 128], keys))
            score_ref[rows, 128 * p : 128 * p + 128] = compact(code, *parts)
    first_lane = group_matrix(3, True)
    all_lanes = group_matrix(2, False)
    blocks = [slice(b * BLOCK, (b + 1) * BLOCK) for b in range(BLOCKS)]
    pairs = [slice(128 * p, 128 * p + 128) for p in range(2)]
    for b, rows in enumerate(blocks):
        allowed = allowed_tile(b, s, u, count)
        for p, cols in enumerate(pairs):
            logits = score_ref[rows, cols] * scale + pos_ref[:, cols]
            logits = jnp.where(allowed, logits, NEGATIVE)
            score_ref[rows, cols] = logits
            for k in (1, 2, 4, 8):
                logits = jnp.maximum(logits, pltpu.roll(logits, 128 - k, 1))
            put_parts(part_refs[p], rows, logits, 3)
    for p, cols in enumerate(pairs):
        group_ref[:, cols] = dot_nn(part_refs[p][...], first_lane)
    for p, cols in enumerate(pairs):
        for rows in blocks:
            e = jnp.exp(score_ref[rows, cols] - group_ref[rows, cols])
            score_ref[rows, cols] = e
            put_parts(part_refs[p], rows, e, 2)
    for p, cols in enumerate(pairs):
        group_ref[:, cols] = dot_nn(part_refs[p][:, :256], all_lanes)
    for p, cols in enumerate(pairs):
        for rows in blocks:
            prob = score_ref[rows, cols] * pl.reciprocal(group_ref[rows, cols])
            prob_ref[rows, cols] = prob
            low_ref[rows, cols] = prob.astype(BF16)
    spread = [jnp.where(code == e, 1.0, 0.0).astype(BF16) for e in range(4)]
    for b in range(BLOCKS):
        rows = slice(b * BLOCK, (b + 1) * BLOCK)
        for p in range(2):
            low = low_ref[rows, 128 * p : 128 * p + 128]
            for g in range(2):
                c0 = 128 * (2 * p + g)
                values = expand_rows(qkv_ref[rows, 2 * width + c0 : 2 * width + c0 + 128], g, lanes)
                wide = jnp.concatenate([low * spread[g], low * spread[2 + g]], axis=1)
                ctxw_ref[rows, c0 : c0 + 128] = dot_nn(wide, values).astype(BF16)
    ctx_ref[...] = dot_tn(perm_ref[...], ctxw_ref[...]).astype(BF16)


def weave(first, second):
    done = 0
    for i, step in enumerate(first):
        step()
        upto = (i + 1) * len(second) // len(first)
        for other in second[done:upto]:
            other()
        done = upto
    for other in second[done:]:
        other()


def mlp_kernel(
    masks, relative, tok_ref, ctx_ref, cot_ref, vec_ref, *refs
):
    pieces = refs[: 1 if masks is None else len(masks)]
    (
        *gelu_refs, gmid_ref, gctx_ref, small_ref, wp_out_ref, wd_out_ref,
    ) = refs[len(pieces) : len(pieces) + 9]
    *send_refs, w_ref, wd_ref, accp_ref, accu_ref, accd_ref, mid_ref, act_ref, branch_ref, gact_ref = refs[
        len(pieces) + 9 : -13
    ]
    hid_refs, gg_refs, gh_refs, sems = refs[-13:-9], refs[-9:-5], refs[-5:-1], refs[-1]
    keeps = [
        pltpu.make_async_copy(w_ref.at[:, : tok_ref.shape[1]], wp_out_ref, sems.at[0]),
        pltpu.make_async_copy(wd_ref, wd_out_ref, sems.at[1]),
    ]
    step = pl.program_id(0)
    tile, width = tok_ref.shape
    ff = 4 * width
    chunk = 512

    @pl.when(step == 0)
    def _():
        copies = fetch_blocks(pieces, masks, w_ref, sems)
        accp_ref[...] = jnp.zeros_like(accp_ref)
        accu_ref[...] = jnp.zeros_like(accu_ref)
        accd_ref[...] = jnp.zeros_like(accd_ref)
        small_ref[...] = jnp.zeros_like(small_ref)
        for copy in copies:
            copy.wait()
        for i in range(SHARDS):
            for q in range(4):
                at = UNIT * (4 * i + q)
                weight = w_ref[UNIT * i : UNIT * i + UNIT, (5 + q) * width : (6 + q) * width]
                wd_ref[at : at + UNIT, :] = weight * jnp.asarray(0.5, BF16)
        for keep in keeps:
            keep.start()

    gain = vec_ref[4:5, :]
    bias = vec_ref[5:6, :]
    half = chunk // 2
    count = ff // chunk
    sums = [jnp.zeros((1, width), F32) for _ in range(4)]

    def norm_rows(r):
        rows = slice(r, r + ROWS)
        mid = mid_ref[rows, :] + tok_ref[rows, :].astype(F32) + vec_ref[6:7, :]
        mid_ref[rows, :] = mid
        normed, _ = norm_stats(mid)
        act_ref[rows, :] = (normed * gain + bias).astype(BF16)

    def back_rows(r):
        rows = slice(r, r + ROWS)
        normed, inv = norm_stats(mid_ref[rows, :])
        g_act = gact_ref[rows, :]
        cot = cot_ref[rows, :].astype(F32)
        g_mid = cot + norm_back(g_act, normed, inv, gain)
        gmid_ref[rows, :] = g_mid
        g_branch = g_mid.astype(BF16)
        branch_ref[rows, :] = g_branch
        for i, part in enumerate((g_act * normed, g_act, g_branch.astype(F32), cot)):
            sums[i] = sums[i] + jnp.sum(part, 0, keepdims=True)

    totals = {}

    def bend(c, k, r):
        lanes = slice(k, k + 128)
        rows = slice(r, r + 64)
        h = hid_refs[c][rows, lanes] + vec_ref[8 + c : 9 + c, lanes]
        z = h * (0.5**0.5)
        double_phi = 1.0 + lax.erf(z)
        double_bell = jnp.exp2(LOG_BELL - (z * z) * LOG2_E)
        gelu_refs[c][rows, lanes] = (h * double_phi).astype(BF16)
        g_hidden = gg_refs[c][rows, lanes] * (double_phi + h * double_bell)
        gh_refs[c][rows, lanes] = g_hidden.astype(BF16)
        part = jnp.sum(g_hidden.reshape(8, 8, 128), 0)
        totals[c, k] = part if r == 0 else totals[c, k] + part
        if r + 64 == tile:
            small_ref[8 + c : 9 + c, lanes] += jnp.sum(totals[c, k], 0, keepdims=True)

    def up(c, m, k):
        at = width + c * chunk + k
        hid_refs[c][m : m + half, k : k + half] = dot_nn(act_ref[m : m + half, :], w_ref[:, at : at + half])

    def down_back(c, m, k):
        at = c * chunk + k
        gg_refs[c][m : m + half, k : k + half] = dot_nt(cot_ref[m : m + half, :], wd_ref[at : at + half, :])

    def up_back(c, m, k):
        weight = w_ref[k : k + half, width + c * chunk : width + (c + 1) * chunk]
        part = dot_nt(gh_refs[c][m : m + half, :], weight)
        if c == 0:
            gact_ref[m : m + half, k : k + half] = part
        else:
            gact_ref[m : m + half, k : k + half] += part

    def down_grad(c, m, k):
        if k == 0:
            at = c * chunk + m
            accd_ref[at : at + half, :] += dot_tn(gelu_refs[c][:, m : m + half], cot_ref[...])

    def up_grad(c, m, k):
        if k == 0:
            at = c * chunk
            accu_ref[m : m + half, at : at + chunk] += dot_tn(act_ref[:, m : m + half], gh_refs[c][...])

    def all_of(fn, c):
        return [functools.partial(fn, c, m, k) for k in (0, half) for m in (0, half)]

    always = step >= 0

    @pl.when(always)
    def _():
        mid_ref[...] = dot_nn(ctx_ref[...], w_ref[:, :width])
        weave(
            all_of(down_back, 0) + all_of(down_back, 1),
            [functools.partial(norm_rows, r) for r in range(0, tile, ROWS)],
        )
        weave(all_of(up, 0), [])

    for c in range(count):

        @pl.when(always)
        def _(c=c):
            products = []
            if c + 1 < count:
                products += all_of(up, c + 1)
            if c > 0:
                products += all_of(up_back, c - 1)
            if c + 2 < count:
                products += all_of(down_back, c + 2)
            if c > 1:
                products += all_of(down_grad, c - 2) + all_of(up_grad, c - 2)
            weave(products, [functools.partial(bend, c, k, r) for k in range(0, chunk, 128) for r in range(0, tile, 64)])

    @pl.when(always)
    def _():
        weave(all_of(up_back, count - 1), [])
        weave(
            all_of(down_grad, count - 2)
            + all_of(up_grad, count - 2)
            + all_of(down_grad, count - 1)
            + all_of(up_grad, count - 1),
            [functools.partial(back_rows, r) for r in range(0, tile, ROWS)],
        )
        for i in range(4):
            small_ref[4 + i : 5 + i, :] += sums[i]
        gctx_ref[...] = dot_nt(branch_ref[...], w_ref[:, :width]).astype(BF16)
        accp_ref[...] += dot_tn(ctx_ref[...], branch_ref[...])

    @pl.when(step == pl.num_programs(0) - 1)
    def _():
        for place in range(SHARDS):
            rows = block_rows(place, relative)
            block = [accp_ref[rows, :], accu_ref[rows, :]]
            down = pl.multiple_of(block_device(place, relative) * (4 * UNIT), 4 * UNIT)
            block += [accd_ref[pl.ds(down + UNIT * q, UNIT), :] * 0.5 for q in range(4)]
            put_block(send_refs, place, jnp.concatenate(block, axis=1).astype(BF16))
        for keep in keeps:
            keep.wait()


def attend_back_kernel(
    start, shift_ref, qkv_ref, prob_ref, gctx_ref, _, gqn_ref, gpos_ref,
    perm_ref, do_ref, dp_ref, low_ref, gs_ref, lowt_ref, gst_ref, gqw_ref, group_ref, *part_refs,
):
    width = gctx_ref.shape[1]
    scale = (width // HEADS) ** (-0.5)
    step = pl.program_id(0)
    s = shift_ref[0, step + start]
    u = shift_ref[1, step + start]

    @pl.when(step == 0)
    def _():
        gpos_ref[...] = jnp.zeros_like(gpos_ref)

    fill_perm(perm_ref, s, u)
    do_ref[...] = dot_nn(perm_ref[...], gctx_ref[...]).astype(BF16)
    lanes = head_lanes(BF16)
    code = compact_code(BLOCK)
    for b in range(BLOCKS):
        rows = slice(b * BLOCK, (b + 1) * BLOCK)
        for p in range(2):
            parts = []
            for g in range(2):
                c0 = 128 * (2 * p + g)
                values = expand_rows(qkv_ref[rows, 2 * width + c0 : 2 * width + c0 + 128], g, lanes)
                parts.append(dot_nt(do_ref[rows, c0 : c0 + 128], values))
            dp_ref[rows, 128 * p : 128 * p + 128] = compact(code, *parts)
    all_lanes = group_matrix(2, False)
    blocks = [slice(b * BLOCK, (b + 1) * BLOCK) for b in range(BLOCKS)]
    pairs = [slice(128 * p, 128 * p + 128) for p in range(2)]
    for p, cols in enumerate(pairs):
        for rows in blocks:
            put_parts(part_refs[p], rows, prob_ref[rows, cols] * dp_ref[rows, cols], 2)
    for p, cols in enumerate(pairs):
        group_ref[:, cols] = dot_nn(part_refs[p][...], all_lanes)
    for p, cols in enumerate(pairs):
        total = jnp.zeros((BLOCK, 128), F32)
        for rows in blocks:
            prob = prob_ref[rows, cols]
            g_scores = (prob * (dp_ref[rows, cols] - group_ref[rows, cols])).astype(BF16)
            gs_ref[rows, cols] = g_scores
            low_ref[rows, cols] = prob.astype(BF16)
            total = total + g_scores.astype(F32)
        gpos_ref[:, cols] += total
    spread = [jnp.where(code == e, 1.0, 0.0).astype(BF16) for e in range(4)]
    for b in range(BLOCKS):
        rows = slice(b * BLOCK, (b + 1) * BLOCK)
        for p in range(2):
            low = gs_ref[rows, 128 * p : 128 * p + 128]
            for g in range(2):
                c0 = 128 * (2 * p + g)
                keys = expand_rows(qkv_ref[rows, width + c0 : width + c0 + 128], g, lanes)
                wide = jnp.concatenate([low * spread[g], low * spread[2 + g]], axis=1)
                gqw_ref[rows, c0 : c0 + 128] = (dot_nn(wide, keys) * scale).astype(BF16)
    lowt_ref[...] = jnp.transpose(low_ref[...])
    gst_ref[...] = jnp.transpose(gs_ref[...])
    row_t = iota((BLOCK, 128), 0)
    lane_t = iota((BLOCK, 128), 1)
    code_t = ((row_t >> 4) - (lane_t >> 4)) & 3
    spread_t = [
        [jnp.where((code_t == d) & ((lane_t >> 6) == blk), 1.0, 0.0).astype(BF16) for d in range(4)]
        for blk in range(2)
    ]
    lane16 = iota((16, 128), 1) >> 5
    for source_ref, other_ref, other_at, out_at, factor in (
        (gst_ref, qkv_ref, 0, width, scale),
        (lowt_ref, do_ref, 0, 2 * width, 1.0),
    ):
        for two in range(BLOCKS // 2):
            places = slice(128 * two, 128 * two + 128)
            for p in range(2):
                halves = [source_ref[128 * p + 64 * h : 128 * p + 64 * h + 64, places] for h in range(2)]
                for g in range(2):
                    c0 = 128 * (2 * p + g)
                    parts = []
                    for blk in range(2):
                        for hh in range(4):
                            half, ab = hh & 1, hh >> 1
                            d = (g + 2 * ab + half) & 3
                            parts.append(halves[half] * spread_t[blk][d])
                    wide = dot_nn(
                        jnp.concatenate(parts, axis=0), other_ref[places, other_at + c0 : other_at + c0 + 128]
                    )
                    for blk in range(2):
                        for w in range(4):
                            pieces = []
                            for hh in range(4):
                                half, ab = hh & 1, hh >> 1
                                slot = (w + half + g + 2 * ab) & 3
                                at = 256 * blk + 64 * hh + 16 * slot
                                pieces.append(wide[at : at + 16, :])
                            total = jnp.where(
                                lane16 == 0,
                                pieces[0],
                                jnp.where(lane16 == 1, pieces[1], jnp.where(lane16 == 2, pieces[2], pieces[3])),
                            )
                            at = 128 * two + 64 * blk + 16 * w
                            gqw_ref[at : at + 16, out_at + c0 : out_at + c0 + 128] = (total * factor).astype(BF16)
    gqn_ref[...] = dot_tn(perm_ref[...], gqw_ref[...]).astype(BF16)


def project_back_kernel(
    relative, gqn_ref, tok_ref, w_ref, small_in_ref, gpos_a_ref, gpos_b_ref, *refs
):
    *send_refs, acc_ref, norm_ref, small_ref, sum_ref, scratch_ref, column_ref = refs
    width = tok_ref.shape[1]
    step = pl.program_id(0)

    @pl.when(step == 0)
    def _():
        acc_ref[...] = jnp.zeros_like(acc_ref)
        sum_ref[...] = jnp.zeros_like(sum_ref)
        small_ref[...] = jnp.zeros_like(small_ref)
        small_ref[:16, :] = small_in_ref[...]

    tile = tok_ref.shape[0]
    half = width // 2

    def norm_rows(r):
        rows = slice(r, r + ROWS)
        normed, _ = norm_stats(tok_ref[rows, :].astype(F32))
        norm_ref[rows, :] = normed.astype(BF16)

    def column_sums(c):
        total = jnp.zeros((8, 128), F32)
        for r in range(0, tile, 64):
            part = gqn_ref[r : r + 64, c : c + 128].astype(F32)
            total = total + jnp.sum(part.reshape(8, 8, 128), 0)
        sum_ref[0:1, c : c + 128] += jnp.sum(total, 0, keepdims=True)

    def product(m, n):
        acc_ref[m : m + half, n : n + half] += dot_tn(norm_ref[:, m : m + half], gqn_ref[:, n : n + half])

    weave([], [functools.partial(norm_rows, r) for r in range(0, tile, ROWS)])
    weave(
        [functools.partial(product, m, n) for n in range(0, 3 * width, half) for m in (0, half)],
        [functools.partial(column_sums, c) for c in range(0, 3 * width, 128)],
    )

    @pl.when(step == pl.num_programs(0) - 1)
    def _():
        small_ref[2:3, :] = sum_ref[0:1, :width]
        small_ref[3:4, :] = sum_ref[0:1, 2 * width :]
        bias = small_ref[8:16, :].astype(BF16)
        flat = dot_nt(bias, mix_matrix())
        for q in range(4):
            small_ref[8 + q : 9 + q, :] = jnp.concatenate(
                [flat[c : c + 1, 128 * q : 128 * q + 128] for c in range(4)], axis=1
            )
        table = table_rows(gpos_a_ref[...] + gpos_b_ref[...], scratch_ref)
        extra = jnp.concatenate([jnp.zeros((UNIT, 16), F32), table, jnp.zeros((UNIT, 48), F32)], axis=1)
        column_ref[...] = jnp.transpose(small_ref[...])
        lane = iota((UNIT, 128), 1)
        for place in range(SHARDS):
            rows = block_rows(place, relative)
            weight = w_ref[rows, : 3 * width].astype(F32)
            gain = w_ref[rows, 3 * width : 3 * width + 1].astype(F32)
            bias = w_ref[rows, 3 * width + 1 : 3 * width + 2].astype(F32)
            product = acc_ref[rows, :]
            total = sum_ref[0:1, :]
            g_gain = jnp.sum(product * weight, 1, keepdims=True)
            g_bias = jnp.sum(total * weight, 1, keepdims=True)
            tail = jnp.where(lane == 0, g_gain, jnp.where(lane == 1, g_bias, column_ref[rows, :] + extra))
            block = jnp.concatenate([gain * product + bias * total, tail], axis=1)
            put_block(send_refs, place, block.astype(BF16))


def token_back_kernel(gqn_ref, tok_ref, gmid_ref, w_ref, vec_ref, gtok_ref, *gact_refs):
    tile, width = tok_ref.shape
    half = tile // 2

    def product(h, n):
        rows = slice(h * half, (h + 1) * half)
        gact_refs[h][:, n : n + half] = dot_nt(gqn_ref[rows, :], w_ref[n : n + half, : 3 * width])

    def back_rows(h, r):
        rows = slice(h * half + r, h * half + r + ROWS)
        normed, inv = norm_stats(tok_ref[rows, :].astype(F32))
        g_act = gact_refs[h][r : r + ROWS, :]
        gtok_ref[rows, :] = gmid_ref[rows, :] + norm_back(g_act, normed, inv, vec_ref[0:1, :])

    steps = [[functools.partial(back_rows, h, r) for r in range(0, half, ROWS)] for h in range(2)]
    products = [[functools.partial(product, h, n) for n in range(0, width, half)] for h in range(2)]
    weave(products[0], [])
    weave(products[1], steps[0])
    weave([], steps[1])


def output_kernel(*refs):
    gelu_refs, (ctx_ref, tok_ref, wp_ref, wd_ref, vec_ref, _, out_ref) = refs[:4], refs[4:]
    tile, width = tok_ref.shape
    half = width // 2
    bias = vec_ref[6:7, :] + vec_ref[7:8, :]
    for n in (0, half):
        cols = slice(n, n + half)
        for m in range(0, tile, half):
            rows = slice(m, m + half)
            gelu = jnp.concatenate([ref[rows, :] for ref in gelu_refs], axis=1)
            total = dot_nn(gelu, wd_ref[:, cols]) + dot_nn(ctx_ref[rows, :], wp_ref[:, cols])
            out_ref[rows, cols] = (total + tok_ref[rows, cols].astype(F32) + bias[:, cols]).astype(BF16)


SMEM_SPEC = pl.BlockSpec(memory_space=pltpu.SMEM)
ANY_SPEC = pl.BlockSpec(memory_space=pl.ANY)


def rows_spec(rows, cols):
    return pl.BlockSpec((rows, cols), lambda i: (i, 0))


def whole_spec(shape):
    return pl.BlockSpec(shape, lambda i: (0,) * len(shape))


def struct(shape, dtype):
    return jax.ShapeDtypeStruct(shape, dtype)


def cost(flops, nbytes):
    return pl.CostEstimate(flops=flops, bytes_accessed=nbytes, transcendentals=0)


def params(mib):
    return pltpu.CompilerParams(vmem_limit_bytes=mib * 1024 * 1024, dimension_semantics=("arbitrary",))


def clip_spec(cols, start):
    return pl.BlockSpec((PATCHES, cols), lambda i: (i + start, 0))


def attend(shifts, counts, tokens, table, pieces, masks):
    n, width = tokens.shape
    cols = 3 * width + 128
    return pl.pallas_call(
        functools.partial(attend_kernel, masks),
        grid=(n // PATCHES,),
        in_specs=[SMEM_SPEC, SMEM_SPEC, rows_spec(PATCHES, width), whole_spec(table.shape)] + [ANY_SPEC] * len(pieces),
        out_specs=[
            rows_spec(PATCHES, 3 * width), rows_spec(PATCHES, 256), rows_spec(PATCHES, width),
            whole_spec((width, cols)), whole_spec((16, width)),
        ],
        out_shape=[
            struct((n, 3 * width), BF16), struct((n, 256), F32), struct((n, width), BF16),
            struct((width, cols), BF16), struct((16, width), F32),
        ],
        scratch_shapes=[
            pltpu.VMEM((PATCHES, PATCHES), BF16),
            pltpu.VMEM((PATCHES, width), F32),
            pltpu.VMEM((PATCHES, width), BF16),
            pltpu.VMEM((PATCHES, 256), F32),
            pltpu.VMEM((PATCHES, 256), BF16),
            pltpu.VMEM((PATCHES, width), BF16),
            pltpu.VMEM((BLOCK, 256), F32),
            pltpu.VMEM((PATCHES, 256), F32),
            *[pltpu.VMEM((PATCHES, 384), BF16)] * 2,
            pltpu.SemaphoreType.DMA((SHARDS,)),
        ],
        compiler_params=params(60),
        cost_estimate=cost(2800000000, n * width),
        name="attend",
    )(shifts, counts, tokens, table, *pieces)


def send_shapes(cols, relative):
    rows = SHARDS * UNIT
    return [struct((rows // 2, cols), BF16)] * 2 if relative else [struct((rows, cols), BF16)]


def mlp(tokens, ctx, cot, vec, pieces, masks, relative, tile=512):
    n, width = tokens.shape
    cols = 9 * width
    ff = 4 * width
    sends = send_shapes(cols, relative)
    return pl.pallas_call(
        functools.partial(mlp_kernel, masks, relative),
        grid=(n // tile,),
        in_specs=[rows_spec(tile, width)] * 3 + [whole_spec(vec.shape)] + [ANY_SPEC] * len(pieces),
        out_specs=[rows_spec(tile, width)] * 6
        + [whole_spec((16, width)), ANY_SPEC, ANY_SPEC]
        + [whole_spec(x.shape) for x in sends],
        out_shape=[struct((n, width), BF16)] * 4
        + [
            struct((n, width), F32), struct((n, width), BF16),
            struct((16, width), F32), struct((width, width), BF16), struct((ff, width), BF16),
        ]
        + sends,
        scratch_shapes=[
            pltpu.VMEM((width, cols), BF16),
            pltpu.VMEM((ff, width), BF16),
            pltpu.VMEM((width, width), F32),
            pltpu.VMEM((width, ff), F32),
            pltpu.VMEM((ff, width), F32),
            pltpu.VMEM((tile, width), F32),
            pltpu.VMEM((tile, width), BF16),
            pltpu.VMEM((tile, width), BF16),
            pltpu.VMEM((tile, width), F32),
            *[pltpu.VMEM((tile, width), F32)] * 8,
            *[pltpu.VMEM((tile, width), BF16)] * 4,
            pltpu.SemaphoreType.DMA((SHARDS,)),
        ],
        compiler_params=params(54),
        cost_estimate=cost(5000000000, n * width),
        name="mlp",
    )(tokens, ctx, cot, vec, *pieces)


def attend_back(shifts, qkv, prob, gctx, into, start, clips):
    n, width = gctx.shape

    def spec(cols):
        return pl.BlockSpec((PATCHES, cols), lambda i: (i + start, 0))

    return pl.pallas_call(
        functools.partial(attend_back_kernel, start),
        grid=(clips,),
        in_specs=[SMEM_SPEC, spec(3 * width), spec(256), spec(width), ANY_SPEC],
        out_specs=[spec(3 * width), whole_spec((BLOCK, 256))],
        out_shape=[struct((n, 3 * width), BF16), struct((BLOCK, 256), F32)],
        scratch_shapes=[
            pltpu.VMEM((PATCHES, PATCHES), BF16),
            pltpu.VMEM((PATCHES, width), BF16),
            pltpu.VMEM((PATCHES, 256), F32),
            pltpu.VMEM((PATCHES, 256), BF16),
            pltpu.VMEM((PATCHES, 256), BF16),
            pltpu.VMEM((256, PATCHES), BF16),
            pltpu.VMEM((256, PATCHES), BF16),
            pltpu.VMEM((PATCHES, 3 * width), BF16),
            pltpu.VMEM((PATCHES, 256), F32),
            *[pltpu.VMEM((PATCHES, 256), BF16)] * 2,
        ],
        input_output_aliases={} if into is None else {4: 0},
        compiler_params=params(24),
        cost_estimate=cost(700000000 * clips, n * width),
        name="attend_back",
    )(shifts, qkv, prob, gctx, prob if into is None else into)


def project_back(gqn, tokens, w_qkv, small, gpos_a, gpos_b, relative, tile=512):
    n, width = tokens.shape
    sends = send_shapes(w_qkv.shape[1], relative)
    return pl.pallas_call(
        functools.partial(project_back_kernel, relative),
        grid=(n // tile,),
        in_specs=[rows_spec(tile, 3 * width), rows_spec(tile, width)]
        + [whole_spec(x.shape) for x in (w_qkv, small, gpos_a, gpos_b)],
        out_specs=[whole_spec(x.shape) for x in sends],
        out_shape=sends,
        scratch_shapes=[
            pltpu.VMEM((width, 3 * width), F32),
            pltpu.VMEM((tile, width), BF16),
            pltpu.VMEM((128, width), F32),
            pltpu.VMEM((8, 3 * width), F32),
            pltpu.VMEM((64, 256), F32),
            pltpu.VMEM((width, 128), F32),
        ],
        compiler_params=params(24),
        cost_estimate=cost(1000000000, n * width),
        name="project_back",
    )(gqn, tokens, w_qkv, small, gpos_a, gpos_b)


def token_back(gqn, tokens, gmid, w_qkv, vec, tile=512):
    n, width = tokens.shape
    return pl.pallas_call(
        token_back_kernel,
        grid=(n // tile,),
        in_specs=[rows_spec(tile, 3 * width), rows_spec(tile, width), rows_spec(tile, width)]
        + [whole_spec(w_qkv.shape), whole_spec(vec.shape)],
        out_specs=rows_spec(tile, width),
        out_shape=struct((n, width), F32),
        scratch_shapes=[pltpu.VMEM((tile // 2, width), F32)] * 2,
        compiler_params=params(24),
        cost_estimate=cost(1000000000, n * width),
        name="token_back",
    )(gqn, tokens, gmid, w_qkv, vec)


def output(gelu, ctx, tokens, wp, wd, vec, into, start, count, tile=512):
    n, width = tokens.shape

    def spec(cols):
        return pl.BlockSpec((tile, cols), lambda i: (i + start, 0))

    return pl.pallas_call(
        output_kernel,
        grid=(count,),
        in_specs=[spec(width)] * 6 + [whole_spec(x.shape) for x in (wp, wd, vec)] + [ANY_SPEC],
        out_specs=spec(width),
        out_shape=struct((n, width), BF16),
        input_output_aliases={} if into is None else {9: 0},
        compiler_params=params(24),
        cost_estimate=cost(1000000000, n * width),
        name="output",
    )(*gelu, ctx, tokens, wp, wd, vec, ctx if into is None else into)


def finish_kernel(*refs):
    first, second = refs[:4], refs[4:8]
    gqkv_ref, gproj_ref, gup_ref, gdown_ref, *vector_refs, table_ref = refs[8:]
    width = gproj_ref.shape[1]

    def total(parts, cols):
        a, b, c, d = (part[:, cols].astype(F32) for part in parts)
        return (a + b) + (c + d)

    gqkv_ref[...] = total(first, slice(0, 3 * width))
    gproj_ref[...] = total(second, slice(0, width))
    gup_ref[...] = total(second, slice(width, 5 * width))
    for q in range(4):
        gdown_ref[UNIT * q : UNIT * q + UNIT, :] = total(second, slice((5 + q) * width, (6 + q) * width))
    extra = total(first, slice(3 * width, 3 * width + 128))
    rows = jnp.transpose(extra)
    for i in range(8):
        vector_refs[i][...] = rows[i, :]
    vector_refs[8][...] = jnp.concatenate([rows[8 + q : 9 + q, :] for q in range(4)], axis=1)[0]
    table_ref[...] = extra[:, 16 : 16 + RELS]


def finish(first, second):
    width = second[0].shape[1] // 9
    return pl.pallas_call(
        finish_kernel,
        out_shape=[
            struct((UNIT, 3 * width), F32), struct((UNIT, width), F32), struct((UNIT, 4 * width), F32),
            struct((4 * UNIT, width), F32),
            *[struct((UNIT,), F32)] * 8, struct((4 * UNIT,), F32), struct((HEADS, RELS), F32),
        ],
        compiler_params=pltpu.CompilerParams(vmem_limit_bytes=16 * 1024 * 1024),
        name="finish",
    )(*first, *second)


def exchange(x, mask):
    size = lax.axis_size(AXES)
    return lax.ppermute(x, AXES, [(i, i ^ mask) for i in range(size)])


def spread_far(block, masks):
    return [block] + [exchange(block, m) for m in masks]


def spread_core(pieces):
    return pieces + [exchange(x, CORE[0]) for x in pieces]


def piece_masks(near, far, start):
    return tuple((start, tuple(n ^ f ^ core for n in (0,) + near)) for core in (0,) + CORE for f in (0,) + far)


def add(*parts):
    parts = [p.astype(F32) for p in parts]
    while len(parts) > 1:
        parts = [parts[i] + parts[i + 1] for i in range(0, len(parts), 2)]
    return parts[0].astype(BF16)


def meet_core(keep, send):
    got = exchange(send, CORE[0])
    quarter = keep.shape[0] // 4
    return [add(keep[quarter * k : quarter * (k + 1)], got[quarter * k : quarter * (k + 1)]) for k in range(4)]


def meet_far(groups, masks):
    return [groups[0]] + [exchange(group, mask) for group, mask in zip(groups[1:], masks)]


def add_blocks(parts):
    return [add(*[p[UNIT * k : UNIT * (k + 1)] for p in parts]) for k in range(4)]


def gather(x):
    return lax.all_gather(x, AXES, axis=0, tiled=True)


def scatter(x):
    return lax.psum_scatter(x, AXES, scatter_dimension=0, tiled=True)


def by_unit(x):
    return jnp.moveaxis(x.reshape((SHARDS, 4, UNIT) + x.shape[1:]), 1, 2).reshape((SHARDS * UNIT, 4) + x.shape[1:])


def by_row(x):
    return jnp.moveaxis(x.reshape((SHARDS, UNIT, 4) + x.shape[2:]), 2, 1).reshape((4 * SHARDS * UNIT,) + x.shape[2:])


def whole_weights(vectors, weights):
    columns = [gather(v)[:, None] for v in vectors[:8]] + [by_unit(gather(vectors[8]))]
    extra = jnp.concatenate(columns, axis=1)
    qkv, proj, up, down = (gather(w) for w in weights)
    first = jnp.concatenate([qkv, extra, jnp.zeros((qkv.shape[0], 128 - extra.shape[1]), BF16)], axis=1)
    second = jnp.concatenate([proj, up, by_unit(down).reshape(proj.shape[0], -1)], axis=1)
    return first, second


def whole_grads(first, second):
    width = second.shape[1] // 9
    mats = [first[:, : 3 * width], second[:, :width], second[:, width : 5 * width]]
    mats.append(by_row(second[:, 5 * width :].reshape(-1, 4, width)))
    extra = first[:, 3 * width :]
    vectors = [extra[:, k] for k in range(8)] + [by_row(extra[:, 8:12])]
    table = lax.psum(extra[:UNIT, 16 : 16 + RELS].astype(F32), AXES).T
    return [scatter(x).astype(F32) for x in mats] + [scatter(x.astype(F32)) for x in vectors] + [table]


def local_test(
    tokens, cotangent, counts, shifts, qkv, proj, up, down, vec1, vec2, ub, table,
):
    shifts, table = shifts.T, table.T
    extra = jnp.concatenate([vec1, vec2], axis=0).T
    extra = jnp.concatenate([extra, by_unit(ub[0]), jnp.zeros((512, 116))], axis=1).astype(BF16)
    first = jnp.concatenate([qkv, extra], axis=1)
    second = jnp.concatenate([proj, up, by_unit(down).reshape(512, -1)], axis=1)
    q, prob, ctx, w_qkv, vec = attend(shifts, counts, tokens, table, [first], None)
    *gelu, gmid, gctx, small, wp, wd, gsecond = mlp(tokens, ctx, cotangent, vec, [second], None, False)
    gqn, gpos_a = attend_back(shifts, q, prob, gctx, None, 0, 2)
    gqn, gpos_b = attend_back(shifts, q, prob, gctx, gqn, 2, 2)
    (gfirst,) = project_back(gqn, tokens, w_qkv, small, gpos_a, gpos_b, False)
    gtok = token_back(gqn, tokens, gmid, w_qkv, vec)
    out = output(gelu, ctx, tokens, wp, wd, vec, None, 0, 2)
    out = output(gelu, ctx, tokens, wp, wd, vec, out, 2, 2)
    width = 512
    e = gfirst[:, 1536:]
    mats = [gfirst[:, :1536], gsecond[:, :width], gsecond[:, width : 5 * width], by_row(gsecond[:, 5 * width :].reshape(-1, 4, width))]
    v = [e[:, k] for k in range(8)]
    return [out, gtok] + mats + [v[0], v[1], v[4], v[5], v[2], v[3], v[6], by_row(e[:, 8:12]), v[7], e[:16, 16:65].T]


def on_device(
    tokens, cotangent, counts, shifts, qkv_weight, proj_weight, up_weight, down_weight,
    first_gain, first_bias, second_gain, second_bias, query_bias, value_bias, proj_bias, up_bias, down_bias,
    rel_table,
):
    shifts, rel_table = shifts.T, rel_table.T
    vectors = [first_gain, first_bias, query_bias, value_bias, second_gain, second_bias, proj_bias, down_bias, up_bias]
    weights = [qkv_weight, proj_weight, up_weight, down_weight]
    stepped = lax.axis_size(AXES) == SHARDS
    if stepped:
        first, second = pack(vectors, weights)
        masks = piece_masks(COLUMN, PLANE, 0)
        first = spread_far(first, COLUMN)
        second = spread_far(second, COLUMN)
        first = spread_far(jnp.concatenate(first), PLANE)
        first[0], second = lax.optimization_barrier((first[0], jnp.concatenate(second)))
        second = spread_far(second, PLANE)
        first = spread_core(first)
    else:
        first, second = ([x] for x in whole_weights(vectors, weights))
        masks = None
    clips = counts.shape[0]
    qkv, prob, ctx, w_qkv, vec = attend(shifts, counts, tokens, rel_table, first, masks)
    if stepped:
        ctx, far = lax.optimization_barrier((ctx, second[1:]))
        second = spread_core(second[:1] + list(far))
    parts = mlp(tokens, ctx, cotangent, vec, second, masks, stepped)
    gelu, (gmid, gctx, small, wp, wd), gsecond = parts[:4], parts[4:9], parts[9:]
    half = max(1, clips // 4)
    gqn, gpos_a = attend_back(shifts, qkv, prob, gctx, None, 0, half)
    if stepped:
        gsecond = meet_core(*gsecond)
        gqn, gsecond = lax.optimization_barrier((gqn, gsecond))
        gsecond = meet_far(gsecond, PLANE)
    gqn, gpos_b = attend_back(shifts, qkv, prob, gctx, gqn, half, clips - half)
    gtok = token_back(gqn, tokens, gmid, w_qkv, vec)
    gqn, gtok = lax.optimization_barrier((gqn, gtok))
    gfirst = project_back(gqn, tokens, w_qkv, small, gpos_a, gpos_b, stepped)
    if stepped:
        gfirst, gsecond = lax.optimization_barrier((gfirst, gsecond))
        gsecond = meet_far(add_blocks(gsecond), COLUMN)
        gfirst = meet_core(*gfirst)
        gfirst, gelu = lax.optimization_barrier((gfirst, gelu))
        gfirst = meet_far(gfirst, PLANE)
    tiles = tokens.shape[0] // 512
    out = output(gelu, ctx, tokens, wp, wd, vec, None, 0, tiles // 2)
    if stepped:
        gfirst, out = lax.optimization_barrier((gfirst, out))
        gfirst, out = lax.optimization_barrier((add_blocks(gfirst), out))
        gfirst = meet_far(gfirst, COLUMN)
    out = output(gelu, ctx, tokens, wp, wd, vec, out, tiles // 2, tiles - tiles // 2)
    if stepped:
        gfirst, gsecond, out = lax.optimization_barrier((gfirst, gsecond, out))
        grads = finish(gfirst, gsecond)
        grads = (*grads[:13], grads[13].T)
    else:
        grads = whole_grads(gfirst[0], gsecond[0])
    mats, vecs, table = grads[:4], grads[4:13], grads[13]
    return (
        out, gtok, *mats, vecs[0], vecs[1], vecs[4], vecs[5], vecs[2], vecs[3], vecs[6], vecs[8], vecs[7], table,
    )


def solution(mesh):
    sharded = P(AXES, None)
    line = P(AXES)
    in_specs = (sharded, sharded, line, sharded) + (sharded,) * 4 + (line,) * 9 + (P(),)
    out_specs = (sharded,) * 6 + (line,) * 9 + (P(),)
    return jax.shard_map(on_device, mesh=mesh, in_specs=in_specs, out_specs=out_specs, check_vma=False)
```
